32 devices in a mesh: grid: 8 (over y, x, core), band: 4 (over z).
Axes of the slice: x: 2, y: 2, z: 4, core: 2. Of those that a mesh axis runs over, the one named last changes fastest.
Arguments:
- coefficients: float32 [2, 4, 131072], P(None, 'band', 'grid'), may hold values from -60 to 60
- index_map: int32 [131072], P('grid'), may hold values from 0 to 884735, as said below
- potential: float32 [192, 36864], P('grid'), may hold values from 0.5 to 2.5
Outputs:
- subspace: float32 [2, 4, 4], P(None, None, 'band')
- residual: float32 [2, 4, 131072], P(None, 'band', 'grid')
The draws below stay inside these ranges and needn't reach their ends.
Inputs may be any that keep to these rules, and one draw needn't show every extreme that they name: `index_map`: entries 16384 * g to 16384 * (g + 1) - 1 name distinct cells m = ga * 24 * 192 + (gb % 24) * 192 + gc of grid device g's slab of frequency planes, all with fa * fa + fc * fc < 2304, where fa and fc are ga and gc folded into -96 to 95.
All inputs are finite; a program needn't handle non-finite values.
Results may differ from the reference program's by a relative error of at most 0.000062.
Values sent between devices are 32-bit elements; how exact they have to be, the bound alone decides.
No kernel may reach another device: no remote copies, remote signals or barrier semaphores. Data moves between devices by JAX's collectives and lax.ppermute only.
A program may use at most 128 MiB of HBM per device.

```python
import math
import jax
import jax.numpy as jnp
from jax import lax

N = 192
NPW_DEV = 16384
SLAB = 24
BANDS = 4
NPW = 131072
N_GRID = 8


def draw_coefficients(key, part):
    key_list = jax.random.split(key, 4)
    common = jnp.clip(jax.random.normal(key_list[0], (2, NPW), jnp.float32), -6.0, 6.0)
    single = jnp.clip(jax.random.normal(key_list[1], (2, BANDS, NPW), jnp.float32), -6.0, 6.0)
    log_low = math.log(0.3)
    log_high = math.log(3.0)
    shared_weight = 0.6
    own_weight = 0.8
    spread = jnp.exp(jax.random.uniform(key_list[2], (NPW,), jnp.float32, log_low, log_high))
    band_gain = jnp.exp(jax.random.uniform(key_list[3], (BANDS,), jnp.float32, math.log(0.5), math.log(2.0)))
    mixed = shared_weight * common[:, None, :] + own_weight * single
    return (band_gain[None, :, None] * spread[None, None, :] * mixed).astype(jnp.float32)


def draw_index_map(key, part):
    planes = N // N_GRID
    cell_total = N * planes * N
    quarter = N // 4
    cell_ids = jnp.arange(cell_total, dtype=jnp.int32)
    row_freq = cell_ids // (planes * N)
    col_freq = cell_ids % N
    row_fold = jnp.where(row_freq < N // 2, row_freq, row_freq - N)
    col_fold = jnp.where(col_freq < N // 2, col_freq, col_freq - N)
    inside = row_fold * row_fold + col_fold * col_fold < quarter * quarter

    def pick(device):
        order_key = jax.random.fold_in(key, device)
        shuffled = jax.random.permutation(order_key, cell_total).astype(jnp.int32)
        outside = jnp.where(inside[shuffled], 0, 1).astype(jnp.int32)
        forced = jnp.logical_or(shuffled == 0, shuffled == cell_total - 1)
        priority = jnp.where(forced, -1, outside).astype(jnp.int32)
        ranking = jnp.argsort(priority, stable=True)
        return shuffled[ranking[:NPW_DEV]]
    chosen = lax.map(pick, jnp.arange(N_GRID, dtype=jnp.int32))
    return chosen.reshape(-1).astype(jnp.int32)


def level_of(stream_key, shape, shards, smallest, high):
    loudness, own = 1.0, jax.random.fold_in(stream_key, 6)
    for dim, shards_of in shards:
        draws = jnp.exp(jax.random.uniform(jax.random.fold_in(own, dim), (shards_of,), jnp.float32, smallest / len(shards), high / len(shards)))
        loudness = loudness * jnp.repeat(draws, shape[dim] // shards_of).reshape([-1 if axis == dim else 1 for axis in range(len(shape))])
    return loudness


def setup_inputs(seed: int = 0) -> dict:
    seeds = jax.random.split(jax.random.key(seed), 4)
    return {
        "coefficients": draw_coefficients(jax.random.fold_in(seeds[3], 71), 0),
        "index_map": draw_index_map(jax.random.fold_in(seeds[3], 71), 0),
        "potential": jnp.clip(0.5 + 2.0 * jax.random.uniform(seeds[2], (N, N * N), jnp.float32) ** level_of(seeds[2], (N, N * N), ((0, 8),), -0.2, 0.2), 0.5, 2.5),
    }


def reference(coefficients, index_map, potential):
    position = jnp.arange(NPW, dtype=jnp.int32)
    owner = position // NPW_DEV
    row_freq = index_map // (SLAB * N)
    mid_freq = owner * SLAB + (index_map // N) % SLAB
    col_freq = index_map % N
    flat_cell = (row_freq * N + mid_freq) * N + col_freq
    cube_pot = potential.reshape(N, N, N)

    def apply_band(band_pair):
        real_part = jnp.zeros((N * N * N,), coefficients.dtype).at[flat_cell].set(band_pair[0])
        imag_part = jnp.zeros((N * N * N,), coefficients.dtype).at[flat_cell].set(band_pair[1])
        spectrum = lax.complex(real_part, imag_part).reshape(N, N, N)
        field = jnp.fft.ifftn(spectrum)
        applied = jnp.fft.fftn(cube_pot * field).reshape(-1)[flat_cell]
        return jnp.real(applied), jnp.imag(applied)

    stacked = jnp.transpose(coefficients, (1, 0, 2))
    applied_re, applied_im = lax.map(apply_band, stacked)
    coef_re = coefficients[0]
    coef_im = coefficients[1]
    highest = lax.Precision.HIGHEST
    sub_re = (jnp.dot(coef_re, applied_re.T, precision=highest) + jnp.dot(coef_im, applied_im.T, precision=highest)) / NPW
    sub_im = (jnp.dot(coef_re, applied_im.T, precision=highest) - jnp.dot(coef_im, applied_re.T, precision=highest)) / NPW
    resid_re = applied_re - (jnp.dot(sub_re.T, coef_re, precision=highest) - jnp.dot(sub_im.T, coef_im, precision=highest))
    resid_im = applied_im - (jnp.dot(sub_im.T, coef_re, precision=highest) + jnp.dot(sub_re.T, coef_im, precision=highest))
    return jnp.stack([sub_re, sub_im]), jnp.stack([resid_re, resid_im])
```

```python
import functools
import math

import jax
import jax.numpy as jnp
import numpy as np
from jax import lax
from jax.experimental import pallas as pl
from jax.experimental.pallas import tpu as pltpu
from jax.sharding import PartitionSpec as P

N = 192
CHUNK = 256
LANES = 128
BF = jnp.bfloat16
F32 = jnp.float32
VMEM_BYTES = 56 * 1024 * 1024
NT = (((1,), (1,)), ((), ()))


def split(x):
    high = x.astype(BF)
    low = (x - high.astype(F32)).astype(BF)
    return high, low


def mm(a, b):
    return jnp.dot(a, b, preferred_element_type=F32)


def split_table(table):
    table = table.astype(np.float32)
    high = table.astype(BF)
    low = (table - high.astype(np.float32)).astype(BF)
    return high, low


@functools.cache
def tables():
    pos = np.arange(N)
    angle = 2.0 * math.pi * ((pos[:, None] * pos[None, :]) % N) / N
    cb, sb = np.cos(angle), np.sin(angle)
    b_fwd = np.block([[cb, -sb], [sb, cb]])
    b_inv = np.block([[cb, sb], [-sb, cb]])
    freq = np.arange(LANES)
    freq = np.where(freq < 64, freq, freq - LANES)
    keep = (np.abs(freq) < 48)[:, None]
    angle = 2.0 * math.pi * ((freq[:, None] * pos[None, :]) % N) / N
    cc, sc = np.cos(angle) * keep, np.sin(angle) * keep
    c_fwd = np.block([[cc, sc], [-sc, cc]])
    c_inv = np.block([[cc.T, -sc.T], [sc.T, cc.T]]) / float(N) ** 3
    bf_h, bf_l = split_table(b_fwd)
    bi_h, bi_l = split_table(b_inv)
    cf_h, cf_l = split_table(c_fwd)
    ci_h, ci_l = split_table(c_inv)
    return (
        np.concatenate([bf_h, bf_l, bf_h], axis=1),
        np.concatenate([cf_h, cf_l, cf_h], axis=0),
        np.concatenate([ci_h, ci_l, ci_h], axis=0),
        np.concatenate([bi_h, bi_l, bi_h], axis=1),
    )


def floor_div(x, divisor):
    return jnp.floor((x + 0.5) * (1.0 / divisor))


def sort_kernel(planes, m_ref, c_ref, out_ref, d_ref, acc_ref, val_ref, sum_ref, above_ref, gb_ref):
    rows = m_ref.shape[0]
    m = m_ref[...].astype(F32)
    line = floor_div(m, N)
    gc = m - N * line
    ga = floor_div(line, planes)
    gb = line - planes * ga
    ga = jnp.where(ga < 96, ga, ga - 96)
    gc = jnp.where(gc < 96, gc, gc - 64)
    lane_r = lax.broadcasted_iota(jnp.int32, (CHUNK, 2 * CHUNK), 0)
    lane_c = lax.broadcasted_iota(jnp.int32, (CHUNK, 2 * CHUNK), 1)
    tri = jnp.where((lane_r < lane_c) | (lane_c >= CHUNK), 1.0, 0.0).astype(BF)
    row_r = lax.broadcasted_iota(jnp.int32, (rows, rows), 0)
    row_c = lax.broadcasted_iota(jnp.int32, (rows, rows), 1)
    below = jnp.where(row_c < row_r, 1.0, 0.0).astype(BF)
    step_id = lax.broadcasted_iota(jnp.int32, (8, CHUNK), 1).astype(F32)
    base = jnp.zeros((1, CHUNK), F32)
    place = jnp.zeros((rows, CHUNK), F32)
    plane_of = jnp.zeros((8, CHUNK), F32)
    gb_ref[...] = gb

    def count(g, carry):
        inside = gb_ref[...] == g.astype(F32)
        sum_ref[g] = mm(jnp.where(inside, 1.0, 0.0).astype(BF), tri)
        return carry

    def climb(g, carry):
        above_ref[g] = mm(below, sum_ref[g, :, CHUNK:].astype(BF))
        return carry

    lax.fori_loop(0, planes, count, 0)
    lax.fori_loop(0, planes, climb, 0)
    for g in range(planes):
        above = above_ref[g]
        place = jnp.where(gb == float(g), sum_ref[g, :, :CHUNK] + above + base, place)
        base = base + above[rows - 1 : rows] + sum_ref[g, rows - 1 : rows, CHUNK:]
        if g < planes - 1:
            rank = g + jnp.floor((jnp.maximum(base, 1.0) - 1.0) * (1.0 / CHUNK))
            plane_of = plane_of + jnp.where(rank < step_id, 1.0, 0.0)
    d_ref[...] = place
    re_h, re_l = split(c_ref[0])
    im_h, im_l = split(c_ref[1])
    for q, value in enumerate((re_h, re_l, im_h, im_l, ga, gb, gc)):
        val_ref[q] = value.astype(F32)
    acc_ref[...] = jnp.zeros_like(acc_ref)
    hi_id = lax.broadcasted_iota(jnp.int32, (rows, CHUNK), 0).astype(F32).astype(BF)
    lo_id = lax.broadcasted_iota(jnp.int32, (CHUNK, CHUNK), 0).astype(F32).astype(BF)
    zero = jnp.zeros((rows, CHUNK), BF)

    def body(i, carry):
        part = pl.ds(pl.multiple_of(i * 8, 8), 8)
        d = d_ref[part, :]
        hi = jnp.floor(d * (1.0 / CHUNK))
        lo = d - CHUNK * hi
        values = [val_ref[q, part, :] for q in range(7)]
        left, right = [], []
        for j in range(8):
            at_hi = jnp.broadcast_to(hi[j : j + 1], (rows, CHUNK)).astype(BF) == hi_id
            at_lo = jnp.broadcast_to(lo[j : j + 1], (CHUNK, CHUNK)).astype(BF) == lo_id
            left.append(
                jnp.concatenate(
                    [
                        jnp.where(at_hi, jnp.broadcast_to(v[j : j + 1], (rows, CHUNK)).astype(BF), zero)
                        for v in values
                    ],
                    axis=0,
                )
            )
            right.append(jnp.where(at_lo, jnp.ones_like(lo_id), jnp.zeros_like(lo_id)))
        acc_ref[...] += lax.dot_general(
            jnp.concatenate(left, axis=1), jnp.concatenate(right, axis=1), NT, preferred_element_type=F32
        )
        return carry

    lax.fori_loop(0, rows // 8, body, 0)
    got = [acc_ref[q * rows : (q + 1) * rows] for q in range(7)]
    out_ref[0:rows] = got[0] + got[1]
    out_ref[rows : 2 * rows] = got[2] + got[3]
    out_ref[2 * rows : 3 * rows] = (got[4] * planes + got[5]) * LANES + got[6]
    out_ref[3 * rows : 3 * rows + 8] = plane_of


def sin_cos(x):
    y = x * x
    s = -1.0 / 39916800.0 + y * (1.0 / 6227020800.0)
    s = 1.0 / 362880.0 + y * s
    s = -1.0 / 5040.0 + y * s
    s = 1.0 / 120.0 + y * s
    s = -1.0 / 6.0 + y * s
    s = x + x * y * s
    c = 1.0 / 479001600.0 - y * (1.0 / 87178291200.0)
    c = -1.0 / 3628800.0 + y * c
    c = 1.0 / 40320.0 + y * c
    c = -1.0 / 720.0 + y * c
    c = 1.0 / 24.0 + y * c
    c = -0.5 + y * c
    c = 1.0 + y * c
    return s, c


def decode(cell, planes):
    line = jnp.floor(cell * (1.0 / LANES))
    gc = cell - LANES * line
    ga = floor_div(line, planes)
    gb = line - planes * ga
    freq = jnp.where(ga < 48, ga, ga - 96)
    return freq, gb, gc


def powers(freq, first, w_ref):
    turn = freq * first
    turn = turn - N * jnp.floor(turn * (1.0 / N) + 0.5)
    s, c = sin_cos(turn * (math.pi / N))
    w_ref[0] = 1.0 - 2.0 * s * s
    w_ref[1] = 2.0 * s * c
    s, c = sin_cos(freq * (2.0 * math.pi / N))
    for q in range(4):
        w_ref[2 + 2 * q] = c
        w_ref[3 + 2 * q] = s
        s, c = 2.0 * s * c, c * c - s * s


def rise(wr, wi, j):
    k = lax.broadcasted_iota(jnp.int32, (8, CHUNK), 0)
    shape = (8, CHUNK)
    er = ei = None
    for bit in range(3):
        on = (k & (1 << bit)) != 0
        fr = jnp.where(on, jnp.broadcast_to(wr[bit][j : j + 1], shape), 1.0)
        fi = jnp.where(on, jnp.broadcast_to(wi[bit][j : j + 1], shape), 0.0)
        if er is None:
            er, ei = fr, fi
        else:
            er, ei = er * fr - ei * fi, er * fi + ei * fr
    return er, ei


def one_hot(code_row):
    ident = lax.broadcasted_iota(jnp.int32, (LANES, CHUNK), 0).astype(F32).astype(BF)
    code = jnp.broadcast_to(code_row, (LANES, CHUNK)).astype(BF)
    return jnp.where(code == ident, jnp.ones_like(ident), jnp.zeros_like(ident))


def pair_of(pairs_ref, s, step, steps):
    g = pairs_ref[s, step]
    c = jnp.minimum(step - g, steps - 1)
    return g, c


def spread_kernel(planes, height, unroll, pairs_ref, first_ref, slab_ref, t_ref, w_ref, code_ref, a_ref):
    s = pl.program_id(0)
    rows = a_ref.shape[0]
    steps = rows + planes - 1
    first = first_ref[0].astype(F32)
    freq, gb, gc = decode(slab_ref[0, 2 * rows : 3 * rows], planes)
    code_ref[0] = gb
    code_ref[1] = gc
    powers(freq, first, w_ref)
    re, im = slab_ref[0, 0:rows], slab_ref[0, rows : 2 * rows]
    sr, si = w_ref[0], w_ref[1]
    w_ref[0] = re * sr - im * si
    w_ref[1] = re * si + im * sr
    shape = (8, CHUNK)

    def build(i, carry):
        part = pl.ds(pl.multiple_of(i * 8, 8), 8)
        w = [w_ref[q, part, :] for q in range(10)]
        for j in range(8):
            er, ei = rise(w[2:8:2], w[3:8:2], j)
            zr = jnp.broadcast_to(w[0][j : j + 1], shape)
            zi = jnp.broadcast_to(w[1][j : j + 1], shape)
            er, ei = er * zr - ei * zi, er * zi + ei * zr
            jr = jnp.broadcast_to(w[8][j : j + 1], shape)
            ji = jnp.broadcast_to(w[9][j : j + 1], shape)
            real, imag = [er], [ei]
            for _ in range(height // 8 - 1):
                er, ei = er * jr - ei * ji, er * ji + ei * jr
                real.append(er)
                imag.append(ei)
            high, low = split(jnp.concatenate(real + imag, axis=0))
            a_ref[i * 8 + j] = jnp.concatenate([high, low], axis=0)
        return carry

    lax.fori_loop(0, rows // 8, build, 0)
    t_ref[...] = jnp.zeros_like(t_ref)

    def visit(i, carry):
        for j in range(unroll):
            step = i * unroll + j
            g, c = pair_of(pairs_ref, s, step, rows)
            wanted = jnp.where(step < steps, g, -1).astype(F32)
            code = jnp.where(code_ref[0, pl.ds(c, 1), :] == wanted, code_ref[1, pl.ds(c, 1), :], -1.0)
            got = lax.dot_general(a_ref[c], one_hot(code), NT, preferred_element_type=F32)
            where = pl.ds(pl.multiple_of(g * (2 * height), 8), 2 * height)
            t_ref[0, where, :] += got[: 2 * height] + got[2 * height :]
        return carry

    lax.fori_loop(0, -(-steps // unroll), visit, 0)


def collect_kernel(planes, height, unroll, pairs_ref, first_ref, slab_ref, u_ref, h_ref, w_ref, code_ref, u2_ref, g_ref):
    s = pl.program_id(0)
    rows = g_ref.shape[0]
    steps = rows + planes - 1
    first = first_ref[0].astype(F32)
    freq, gb, gc = decode(slab_ref[0, 2 * rows : 3 * rows], planes)
    code_ref[0] = gb
    code_ref[1] = gc
    powers(freq, first, w_ref)
    for g in range(planes):
        high, low = split(u_ref[0, g * 2 * height : (g + 1) * 2 * height, :])
        u2_ref[g] = jnp.concatenate([high, low], axis=0)
    g_ref[...] = jnp.zeros_like(g_ref)

    def visit(i, carry):
        for j in range(unroll):
            step = i * unroll + j
            g, c = pair_of(pairs_ref, s, step, rows)
            wanted = jnp.where(step < steps, g, -1).astype(F32)
            code = jnp.where(code_ref[0, pl.ds(c, 1), :] == wanted, code_ref[1, pl.ds(c, 1), :], -1.0)
            got = mm(u2_ref[g], one_hot(code))
            g_ref[c] += got[: 2 * height] + got[2 * height :]
        return carry

    lax.fori_loop(0, -(-steps // unroll), visit, 0)
    shape = (8, CHUNK)

    def finish(i, carry):
        part = pl.ds(pl.multiple_of(i * 8, 8), 8)
        w = [w_ref[q, part, :] for q in range(10)]
        real, imag = [], []
        for j in range(8):
            jr = jnp.broadcast_to(w[8][j : j + 1], shape)
            ji = jnp.broadcast_to(w[9][j : j + 1], shape)
            value = g_ref[i * 8 + j]
            tiles = height // 8
            ar = value[height - 8 : height]
            ai = value[2 * height - 8 : 2 * height]
            for t in range(tiles - 2, -1, -1):
                ar, ai = (
                    ar * jr + ai * ji + value[8 * t : 8 * t + 8],
                    ai * jr - ar * ji + value[height + 8 * t : height + 8 * t + 8],
                )
            er, ei = rise(w[2:8:2], w[3:8:2], j)
            real.append(jnp.sum(ar * er + ai * ei, axis=0, keepdims=True))
            imag.append(jnp.sum(ai * er - ar * ei, axis=0, keepdims=True))
        hr = jnp.concatenate(real, axis=0)
        hi = jnp.concatenate(imag, axis=0)
        h_ref[0, part, :] = hr * w[0] + hi * w[1]
        h_ref[0, pl.ds(pl.multiple_of(rows + i * 8, 8), 8), :] = hi * w[0] - hr * w[1]
        return carry

    lax.fori_loop(0, rows // 8, finish, 0)


def potential_kernel(group, height, planes, t_ref, v_ref, bf_ref, cf_ref, ci_ref, bi_ref, u_ref):
    step = pl.program_id(0)
    if height > planes:

        @pl.when(step == 0)
        def _():
            u_ref[...] = jnp.zeros_like(u_ref)

    stride = 2 * height
    real, imag = [], []
    for j in range(group):
        k = step * group + j
        real.append(t_ref[pl.ds(k, N, stride=stride), :])
        imag.append(t_ref[pl.ds(k + height, N, stride=stride), :])
    x = jnp.concatenate([jnp.concatenate(real, axis=1), jnp.concatenate(imag, axis=1)], axis=0)
    high, low = split(x)
    x = mm(bf_ref[...], jnp.concatenate([high, high, low], axis=0))
    x = jnp.concatenate(
        [
            jnp.concatenate([x[:N, j * LANES : (j + 1) * LANES], x[N:, j * LANES : (j + 1) * LANES]], axis=1)
            for j in range(group)
        ],
        axis=0,
    )
    high, low = split(x)
    x = mm(jnp.concatenate([high, high, low], axis=1), cf_ref[...])
    v = jnp.concatenate([v_ref[j] for j in range(group)], axis=0)
    x = x * jnp.concatenate([v, v], axis=1)
    high, low = split(x)
    x = mm(jnp.concatenate([high, high, low], axis=1), ci_ref[...])
    x = jnp.concatenate(
        [
            jnp.concatenate([x[j * N : (j + 1) * N, q * LANES : (q + 1) * LANES] for j in range(group)], axis=1)
            for q in range(2)
        ],
        axis=0,
    )
    high, low = split(x)
    x = mm(bi_ref[...], jnp.concatenate([high, high, low], axis=0))
    for j in range(group):
        k = step * group + j
        u_ref[pl.ds(k, N, stride=stride), :] = x[:N, j * LANES : (j + 1) * LANES]
        u_ref[pl.ds(k + height, N, stride=stride), :] = x[N:, j * LANES : (j + 1) * LANES]


def unsort_kernel(bands, recv_ref, d_ref, *refs):
    coef_refs, (h_ref, part_ref, hl_ref) = refs[:bands], refs[bands:]
    rows = d_ref.shape[0]
    total = recv_ref[0]
    for s in range(1, recv_ref.shape[0]):
        total = total + recv_ref[s]
    high, low = split(total)
    hl_ref[0 : 2 * rows] = high
    hl_ref[2 * rows :] = low
    hi_id = lax.broadcasted_iota(jnp.int32, (rows, CHUNK), 0).astype(F32)
    lo_id = lax.broadcasted_iota(jnp.int32, (CHUNK, CHUNK), 0).astype(F32).astype(BF)

    def body(i, carry):
        part = pl.ds(pl.multiple_of(i * 8, 8), 8)
        d = d_ref[part, :]
        hi = jnp.floor(d * (1.0 / CHUNK))
        lo = d - CHUNK * hi
        real, imag = [], []
        for j in range(8):
            at_lo = jnp.broadcast_to(lo[j : j + 1], (CHUNK, CHUNK)).astype(BF) == lo_id
            got = mm(hl_ref[...], jnp.where(at_lo, jnp.ones_like(lo_id), jnp.zeros_like(lo_id)))
            got = got[: 2 * rows] + got[2 * rows :]
            at_hi = jnp.broadcast_to(hi[j : j + 1], (rows, CHUNK)) == hi_id
            real.append(jnp.sum(jnp.where(at_hi, got[:rows], 0.0), axis=0, keepdims=True))
            imag.append(jnp.sum(jnp.where(at_hi, got[rows:], 0.0), axis=0, keepdims=True))
        h_ref[0, part, :] = jnp.concatenate(real, axis=0)
        h_ref[1, part, :] = jnp.concatenate(imag, axis=0)
        return carry

    lax.fori_loop(0, rows // 8, body, 0)
    hr, hi = h_ref[0], h_ref[1]
    sums = []
    for coef in coef_refs:
        cr, ci = coef[0], coef[1]
        for value in (cr * hr + ci * hi, cr * hi - ci * hr):
            line = jnp.sum(value, axis=0, keepdims=True)
            sums.append(line[:, :LANES] + line[:, LANES:])
    part_ref[...] = jnp.concatenate(sums, axis=0)


def residual_kernel(bands, scale, sum_ref, h_ref, *refs):
    coef_refs, (out_ref, sub_ref) = refs[:bands], refs[bands:]
    sub = jnp.sum(sum_ref[...], axis=1, keepdims=True) * scale
    sub_ref[...] = jnp.broadcast_to(sub, sub_ref.shape)
    hr, hi = h_ref[0], h_ref[1]
    for i, coef in enumerate(coef_refs):
        sr, si = sub[2 * i : 2 * i + 1], sub[2 * i + 1 : 2 * i + 2]
        cr, ci = coef[0], coef[1]
        hr = hr - (sr * cr - si * ci)
        hi = hi - (si * cr + sr * ci)
    out_ref[0] = hr
    out_ref[1] = hi


def params(**extra):
    return pltpu.CompilerParams(vmem_limit_bytes=VMEM_BYTES, **extra)


def whole(shape):
    return pl.BlockSpec(shape, lambda *_: (0,) * len(shape))


def local(coefficients, index_map, potential):
    slabs = lax.axis_size("grid")
    bands = lax.axis_size("band")
    planes = potential.shape[0]
    count = coefficients.shape[2]
    rows = count // CHUNK
    height = -(-planes // 8) * 8
    group = 2 if planes % 2 == 0 else 1
    steps = rows + planes - 1
    unroll = 8
    me = lax.axis_index("grid")
    band = lax.axis_index("band")
    coef = coefficients.reshape(2, rows, CHUNK)
    sorted_pts, dest = pl.pallas_call(
        functools.partial(sort_kernel, planes),
        out_shape=(
            jax.ShapeDtypeStruct((3 * rows + 8, CHUNK), F32),
            jax.ShapeDtypeStruct((rows, CHUNK), F32),
        ),
        scratch_shapes=[
            pltpu.VMEM((7 * rows, CHUNK), F32),
            pltpu.VMEM((7, rows, CHUNK), F32),
            pltpu.VMEM((planes, rows, 2 * CHUNK), F32),
            pltpu.VMEM((planes, rows, CHUNK), F32),
            pltpu.VMEM((rows, CHUNK), F32),
        ],
        compiler_params=params(),
        name="sort_points",
    )(index_map.reshape(rows, CHUNK), coef)
    coefs = [coef]
    for shift in range(1, bands):
        coefs.append(lax.ppermute(coef, "band", [(i, (i + shift) % bands) for i in range(bands)]))
    points = lax.all_gather(sorted_pts, "grid")
    pairs = points[:, 3 * rows, :].astype(jnp.int32)
    first = (me * planes).astype(jnp.int32).reshape(1)
    slab_spec = pl.BlockSpec((1, 3 * rows + 8, CHUNK), lambda s, *_: (s, 0, 0))
    plane_rows = planes * 2 * height
    t_spec = pl.BlockSpec((1, plane_rows, LANES), lambda s, *_: (s, 0, 0))
    spectrum = pl.pallas_call(
        functools.partial(spread_kernel, planes, height, unroll),
        grid_spec=pltpu.PrefetchScalarGridSpec(
            num_scalar_prefetch=2,
            grid=(slabs,),
            in_specs=[slab_spec],
            out_specs=t_spec,
            scratch_shapes=[
                pltpu.VMEM((10, rows, CHUNK), F32),
                pltpu.VMEM((2, rows, CHUNK), F32),
                pltpu.VMEM((rows, 4 * height, CHUNK), BF),
            ],
        ),
        out_shape=jax.ShapeDtypeStruct((slabs, plane_rows, LANES), F32),
        compiler_params=params(),
        name="spread_points",
    )(pairs, first, points)
    b_fwd, c_fwd, c_inv, b_inv = (jnp.asarray(t) for t in tables())
    full = (slabs * plane_rows, LANES)
    weighted = pl.pallas_call(
        functools.partial(potential_kernel, group, height, planes),
        grid=(planes // group,),
        in_specs=[whole(full), pl.BlockSpec((group, N, N), lambda i: (i, 0, 0))]
        + [whole(t.shape) for t in (b_fwd, c_fwd, c_inv, b_inv)],
        out_specs=whole(full),
        out_shape=jax.ShapeDtypeStruct(full, F32),
        compiler_params=params(),
        name="apply_potential",
    )(spectrum.reshape(full), potential.reshape(planes, N, N), b_fwd, c_fwd, c_inv, b_inv)
    partial = pl.pallas_call(
        functools.partial(collect_kernel, planes, height, unroll),
        grid_spec=pltpu.PrefetchScalarGridSpec(
            num_scalar_prefetch=2,
            grid=(slabs,),
            in_specs=[slab_spec, t_spec],
            out_specs=pl.BlockSpec((1, 2 * rows, CHUNK), lambda s, *_: (s, 0, 0)),
            scratch_shapes=[
                pltpu.VMEM((10, rows, CHUNK), F32),
                pltpu.VMEM((2, rows, CHUNK), F32),
                pltpu.VMEM((planes, 4 * height, LANES), BF),
                pltpu.VMEM((rows, 2 * height, CHUNK), F32),
            ],
        ),
        out_shape=jax.ShapeDtypeStruct((slabs, 2 * rows, CHUNK), F32),
        compiler_params=params(),
        name="collect_points",
    )(pairs, first, points, weighted.reshape(slabs, plane_rows, LANES))
    arrived = lax.all_to_all(partial, "grid", split_axis=0, concat_axis=0, tiled=True)
    applied, part = pl.pallas_call(
        functools.partial(unsort_kernel, bands),
        out_shape=(
            jax.ShapeDtypeStruct((2, rows, CHUNK), F32),
            jax.ShapeDtypeStruct((2 * bands, LANES), F32),
        ),
        scratch_shapes=[pltpu.VMEM((4 * rows, CHUNK), BF)],
        compiler_params=params(),
        name="unsort_points",
    )(arrived, dest, *coefs)
    sums = lax.psum(part, "grid")
    resid, sub = pl.pallas_call(
        functools.partial(residual_kernel, bands, 1.0 / (count * slabs)),
        out_shape=(
            jax.ShapeDtypeStruct((2, rows, CHUNK), F32),
            jax.ShapeDtypeStruct((2 * bands, LANES), F32),
        ),
        compiler_params=params(),
        name="residual",
    )(sums, applied, *coefs)
    turned = sub[:, 0].reshape(bands, 2)
    ids = jnp.arange(bands)
    pick = (ids[None, :] == (band - ids[:, None]) % bands).astype(F32)
    ordered = jnp.sum(pick[:, :, None] * turned[None], axis=1)
    return ordered.T.reshape(2, bands, 1), resid.reshape(2, 1, count)


def solution(mesh):
    return jax.shard_map(
        local,
        mesh=mesh,
        in_specs=(P(None, "band", "grid"), P("grid"), P("grid", None)),
        out_specs=(P(None, None, "band"), P(None, "band", "grid")),
        check_vma=False,
    )
```

```python
import functools
import math

import jax
import jax.numpy as jnp
import numpy as np
from jax import lax
from jax.experimental import pallas as pl
from jax.experimental.pallas import tpu as pltpu
from jax.sharding import PartitionSpec as P

N = 192
CHUNK = 256
LANES = 128
BF = jnp.bfloat16
F32 = jnp.float32
VMEM_BYTES = 56 * 1024 * 1024
NT = (((1,), (1,)), ((), ()))


def split(x):
    high = x.astype(BF)
    low = (x - high.astype(F32)).astype(BF)
    return high, low


def mm(a, b):
    return jnp.dot(a, b, preferred_element_type=F32)


def split_table(table):
    table = table.astype(np.float32)
    high = table.astype(BF)
    low = (table - high.astype(np.float32)).astype(BF)
    return high, low


@functools.cache
def tables():
    pos = np.arange(N)
    angle = 2.0 * math.pi * ((pos[:, None] * pos[None, :]) % N) / N
    cb, sb = np.cos(angle), np.sin(angle)
    b_fwd = np.block([[cb, -sb], [sb, cb]])
    b_inv = np.block([[cb, sb], [-sb, cb]])
    freq = np.arange(LANES)
    freq = np.where(freq < 64, freq, freq - LANES)
    keep = (np.abs(freq) < 48)[:, None]
    angle = 2.0 * math.pi * ((freq[:, None] * pos[None, :]) % N) / N
    cc, sc = np.cos(angle) * keep, np.sin(angle) * keep
    c_fwd = np.block([[cc, sc], [-sc, cc]])
    c_inv = np.block([[cc.T, -sc.T], [sc.T, cc.T]]) / float(N) ** 3
    bf_h, bf_l = split_table(b_fwd)
    bi_h, bi_l = split_table(b_inv)
    cf_h, cf_l = split_table(c_fwd)
    ci_h, ci_l = split_table(c_inv)
    return (
        np.concatenate([bf_h, bf_l, bf_h], axis=1),
        np.concatenate([cf_h, cf_l, cf_h], axis=0),
        np.concatenate([ci_h, ci_l, ci_h], axis=0),
        np.concatenate([bi_h, bi_l, bi_h], axis=1),
    )


def fold(x):
    half = x.shape[0] // 2
    return jnp.concatenate([x[:half], x[half:]], axis=1)


def unfold(x):
    return jnp.concatenate([x[:, :LANES], x[:, LANES:]], axis=0)


def floor_div(x, divisor):
    return jnp.floor((x + 0.5) * (1.0 / divisor))


def sort_kernel(planes, m_ref, c_ref, out_ref, d_ref, acc_ref, val_ref, sum_ref, above_ref, gb_ref):
    rows = m_ref.shape[0] // 2
    m = fold(m_ref[...]).astype(F32)
    line = floor_div(m, N)
    gc = m - N * line
    ga = floor_div(line, planes)
    gb = line - planes * ga
    ga = jnp.where(ga < 96, ga, ga - 96)
    gc = jnp.where(gc < 96, gc, gc - 64)
    lane_r = lax.broadcasted_iota(jnp.int32, (CHUNK, 2 * CHUNK), 0)
    lane_c = lax.broadcasted_iota(jnp.int32, (CHUNK, 2 * CHUNK), 1)
    tri = jnp.where((lane_r < lane_c) | (lane_c >= CHUNK), 1.0, 0.0).astype(BF)
    row_r = lax.broadcasted_iota(jnp.int32, (rows, rows), 0)
    row_c = lax.broadcasted_iota(jnp.int32, (rows, rows), 1)
    below = jnp.where(row_c < row_r, 1.0, 0.0).astype(BF)
    step_id = lax.broadcasted_iota(jnp.int32, (8, CHUNK), 1).astype(F32)
    base = jnp.zeros((1, CHUNK), F32)
    place = jnp.zeros((rows, CHUNK), F32)
    plane_of = jnp.zeros((8, CHUNK), F32)
    gb_ref[...] = gb

    def count(g, carry):
        inside = gb_ref[...] == g.astype(F32)
        sum_ref[g] = mm(jnp.where(inside, 1.0, 0.0).astype(BF), tri)
        return carry

    def climb(g, carry):
        above_ref[g] = mm(below, sum_ref[g, :, CHUNK:].astype(BF))
        return carry

    lax.fori_loop(0, planes, count, 0)
    lax.fori_loop(0, planes, climb, 0)
    for g in range(planes):
        above = above_ref[g]
        place = jnp.where(gb == float(g), sum_ref[g, :, :CHUNK] + above + base, place)
        base = base + above[rows - 1 : rows] + sum_ref[g, rows - 1 : rows, CHUNK:]
        if g < planes - 1:
            rank = g + jnp.floor((jnp.maximum(base, 1.0) - 1.0) * (1.0 / CHUNK))
            plane_of = plane_of + jnp.where(rank < step_id, 1.0, 0.0)
    d_ref[...] = place
    re_h, re_l = split(fold(c_ref[0]))
    im_h, im_l = split(fold(c_ref[1]))
    for q, value in enumerate((re_h, re_l, im_h, im_l, ga, gb, gc)):
        val_ref[q] = value.astype(F32)
    acc_ref[...] = jnp.zeros_like(acc_ref)
    hi_id = lax.broadcasted_iota(jnp.int32, (rows, CHUNK), 0).astype(F32).astype(BF)
    lo_id = lax.broadcasted_iota(jnp.int32, (CHUNK, CHUNK), 0).astype(F32).astype(BF)
    zero = jnp.zeros((rows, CHUNK), BF)

    def body(i, carry):
        part = pl.ds(pl.multiple_of(i * 8, 8), 8)
        d = d_ref[part, :]
        hi = jnp.floor(d * (1.0 / CHUNK))
        lo = d - CHUNK * hi
        values = [val_ref[q, part, :] for q in range(7)]
        left, right = [], []
        for j in range(8):
            at_hi = jnp.broadcast_to(hi[j : j + 1], (rows, CHUNK)).astype(BF) == hi_id
            at_lo = jnp.broadcast_to(lo[j : j + 1], (CHUNK, CHUNK)).astype(BF) == lo_id
            left.append(
                jnp.concatenate(
                    [
                        jnp.where(at_hi, jnp.broadcast_to(v[j : j + 1], (rows, CHUNK)).astype(BF), zero)
                        for v in values
                    ],
                    axis=0,
                )
            )
            right.append(jnp.where(at_lo, jnp.ones_like(lo_id), jnp.zeros_like(lo_id)))
        acc_ref[...] += lax.dot_general(
            jnp.concatenate(left, axis=1), jnp.concatenate(right, axis=1), NT, preferred_element_type=F32
        )
        return carry

    lax.fori_loop(0, rows // 8, body, 0)
    got = [acc_ref[q * rows : (q + 1) * rows] for q in range(7)]
    out_ref[0:rows] = got[0] + got[1]
    out_ref[rows : 2 * rows] = got[2] + got[3]
    out_ref[2 * rows : 3 * rows] = (got[4] * planes + got[5]) * LANES + got[6]
    out_ref[3 * rows : 3 * rows + 8] = plane_of


def sin_cos(x):
    y = x * x
    s = -1.0 / 39916800.0 + y * (1.0 / 6227020800.0)
    s = 1.0 / 362880.0 + y * s
    s = -1.0 / 5040.0 + y * s
    s = 1.0 / 120.0 + y * s
    s = -1.0 / 6.0 + y * s
    s = x + x * y * s
    c = 1.0 / 479001600.0 - y * (1.0 / 87178291200.0)
    c = -1.0 / 3628800.0 + y * c
    c = 1.0 / 40320.0 + y * c
    c = -1.0 / 720.0 + y * c
    c = 1.0 / 24.0 + y * c
    c = -0.5 + y * c
    c = 1.0 + y * c
    return s, c


def decode(cell, planes):
    line = jnp.floor(cell * (1.0 / LANES))
    gc = cell - LANES * line
    ga = floor_div(line, planes)
    gb = line - planes * ga
    freq = jnp.where(ga < 48, ga, ga - 96)
    return freq, gb, gc


def phase(freq, first):
    turn = freq * first
    turn = turn - N * jnp.floor(turn * (1.0 / N) + 0.5)
    s, c = sin_cos(turn * (math.pi / N))
    return 1.0 - 2.0 * s * s, 2.0 * s * c


def powers(freq, w_ref):
    s, c = sin_cos(freq * (2.0 * math.pi / N))
    for q in range(4):
        w_ref[4 + 2 * q] = c
        w_ref[5 + 2 * q] = s
        s, c = 2.0 * s * c, c * c - s * s


def rise(wr, wi, j):
    k = lax.broadcasted_iota(jnp.int32, (8, CHUNK), 0)
    shape = (8, CHUNK)
    er = ei = None
    for bit in range(3):
        on = (k & (1 << bit)) != 0
        fr = jnp.where(on, jnp.broadcast_to(wr[bit][j : j + 1], shape), 1.0)
        fi = jnp.where(on, jnp.broadcast_to(wi[bit][j : j + 1], shape), 0.0)
        if er is None:
            er, ei = fr, fi
        else:
            er, ei = er * fr - ei * fi, er * fi + ei * fr
    return er, ei


def one_hot(code_row):
    ident = lax.broadcasted_iota(jnp.int32, (LANES, CHUNK), 0).astype(F32).astype(BF)
    code = jnp.broadcast_to(code_row, (LANES, CHUNK)).astype(BF)
    return jnp.where(code == ident, jnp.ones_like(ident), jnp.zeros_like(ident))


def firsts(planes):
    me = lax.axis_index("grid")
    return (me * planes).astype(F32), ((me ^ 1) * planes).astype(F32)


def pair_code(planes, steps_ref, code_ref, rows, step):
    g = steps_ref[0, step].astype(jnp.int32)
    c = jnp.minimum(step - g, rows - 1)
    wanted = jnp.where(step < rows + planes - 1, g, -1).astype(F32)
    code = jnp.where(code_ref[0, pl.ds(c, 1), :] == wanted, code_ref[1, pl.ds(c, 1), :], -1.0)
    return g, c, code


def spread_kernel(planes, height, unroll, slab_ref, steps_ref, own_ref, sib_ref, w_ref, code_ref, a_ref):
    rows = a_ref.shape[0]
    freq, gb, gc = decode(slab_ref[0, 2 * rows : 3 * rows], planes)
    code_ref[0] = gb
    code_ref[1] = gc
    re, im = slab_ref[0, 0:rows], slab_ref[0, rows : 2 * rows]
    for q, first in enumerate(firsts(planes)):
        sr, si = phase(freq, first)
        w_ref[2 * q] = re * sr - im * si
        w_ref[2 * q + 1] = re * si + im * sr
    powers(freq, w_ref)
    shape = (8, CHUNK)

    def build(i, carry):
        part = pl.ds(pl.multiple_of(i * 8, 8), 8)
        w = [w_ref[q, part, :] for q in range(12)]
        for j in range(8):
            er, ei = rise(w[4:10:2], w[5:10:2], j)
            jr = jnp.broadcast_to(w[10][j : j + 1], shape)
            ji = jnp.broadcast_to(w[11][j : j + 1], shape)
            lines = []
            for q in range(2):
                zr = jnp.broadcast_to(w[2 * q][j : j + 1], shape)
                zi = jnp.broadcast_to(w[2 * q + 1][j : j + 1], shape)
                zr, zi = er * zr - ei * zi, er * zi + ei * zr
                real, imag = [zr], [zi]
                for _ in range(height // 8 - 1):
                    zr, zi = zr * jr - zi * ji, zr * ji + zi * jr
                    real.append(zr)
                    imag.append(zi)
                lines += real + imag
            high, low = split(jnp.concatenate(lines, axis=0))
            a_ref[i * 8 + j] = jnp.concatenate([high, low], axis=0)
        return carry

    lax.fori_loop(0, rows // 8, build, 0)
    own_ref[...] = jnp.zeros_like(own_ref)
    sib_ref[...] = jnp.zeros_like(sib_ref)

    def visit(i, carry):
        for j in range(unroll):
            g, c, code = pair_code(planes, steps_ref, code_ref, rows, i * unroll + j)
            got = lax.dot_general(a_ref[c], one_hot(code), NT, preferred_element_type=F32)
            got = got[: 4 * height] + got[4 * height :]
            where = pl.ds(pl.multiple_of(g * (2 * height), 8), 2 * height)
            own_ref[0, where, :] += got[: 2 * height]
            sib_ref[0, where, :] += got[2 * height :]
        return carry

    lax.fori_loop(0, -(-(rows + planes - 1) // unroll), visit, 0)


def collect_kernel(
    planes, height, unroll, slab_ref, steps_ref, own_ref, sib_ref, h_ref, w_ref, code_ref, u2_ref, g_ref
):
    rows = g_ref.shape[0]
    freq, gb, gc = decode(slab_ref[0, 2 * rows : 3 * rows], planes)
    code_ref[0] = gb
    code_ref[1] = gc
    for q, first in enumerate(firsts(planes)):
        w_ref[2 * q], w_ref[2 * q + 1] = phase(freq, first)
    powers(freq, w_ref)
    for g in range(planes):
        where = slice(g * 2 * height, (g + 1) * 2 * height)
        high, low = split(jnp.concatenate([own_ref[0, where, :], sib_ref[0, where, :]], axis=0))
        u2_ref[g] = jnp.concatenate([high, low], axis=0)
    g_ref[...] = jnp.zeros_like(g_ref)

    def visit(i, carry):
        for j in range(unroll):
            g, c, code = pair_code(planes, steps_ref, code_ref, rows, i * unroll + j)
            got = mm(u2_ref[g], one_hot(code))
            g_ref[c] += got[: 4 * height] + got[4 * height :]
        return carry

    lax.fori_loop(0, -(-(rows + planes - 1) // unroll), visit, 0)
    shape = (8, CHUNK)

    def finish(i, carry):
        part = pl.ds(pl.multiple_of(i * 8, 8), 8)
        w = [w_ref[q, part, :] for q in range(12)]
        real, imag = [], []
        for j in range(8):
            jr = jnp.broadcast_to(w[10][j : j + 1], shape)
            ji = jnp.broadcast_to(w[11][j : j + 1], shape)
            hr = hi = 0.0
            for q in range(2):
                value = g_ref[i * 8 + j, q * 2 * height : (q + 1) * 2 * height]
                ar = value[height - 8 : height]
                ai = value[2 * height - 8 : 2 * height]
                for t in range(height // 8 - 2, -1, -1):
                    ar, ai = (
                        ar * jr + ai * ji + value[8 * t : 8 * t + 8],
                        ai * jr - ar * ji + value[height + 8 * t : height + 8 * t + 8],
                    )
                zr = jnp.broadcast_to(w[2 * q][j : j + 1], shape)
                zi = jnp.broadcast_to(w[2 * q + 1][j : j + 1], shape)
                hr, hi = hr + ar * zr + ai * zi, hi + ai * zr - ar * zi
            er, ei = rise(w[4:10:2], w[5:10:2], j)
            real.append(jnp.sum(hr * er + hi * ei, axis=0, keepdims=True))
            imag.append(jnp.sum(hi * er - hr * ei, axis=0, keepdims=True))
        h_ref[0, part, :] = jnp.concatenate(real, axis=0)
        h_ref[0, pl.ds(pl.multiple_of(rows + i * 8, 8), 8), :] = jnp.concatenate(imag, axis=0)
        return carry

    lax.fori_loop(0, rows // 8, finish, 0)


def potential_kernel(group, height, planes, calls, *refs):
    own, sib = refs[:calls], refs[calls : 2 * calls]
    v_ref, bf_ref, cf_ref, ci_ref, bi_ref, keep_ref, send_ref, t_ref, u_ref, sems = refs[2 * calls :]
    step = pl.program_id(0)
    me = lax.axis_index("grid")
    lines = planes * 2 * height

    def place(j, mine):
        slab = me ^ (2 * j) if mine else me ^ (2 * j + 1)
        return pl.ds(pl.multiple_of(slab * lines, 8), lines)

    half = keep_ref.shape[0]
    per_call = half // calls

    def arrivals(j):
        for q, blocks in enumerate((own, sib)):
            yield pltpu.make_async_copy(
                blocks[j // per_call].at[j % per_call], t_ref.at[place(j, q == 0)], sems.at[q, j]
            )

    def departures(j):
        for q, block in enumerate((keep_ref, send_ref)):
            yield pltpu.make_async_copy(u_ref.at[place(j, q == 0)], block.at[j], sems.at[q, j])

    @pl.when(step == 0)
    def _():
        for j in range(half):
            for copy in arrivals(j):
                copy.start()
        for j in range(half):
            for copy in arrivals(j):
                copy.wait()

    if height > planes:

        @pl.when(step == 0)
        def _():
            u_ref[...] = jnp.zeros_like(u_ref)

    stride = 2 * height
    real, imag = [], []
    for j in range(group):
        k = step * group + j
        real.append(t_ref[pl.ds(k, N, stride=stride), :])
        imag.append(t_ref[pl.ds(k + height, N, stride=stride), :])
    x = jnp.concatenate([jnp.concatenate(real, axis=1), jnp.concatenate(imag, axis=1)], axis=0)
    high, low = split(x)
    x = mm(bf_ref[...], jnp.concatenate([high, high, low], axis=0))
    x = jnp.concatenate(
        [
            jnp.concatenate([x[:N, j * LANES : (j + 1) * LANES], x[N:, j * LANES : (j + 1) * LANES]], axis=1)
            for j in range(group)
        ],
        axis=0,
    )
    high, low = split(x)
    x = mm(jnp.concatenate([high, high, low], axis=1), cf_ref[...])
    v = jnp.concatenate([v_ref[j] for j in range(group)], axis=0)
    x = x * jnp.concatenate([v, v], axis=1)
    high, low = split(x)
    x = mm(jnp.concatenate([high, high, low], axis=1), ci_ref[...])
    x = jnp.concatenate(
        [
            jnp.concatenate([x[j * N : (j + 1) * N, q * LANES : (q + 1) * LANES] for j in range(group)], axis=1)
            for q in range(2)
        ],
        axis=0,
    )
    high, low = split(x)
    x = mm(bi_ref[...], jnp.concatenate([high, high, low], axis=0))
    for j in range(group):
        k = step * group + j
        u_ref[pl.ds(k, N, stride=stride), :] = x[:N, j * LANES : (j + 1) * LANES]
        u_ref[pl.ds(k + height, N, stride=stride), :] = x[N:, j * LANES : (j + 1) * LANES]

    @pl.when(step == pl.num_programs(0) - 1)
    def _():
        for j in range(half):
            for copy in departures(j):
                copy.start()
        for j in range(half):
            for copy in departures(j):
                copy.wait()


def unsort_kernel(arrivals, *refs):
    recv_refs = refs[:arrivals]
    d_ref, coef_ref, h_ref, part_ref, hl_ref, wide_ref = refs[arrivals:]
    rows = d_ref.shape[0]
    total = None
    for recv in recv_refs:
        for s in range(recv.shape[0]):
            total = recv[s] if total is None else total + recv[s]
    high, low = split(total)
    hl_ref[0 : 2 * rows] = high
    hl_ref[2 * rows :] = low
    hi_id = lax.broadcasted_iota(jnp.int32, (rows, CHUNK), 0).astype(F32)
    lo_id = lax.broadcasted_iota(jnp.int32, (CHUNK, CHUNK), 0).astype(F32).astype(BF)

    def body(i, carry):
        part = pl.ds(pl.multiple_of(i * 8, 8), 8)
        d = d_ref[part, :]
        hi = jnp.floor(d * (1.0 / CHUNK))
        lo = d - CHUNK * hi
        real, imag = [], []
        for j in range(8):
            at_lo = jnp.broadcast_to(lo[j : j + 1], (CHUNK, CHUNK)).astype(BF) == lo_id
            got = mm(hl_ref[...], jnp.where(at_lo, jnp.ones_like(lo_id), jnp.zeros_like(lo_id)))
            got = got[: 2 * rows] + got[2 * rows :]
            at_hi = jnp.broadcast_to(hi[j : j + 1], (rows, CHUNK)) == hi_id
            real.append(jnp.sum(jnp.where(at_hi, got[:rows], 0.0), axis=0, keepdims=True))
            imag.append(jnp.sum(jnp.where(at_hi, got[rows:], 0.0), axis=0, keepdims=True))
        wide_ref[0, part, :] = jnp.concatenate(real, axis=0)
        wide_ref[1, part, :] = jnp.concatenate(imag, axis=0)
        return carry

    lax.fori_loop(0, rows // 8, body, 0)
    hr, hi = unfold(wide_ref[0]), unfold(wide_ref[1])
    h_ref[0] = hr
    h_ref[1] = hi
    real, imag = [], []
    for i in range(coef_ref.shape[0]):
        cr, ci = coef_ref[i, 0], coef_ref[i, 1]
        real.append(jnp.sum(cr * hr + ci * hi, axis=0, keepdims=True))
        imag.append(jnp.sum(cr * hi - ci * hr, axis=0, keepdims=True))
    sums = jnp.concatenate(real + imag, axis=0)
    for s in range(part_ref.shape[0]):
        part_ref[s] = sums


def residual_kernel(scale, sum_ref, h_ref, coef_ref, out_ref, sub_ref):
    bands = coef_ref.shape[0]
    sub = sum_ref[0]
    for s in range(1, sum_ref.shape[0]):
        sub = sub + sum_ref[s]
    sub = jnp.sum(sub, axis=1, keepdims=True) * scale
    sub_ref[0] = sub[:bands]
    sub_ref[1] = sub[bands:]
    hr, hi = h_ref[0], h_ref[1]
    for i in range(bands):
        sr, si = sub[i : i + 1], sub[bands + i : bands + i + 1]
        cr, ci = coef_ref[i, 0], coef_ref[i, 1]
        hr = hr - (sr * cr - si * ci)
        hi = hi - (si * cr + sr * ci)
    out_ref[0] = hr
    out_ref[1] = hi


def params(**extra):
    return pltpu.CompilerParams(vmem_limit_bytes=VMEM_BYTES, **extra)


def whole(shape):
    return pl.BlockSpec(shape, lambda *_: (0,) * len(shape))


def local(coefficients, index_map, potential):
    slabs = lax.axis_size("grid")
    bands = lax.axis_size("band")
    planes = potential.shape[0]
    count = coefficients.shape[2]
    rows = count // CHUNK
    height = -(-planes // 8) * 8
    group = 2 if planes % 2 == 0 else 1
    unroll = 22
    me = lax.axis_index("grid")
    half = slabs // 2
    coef = coefficients.reshape(2, 2 * rows, LANES)
    coefs = lax.all_gather(coef, "band")
    table_rows = 3 * rows + 8
    sorted_pts, dest = pl.pallas_call(
        functools.partial(sort_kernel, planes),
        out_shape=(
            jax.ShapeDtypeStruct((table_rows, CHUNK), F32),
            jax.ShapeDtypeStruct((rows, CHUNK), F32),
        ),
        scratch_shapes=[
            pltpu.VMEM((7 * rows, CHUNK), F32),
            pltpu.VMEM((7, rows, CHUNK), F32),
            pltpu.VMEM((planes, rows, 2 * CHUNK), F32),
            pltpu.VMEM((planes, rows, CHUNK), F32),
            pltpu.VMEM((rows, CHUNK), F32),
        ],
        compiler_params=params(),
        name="sort_points",
    )(index_map.reshape(2 * rows, LANES), coef)

    def swap(x, bits):
        return lax.ppermute(x, "grid", [(i, i ^ bits) for i in range(slabs)])

    if half <= 4:
        points = [sorted_pts[None]] + [swap(sorted_pts, 2 * j)[None] for j in range(1, half)]
    else:
        everything = lax.all_gather(sorted_pts, "grid")
        points = [jnp.take(everything, me ^ (2 * jnp.arange(half)), axis=0)]
    calls = len(points)
    per_call = half // calls
    lines = planes * 2 * height
    slab_spec = pl.BlockSpec((1, table_rows, CHUNK), lambda s: (s, 0, 0))
    steps_spec = pl.BlockSpec((None, 8, CHUNK), lambda s: (s, table_rows // 8 - 1, 0), memory_space=pltpu.SMEM)
    block_spec = pl.BlockSpec((1, lines, LANES), lambda s: (s, 0, 0))
    point_scratch = [pltpu.VMEM((12, rows, CHUNK), F32), pltpu.VMEM((2, rows, CHUNK), F32)]
    spread = pl.pallas_call(
        functools.partial(spread_kernel, planes, height, unroll),
        grid=(per_call,),
        in_specs=[slab_spec, steps_spec],
        out_specs=(block_spec, block_spec),
        out_shape=(jax.ShapeDtypeStruct((per_call, lines, LANES), F32),) * 2,
        scratch_shapes=point_scratch + [pltpu.VMEM((rows, 8 * height, CHUNK), BF)],
        compiler_params=params(),
        name="spread_points",
    )
    own, sib = [], []
    for table in points:
        mine, theirs = spread(table, table)
        own.append(mine)
        sib.append(swap(theirs, 1))
    constants = [jnp.asarray(t) for t in tables()]
    anywhere = pl.BlockSpec(memory_space=pl.ANY)
    keep, send = pl.pallas_call(
        functools.partial(potential_kernel, group, height, planes, calls),
        grid=(planes // group,),
        in_specs=[anywhere] * (2 * calls)
        + [pl.BlockSpec((group, N, N), lambda i: (i, 0, 0))]
        + [whole(t.shape) for t in constants],
        out_specs=(anywhere, anywhere),
        out_shape=(jax.ShapeDtypeStruct((half, lines, LANES), F32),) * 2,
        scratch_shapes=[
            pltpu.VMEM((slabs * lines, LANES), F32),
            pltpu.VMEM((slabs * lines, LANES), F32),
            pltpu.SemaphoreType.DMA((2, half)),
        ],
        compiler_params=params(),
        name="apply_potential",
    )(*own, *sib, potential.reshape(planes, N, N), *constants)
    other = swap(send, 1)
    partial = []
    for call, table in enumerate(points):
        set_spec = pl.BlockSpec((1, lines, LANES), functools.partial(lambda call, s: (call * per_call + s, 0, 0), call))
        partial.append(
            pl.pallas_call(
                functools.partial(collect_kernel, planes, height, unroll),
                grid=(per_call,),
                in_specs=[slab_spec, steps_spec, set_spec, set_spec],
                out_specs=pl.BlockSpec((1, 2 * rows, CHUNK), lambda s: (s, 0, 0)),
                out_shape=jax.ShapeDtypeStruct((per_call, 2 * rows, CHUNK), F32),
                scratch_shapes=point_scratch
                + [
                    pltpu.VMEM((planes, 8 * height, LANES), BF),
                    pltpu.VMEM((rows, 4 * height, CHUNK), F32),
                ],
                compiler_params=params(),
                name="collect_points",
            )(table, table, keep, other)
        )
    if half <= 4:
        arrived = [partial[0]] + [swap(partial[j], 2 * j) for j in range(1, half)]
    else:
        ids = jnp.arange(slabs)
        blocks = jnp.take(partial[0], (ids ^ me) // 2, axis=0)
        blocks = jnp.where(((ids ^ me) % 2 == 0)[:, None, None], blocks, 0.0)
        arrived = [lax.all_to_all(blocks, "grid", split_axis=0, concat_axis=0, tiled=True)]
    applied, part = pl.pallas_call(
        functools.partial(unsort_kernel, len(arrived)),
        out_shape=(
            jax.ShapeDtypeStruct((2, 2 * rows, LANES), F32),
            jax.ShapeDtypeStruct((slabs, 2 * bands, LANES), F32),
        ),
        scratch_shapes=[pltpu.VMEM((4 * rows, CHUNK), BF), pltpu.VMEM((2, rows, CHUNK), F32)],
        compiler_params=params(),
        name="unsort_points",
    )(*arrived, dest, coefs)
    sums = lax.all_to_all(part, "grid", split_axis=0, concat_axis=0, tiled=True)
    resid, sub = pl.pallas_call(
        functools.partial(residual_kernel, 1.0 / (count * slabs)),
        out_shape=(
            jax.ShapeDtypeStruct((2, 2 * rows, LANES), F32),
            jax.ShapeDtypeStruct((2, bands, 1), F32),
        ),
        compiler_params=params(),
        name="residual",
    )(sums, applied, coefs)
    return sub, resid.reshape(2, 1, count)


def solution(mesh):
    return jax.shard_map(
        local,
        mesh=mesh,
        in_specs=(P(None, "band", "grid"), P("grid"), P("grid", None)),
        out_specs=(P(None, None, "band"), P(None, "band", "grid")),
        check_vma=False,
    )
```

```python
import functools
import math

import jax
import jax.numpy as jnp
import numpy as np
from jax import lax
from jax.experimental import pallas as pl
from jax.experimental.pallas import tpu as pltpu
from jax.sharding import PartitionSpec as P

N = 192
CHUNK = 256
LANES = 128
BF = jnp.bfloat16
F32 = jnp.float32
NT = (((1,), (1,)), ((), ()))


def split(x):
    high = x.astype(BF)
    low = (x - high.astype(F32)).astype(BF)
    return high, low


def mm(a, b):
    return jnp.dot(a, b, preferred_element_type=F32)


def split_table(table):
    table = table.astype(np.float32)
    high = table.astype(BF)
    low = (table - high.astype(np.float32)).astype(BF)
    return high, low


@functools.cache
def tables():
    pos = np.arange(N)
    angle = 2.0 * math.pi * ((pos[:, None] * pos[None, :]) % N) / N
    cb, sb = np.cos(angle), np.sin(angle)
    order = np.concatenate([pos[0::2], pos[1::2]])
    co, so = cb[order], sb[order]
    b_fwd = np.block([[co, -so], [so, co]])
    b_inv = np.block([[co.T, so.T], [-so.T, co.T]])
    freq = np.arange(LANES)
    freq = np.where(freq < 64, freq, freq - LANES)
    keep = (np.abs(freq) < 48)[:, None]
    angle = 2.0 * math.pi * ((freq[:, None] * pos[None, :]) % N) / N
    cc, sc = np.cos(angle) * keep, np.sin(angle) * keep
    c_fwd = np.block([[cc, sc], [-sc, cc]])
    c_inv = np.block([[cc.T, -sc.T], [sc.T, cc.T]]) / float(N) ** 3
    bf_h, bf_l = split_table(b_fwd)
    bi_h, bi_l = split_table(b_inv)
    cf_h, cf_l = split_table(c_fwd)
    ci_h, ci_l = split_table(c_inv)
    return (
        np.concatenate([bf_h, bf_l, bf_h], axis=1),
        np.concatenate([cf_h, cf_l, cf_h], axis=0),
        np.concatenate([ci_h, ci_l, ci_h], axis=0),
        np.concatenate([bi_h, bi_l, bi_h], axis=1),
    )


def fold(x):
    half = x.shape[0] // 2
    return jnp.concatenate([x[:half], x[half:]], axis=1)


def unfold(x):
    return jnp.concatenate([x[:, :LANES], x[:, LANES:]], axis=0)


def wide(row, count):
    tile = jnp.broadcast_to(row, (16, row.shape[1])).astype(BF)
    return jnp.concatenate([tile] * (count // 16), axis=0)


def ident(count):
    return lax.broadcasted_iota(jnp.int32, (count, LANES), 0).astype(F32).astype(BF)


def equal(row, ids):
    code = wide(row, ids.shape[0])
    return code == jnp.concatenate([ids, ids], axis=1)


def one_hot(row, ids):
    one = jnp.ones((ids.shape[0], CHUNK), BF)
    return jnp.where(equal(row, ids), one, jnp.zeros_like(one))


def floor_div(x, divisor):
    return jnp.floor((x + 0.5) * (1.0 / divisor))


def sort_kernel(planes, m_ref, c_ref, out_ref, d_ref, acc_ref, val_ref, gb_ref, cum_ref, tot_ref, lane_ref):
    rows = gb_ref.shape[0]
    m = fold(m_ref[...]).astype(F32)
    line = floor_div(m, N)
    gc = m - N * line
    ga = floor_div(line, planes)
    gb = line - planes * ga
    ga = jnp.where(ga < 96, ga, ga - 96)
    gc = jnp.where(gc < 96, gc, gc - 64)
    gb_ref[...] = gb
    lane_r = lax.broadcasted_iota(jnp.int32, (CHUNK, 2 * CHUNK), 0)
    lane_c = lax.broadcasted_iota(jnp.int32, (CHUNK, 2 * CHUNK), 1)
    tri = jnp.where((lane_r < lane_c) | (lane_c >= CHUNK), 1.0, 0.0).astype(BF)
    row_r = lax.broadcasted_iota(jnp.int32, (rows + 16, rows), 0)
    row_c = lax.broadcasted_iota(jnp.int32, (rows + 16, rows), 1)
    below = jnp.where(row_c < row_r, 1.0, 0.0).astype(BF)
    masks = [jnp.where(gb == float(g), 1.0, 0.0).astype(BF) for g in range(planes)]
    cum_ref[...] = mm(below, jnp.concatenate(masks, axis=1))
    tot_ref[...] = jnp.zeros_like(tot_ref)
    step = 3 if planes % 3 == 0 and planes > 3 else 1

    def at(g):
        return pl.ds(pl.multiple_of(g * CHUNK, CHUNK), CHUNK)

    def gather(i, carry):
        for j in range(step):
            g = i * step + j
            tot_ref[pl.ds(g, 1), :] = cum_ref[rows : rows + 8, at(g)][0:1]
        return carry

    lax.fori_loop(0, planes // step, gather, 0)
    lane_ref[...] = mm(tot_ref[...].astype(BF), tri)
    step_id = lax.broadcasted_iota(jnp.int32, (8, CHUNK), 1).astype(F32)

    def rank(i, carry):
        base, place, plane_of = carry
        for j in range(step):
            g = i * step + j
            gf = g.astype(F32)
            lanes = lane_ref[pl.ds(g, 1), :]
            here = cum_ref[0:rows, at(g)] + (lanes[:, :CHUNK] + base)
            place = jnp.where(gb_ref[...] == gf, here, place)
            base = base + lanes[:, CHUNK:]
            end = gf + jnp.floor((jnp.maximum(base, 1.0) - 1.0) * (1.0 / CHUNK))
            end = jnp.where(gf < planes - 1.0, end, 1e6)
            plane_of = plane_of + jnp.where(end < step_id, 1.0, 0.0)
        return base, place, plane_of

    _, place, plane_of = lax.fori_loop(
        0,
        planes // step,
        rank,
        (jnp.zeros((1, CHUNK), F32), jnp.zeros((rows, CHUNK), F32), jnp.zeros((8, CHUNK), F32)),
    )
    d_ref[...] = place
    re_h, re_l = split(fold(c_ref[0]))
    im_h, im_l = split(fold(c_ref[1]))
    for q, value in enumerate((re_h, re_l, im_h, im_l, ga, gb, gc)):
        val_ref[q] = value.astype(F32)
    acc_ref[...] = jnp.zeros_like(acc_ref)
    hi_id, lo_id = ident(rows), ident(CHUNK)
    zero = jnp.zeros((rows, CHUNK), BF)

    def body(i, carry):
        part = pl.ds(pl.multiple_of(i * 8, 8), 8)
        d = d_ref[part, :]
        hi = jnp.floor(d * (1.0 / CHUNK))
        lo = d - CHUNK * hi
        values = [val_ref[q, part, :] for q in range(7)]
        left, right = [], []
        for j in range(8):
            at_hi = equal(hi[j : j + 1], hi_id)
            left.append(
                jnp.concatenate([jnp.where(at_hi, wide(v[j : j + 1], rows), zero) for v in values], axis=0)
            )
            right.append(one_hot(lo[j : j + 1], lo_id))
        acc_ref[...] += lax.dot_general(
            jnp.concatenate(left, axis=1), jnp.concatenate(right, axis=1), NT, preferred_element_type=F32
        )
        return carry

    lax.fori_loop(0, rows // 8, body, 0)
    got = [acc_ref[q * rows : (q + 1) * rows] for q in range(7)]
    out_ref[0:rows] = got[0] + got[1]
    out_ref[rows : 2 * rows] = got[2] + got[3]
    out_ref[2 * rows : 3 * rows] = (got[4] * planes + got[5]) * LANES + got[6]
    out_ref[3 * rows : 3 * rows + 8] = plane_of


def sin_cos(x):
    y = x * x
    s = -1.0 / 39916800.0 + y * (1.0 / 6227020800.0)
    s = 1.0 / 362880.0 + y * s
    s = -1.0 / 5040.0 + y * s
    s = 1.0 / 120.0 + y * s
    s = -1.0 / 6.0 + y * s
    s = x + x * y * s
    c = 1.0 / 479001600.0 - y * (1.0 / 87178291200.0)
    c = -1.0 / 3628800.0 + y * c
    c = 1.0 / 40320.0 + y * c
    c = -1.0 / 720.0 + y * c
    c = 1.0 / 24.0 + y * c
    c = -0.5 + y * c
    c = 1.0 + y * c
    return s, c


def decode(cell, planes):
    line = jnp.floor(cell * (1.0 / LANES))
    gc = cell - LANES * line
    ga = floor_div(line, planes)
    gb = line - planes * ga
    freq = jnp.where(ga < 48, ga, ga - 96)
    return freq, gb, gc


def phase(freq, first):
    turn = freq * first
    turn = turn - N * jnp.floor(turn * (1.0 / N) + 0.5)
    s, c = sin_cos(turn * (math.pi / N))
    return 1.0 - 2.0 * s * s, 2.0 * s * c


def powers(freq, w_ref):
    s, c = sin_cos(freq * (2.0 * math.pi / N))
    for q in range(4):
        w_ref[4 + 2 * q] = c
        w_ref[5 + 2 * q] = s
        s, c = 2.0 * s * c, c * c - s * s


def rise(wr, wi, j):
    k = lax.broadcasted_iota(jnp.int32, (8, CHUNK), 0)
    shape = (8, CHUNK)
    er = ei = None
    for bit in range(3):
        on = (k & (1 << bit)) != 0
        fr = jnp.where(on, jnp.broadcast_to(wr[bit][j : j + 1], shape), 1.0)
        fi = jnp.where(on, jnp.broadcast_to(wi[bit][j : j + 1], shape), 0.0)
        if er is None:
            er, ei = fr, fi
        else:
            er, ei = er * fr - ei * fi, er * fi + ei * fr
    return er, ei


def firsts(planes):
    me = lax.axis_index("grid")
    return (me * planes).astype(F32), ((me ^ 1) * planes).astype(F32)


def pair_code(planes, steps_ref, code_ref, rows, step):
    g = steps_ref[0, step].astype(jnp.int32)
    c = jnp.minimum(step - g, rows - 1)
    wanted = jnp.where(step < rows + planes - 1, g, -1).astype(F32)
    code = jnp.where(code_ref[0, pl.ds(c, 1), :] == wanted, code_ref[1, pl.ds(c, 1), :], -1.0)
    return g, c, code


def spread_kernel(planes, height, unroll, slab_ref, steps_ref, own_ref, sib_ref, w_ref, code_ref, id_ref, a_ref):
    rows = a_ref.shape[0]
    freq, gb, gc = decode(slab_ref[0, 2 * rows : 3 * rows], planes)
    code_ref[0] = gb
    code_ref[1] = gc
    id_ref[...] = ident(LANES)
    re, im = slab_ref[0, 0:rows], slab_ref[0, rows : 2 * rows]
    for q, first in enumerate(firsts(planes)):
        sr, si = phase(freq, first)
        w_ref[2 * q] = re * sr - im * si
        w_ref[2 * q + 1] = re * si + im * sr
    powers(freq, w_ref)
    shape = (8, CHUNK)

    def build(i, carry):
        part = pl.ds(pl.multiple_of(i * 8, 8), 8)
        w = [w_ref[q, part, :] for q in range(12)]
        for j in range(8):
            er, ei = rise(w[4:10:2], w[5:10:2], j)
            jr = jnp.broadcast_to(w[10][j : j + 1], shape)
            ji = jnp.broadcast_to(w[11][j : j + 1], shape)
            lines = []
            for q in range(2):
                zr = jnp.broadcast_to(w[2 * q][j : j + 1], shape)
                zi = jnp.broadcast_to(w[2 * q + 1][j : j + 1], shape)
                zr, zi = er * zr - ei * zi, er * zi + ei * zr
                real, imag = [zr], [zi]
                for _ in range(height // 8 - 1):
                    zr, zi = zr * jr - zi * ji, zr * ji + zi * jr
                    real.append(zr)
                    imag.append(zi)
                lines += real + imag
            high, low = split(jnp.concatenate(lines, axis=0))
            a_ref[i * 8 + j] = jnp.concatenate([high, low], axis=0)
        return carry

    lax.fori_loop(0, rows // 8, build, 0)
    own_ref[...] = jnp.zeros_like(own_ref)
    sib_ref[...] = jnp.zeros_like(sib_ref)

    def visit(i, carry):
        ids = id_ref[...]
        for j in range(unroll):
            g, c, code = pair_code(planes, steps_ref, code_ref, rows, i * unroll + j)
            got = lax.dot_general(a_ref[c], one_hot(code, ids), NT, preferred_element_type=F32)
            got = got[: 4 * height] + got[4 * height :]
            where = pl.ds(pl.multiple_of(g * (2 * height), 8), 2 * height)
            own_ref[0, where, :] += got[: 2 * height]
            sib_ref[0, where, :] += got[2 * height :]
        return carry

    lax.fori_loop(0, -(-(rows + planes - 1) // unroll), visit, 0)


def collect_kernel(
    planes, height, unroll, slab_ref, steps_ref, own_ref, sib_ref, h_ref, w_ref, code_ref, id_ref, u2_ref, g_ref
):
    rows = g_ref.shape[0]
    freq, gb, gc = decode(slab_ref[0, 2 * rows : 3 * rows], planes)
    code_ref[0] = gb
    code_ref[1] = gc
    id_ref[...] = ident(LANES)
    for q, first in enumerate(firsts(planes)):
        w_ref[2 * q], w_ref[2 * q + 1] = phase(freq, first)
    powers(freq, w_ref)
    for g in range(planes):
        where = slice(g * 2 * height, (g + 1) * 2 * height)
        high, low = split(jnp.concatenate([own_ref[0, where, :], sib_ref[0, where, :]], axis=0))
        u2_ref[g] = jnp.concatenate([high, low], axis=0)
    g_ref[...] = jnp.zeros_like(g_ref)

    def visit(i, carry):
        ids = id_ref[...]
        for j in range(unroll):
            g, c, code = pair_code(planes, steps_ref, code_ref, rows, i * unroll + j)
            got = mm(u2_ref[g], one_hot(code, ids))
            g_ref[c] += got[: 4 * height] + got[4 * height :]
        return carry

    lax.fori_loop(0, -(-(rows + planes - 1) // unroll), visit, 0)
    shape = (8, CHUNK)

    def finish(i, carry):
        part = pl.ds(pl.multiple_of(i * 8, 8), 8)
        w = [w_ref[q, part, :] for q in range(12)]
        real, imag = [], []
        for j in range(8):
            jr = jnp.broadcast_to(w[10][j : j + 1], shape)
            ji = jnp.broadcast_to(w[11][j : j + 1], shape)
            hr = hi = 0.0
            for q in range(2):
                value = g_ref[i * 8 + j, q * 2 * height : (q + 1) * 2 * height]
                ar = value[height - 8 : height]
                ai = value[2 * height - 8 : 2 * height]
                for t in range(height // 8 - 2, -1, -1):
                    ar, ai = (
                        ar * jr + ai * ji + value[8 * t : 8 * t + 8],
                        ai * jr - ar * ji + value[height + 8 * t : height + 8 * t + 8],
                    )
                zr = jnp.broadcast_to(w[2 * q][j : j + 1], shape)
                zi = jnp.broadcast_to(w[2 * q + 1][j : j + 1], shape)
                hr, hi = hr + ar * zr + ai * zi, hi + ai * zr - ar * zi
            er, ei = rise(w[4:10:2], w[5:10:2], j)
            real.append(jnp.sum(hr * er + hi * ei, axis=0, keepdims=True))
            imag.append(jnp.sum(hi * er - hr * ei, axis=0, keepdims=True))
        h_ref[0, part, :] = jnp.concatenate(real, axis=0)
        h_ref[0, pl.ds(pl.multiple_of(rows + i * 8, 8), 8), :] = jnp.concatenate(imag, axis=0)
        return carry

    lax.fori_loop(0, rows // 8, finish, 0)


def potential_kernel(group, height, planes, calls, *refs):
    own, sib = refs[:calls], refs[calls : 2 * calls]
    v_ref, bf_ref, cf_ref, ci_ref, bi_ref = refs[2 * calls : 2 * calls + 5]
    keep_ref, send_ref, t_ref, u_ref, sems = refs[-5:]
    step = pl.program_id(0)
    me = lax.axis_index("grid")
    lines = planes * 2 * height

    def place(j, mine):
        slab = me ^ (2 * j) if mine else me ^ (2 * j + 1)
        return pl.ds(pl.multiple_of(slab * lines, 8), lines)

    half = keep_ref.shape[0]
    per_call = half // calls

    def arrivals(j):
        for q, blocks in enumerate((own, sib)):
            yield pltpu.make_async_copy(
                blocks[j // per_call].at[j % per_call], t_ref.at[place(j, q == 0)], sems.at[q, j]
            )

    def departures(j):
        for q, block in enumerate((keep_ref, send_ref)):
            yield pltpu.make_async_copy(u_ref.at[place(j, q == 0)], block.at[j], sems.at[q, j])

    @pl.when(step == 0)
    def _():
        for j in range(half):
            for copy in arrivals(j):
                copy.start()
        for j in range(half):
            for copy in arrivals(j):
                copy.wait()

    if height > planes:

        @pl.when(step == 0)
        def _():
            u_ref[...] = jnp.zeros_like(u_ref)

    stride = 2 * height
    real, imag = [], []
    for j in range(group):
        k = step * group + j
        real.append(t_ref[pl.ds(k, N, stride=stride), :])
        imag.append(t_ref[pl.ds(k + height, N, stride=stride), :])
    x = jnp.concatenate([jnp.concatenate(real, axis=1), jnp.concatenate(imag, axis=1)], axis=0)
    high, low = split(x)
    x = mm(bf_ref[...], jnp.concatenate([high, high, low], axis=0))
    x = jnp.concatenate(
        [
            jnp.concatenate([x[:N, j * LANES : (j + 1) * LANES], x[N:, j * LANES : (j + 1) * LANES]], axis=1)
            for j in range(group)
        ],
        axis=0,
    )
    high, low = split(x)
    x = mm(jnp.concatenate([high, high, low], axis=1), cf_ref[...])
    v = []
    for j in range(group):
        line = (step * group + j) % 8
        t = [v_ref[0, pl.ds(8 * q + line, N // 2, stride=24), :] for q in range(3)]
        v.append(jnp.concatenate([t[0], t[1][:, :64]], axis=1))
        v.append(jnp.concatenate([t[1][:, 64:], t[2]], axis=1))
    v = jnp.concatenate(v, axis=0)
    x = x * jnp.concatenate([v, v], axis=1)
    high, low = split(x)
    x = mm(jnp.concatenate([high, high, low], axis=1), ci_ref[...])
    x = jnp.concatenate(
        [
            jnp.concatenate([x[j * N : (j + 1) * N, q * LANES : (q + 1) * LANES] for j in range(group)], axis=1)
            for q in range(2)
        ],
        axis=0,
    )
    high, low = split(x)
    x = mm(bi_ref[...], jnp.concatenate([high, high, low], axis=0))
    for j in range(group):
        k = step * group + j
        u_ref[pl.ds(k, N, stride=stride), :] = x[:N, j * LANES : (j + 1) * LANES]
        u_ref[pl.ds(k + height, N, stride=stride), :] = x[N:, j * LANES : (j + 1) * LANES]

    @pl.when(step == pl.num_programs(0) - 1)
    def _():
        for j in range(half):
            for copy in departures(j):
                copy.start()
        for j in range(half):
            for copy in departures(j):
                copy.wait()


def unsort_kernel(arrivals, bands, *refs):
    recv_refs = refs[:arrivals]
    d_ref, *coef_refs = refs[arrivals : arrivals + 1 + bands]
    h_ref, part_ref, hl_ref, wide_ref = refs[arrivals + 1 + bands :]
    rows = d_ref.shape[0]
    total = None
    for recv in recv_refs:
        for s in range(recv.shape[0]):
            total = recv[s] if total is None else total + recv[s]
    high, low = split(total)
    hl_ref[0 : 2 * rows] = high
    hl_ref[2 * rows :] = low
    hi_id = lax.broadcasted_iota(jnp.int32, (rows, CHUNK), 0).astype(F32)
    lo_id = ident(CHUNK)

    def body(i, carry):
        part = pl.ds(pl.multiple_of(i * 8, 8), 8)
        d = d_ref[part, :]
        hi = jnp.floor(d * (1.0 / CHUNK))
        lo = d - CHUNK * hi
        real, imag = [], []
        for j in range(8):
            got = mm(hl_ref[...], one_hot(lo[j : j + 1], lo_id))
            got = got[: 2 * rows] + got[2 * rows :]
            at_hi = jnp.broadcast_to(hi[j : j + 1], (rows, CHUNK)) == hi_id
            real.append(jnp.sum(jnp.where(at_hi, got[:rows], 0.0), axis=0, keepdims=True))
            imag.append(jnp.sum(jnp.where(at_hi, got[rows:], 0.0), axis=0, keepdims=True))
        wide_ref[0, part, :] = jnp.concatenate(real, axis=0)
        wide_ref[1, part, :] = jnp.concatenate(imag, axis=0)
        return carry

    lax.fori_loop(0, rows // 8, body, 0)
    hr, hi = unfold(wide_ref[0]), unfold(wide_ref[1])
    h_ref[0] = hr
    h_ref[1] = hi
    real, imag = [], []
    for coef in coef_refs:
        cr, ci = coef[0], coef[1]
        real.append(jnp.sum(cr * hr + ci * hi, axis=0, keepdims=True))
        imag.append(jnp.sum(cr * hi - ci * hr, axis=0, keepdims=True))
    sums = jnp.concatenate(real + imag, axis=0)
    for s in range(part_ref.shape[0]):
        part_ref[s] = sums


def residual_kernel(scale, bands, sum_ref, h_ref, *refs):
    coef_refs, (out_ref, sub_ref) = refs[:bands], refs[bands:]
    band = lax.axis_index("band")
    sub = sum_ref[0]
    for s in range(1, sum_ref.shape[0]):
        sub = sub + sum_ref[s]
    sub = jnp.sum(sub, axis=1, keepdims=True) * scale
    lane = lax.broadcasted_iota(jnp.int32, (1, LANES), 1)
    hr, hi = h_ref[0], h_ref[1]
    line_re = line_im = jnp.zeros((1, LANES), F32)
    for shift, coef in enumerate(coef_refs):
        sr, si = sub[shift : shift + 1], sub[bands + shift : bands + shift + 1]
        here = lane == lax.rem(band + bands - shift, bands)
        line_re = jnp.where(here, sr, line_re)
        line_im = jnp.where(here, si, line_im)
        cr, ci = coef[0], coef[1]
        hr = hr - (sr * cr - si * ci)
        hi = hi - (si * cr + sr * ci)
    out_ref[0] = hr
    out_ref[1] = hi
    sub_ref[0] = line_re[:, :bands]
    sub_ref[1] = line_im[:, :bands]


def params(mib):
    return pltpu.CompilerParams(vmem_limit_bytes=mib * 1024 * 1024)


def cost(flops):
    return pl.CostEstimate(flops=int(flops), bytes_accessed=0, transcendentals=0)


def whole(shape):
    return pl.BlockSpec(shape, lambda *_: (0,) * len(shape))


def local(coefficients, index_map, potential):
    slabs = lax.axis_size("grid")
    bands = lax.axis_size("band")
    planes = potential.shape[0]
    count = coefficients.shape[2]
    rows = count // CHUNK
    height = -(-planes // 8) * 8
    group = 4 if planes % 4 == 0 else 1
    unroll = 22
    me = lax.axis_index("grid")
    half = slabs // 2
    coef = coefficients.reshape(2, 2 * rows, LANES)
    coefs = [coef]
    for shift in range(1, bands):
        coefs.append(lax.ppermute(coef, "band", [(i, (i + shift) % bands) for i in range(bands)]))
    table_rows = 3 * rows + 8
    sorted_pts, dest = pl.pallas_call(
        functools.partial(sort_kernel, planes),
        out_shape=(
            jax.ShapeDtypeStruct((table_rows, CHUNK), F32),
            jax.ShapeDtypeStruct((rows, CHUNK), F32),
        ),
        scratch_shapes=[
            pltpu.VMEM((7 * rows, CHUNK), F32),
            pltpu.VMEM((7, rows, CHUNK), F32),
            pltpu.VMEM((rows, CHUNK), F32),
            pltpu.VMEM((rows + 16, planes * CHUNK), F32),
            pltpu.VMEM((-(-planes // 16) * 16, CHUNK), F32),
            pltpu.VMEM((-(-planes // 16) * 16, 2 * CHUNK), F32),
        ],
        compiler_params=params(16),
        cost_estimate=cost(1e10),
        name="sort_points",
    )(index_map.reshape(2 * rows, LANES), coef)

    def swap(x, bits):
        return lax.ppermute(x, "grid", [(i, i ^ bits) for i in range(slabs)])

    if half <= 4:
        points = [sorted_pts[None]] + [swap(sorted_pts, 2 * j)[None] for j in range(1, half)]
    else:
        everything = lax.all_gather(sorted_pts, "grid")
        points = [jnp.take(everything, me ^ (2 * jnp.arange(half)), axis=0)]
    calls = len(points)
    per_call = half // calls
    lines = planes * 2 * height
    slab_spec = pl.BlockSpec((1, table_rows, CHUNK), lambda s: (s, 0, 0))
    steps_spec = pl.BlockSpec((None, 8, CHUNK), lambda s: (s, table_rows // 8 - 1, 0), memory_space=pltpu.SMEM)
    block_spec = pl.BlockSpec((1, lines, LANES), lambda s: (s, 0, 0))
    point_scratch = [pltpu.VMEM((12, rows, CHUNK), F32), pltpu.VMEM((2, rows, CHUNK), F32), pltpu.VMEM((LANES, LANES), BF)]
    spread = pl.pallas_call(
        functools.partial(spread_kernel, planes, height, unroll),
        grid=(per_call,),
        in_specs=[slab_spec, steps_spec],
        out_specs=(block_spec, block_spec),
        out_shape=(jax.ShapeDtypeStruct((per_call, lines, LANES), F32),) * 2,
        scratch_shapes=point_scratch + [pltpu.VMEM((rows, 8 * height, CHUNK), BF)],
        compiler_params=params(20),
        cost_estimate=cost(8e9),
        name="spread_points",
    )
    own, sib = [], []
    for table in points:
        mine, theirs = spread(table, table)
        own.append(mine)
        sib.append(swap(theirs, 1))
    cells = potential if height == planes else jnp.pad(potential, ((0, height - planes), (0, 0)))
    cells = cells.reshape(height // 8, 8, N * N // LANES, LANES).transpose(0, 2, 1, 3)
    cells = cells.reshape(height // 8, N * N // 16, LANES)
    constants = [jnp.asarray(t) for t in tables()]
    anywhere = pl.BlockSpec(memory_space=pl.ANY)
    keep, send = pl.pallas_call(
        functools.partial(potential_kernel, group, height, planes, calls),
        grid=(planes // group,),
        in_specs=[anywhere] * (2 * calls)
        + [pl.BlockSpec((1, N * N // 16, LANES), lambda i: (i * group // 8, 0, 0))]
        + [whole(t.shape) for t in constants]
        + [anywhere] * (bands - 1),
        out_specs=(anywhere, anywhere),
        out_shape=(jax.ShapeDtypeStruct((half, lines, LANES), F32),) * 2,
        scratch_shapes=[
            pltpu.VMEM((slabs * lines, LANES), F32),
            pltpu.VMEM((slabs * lines, LANES), F32),
            pltpu.SemaphoreType.DMA((2, half)),
        ],
        compiler_params=params(40),
        cost_estimate=cost(4e10),
        name="apply_potential",
    )(*own, *sib, cells, *constants, *coefs[1:])
    other = swap(send, 1)
    partial = []
    for call, table in enumerate(points):
        set_spec = pl.BlockSpec((1, lines, LANES), functools.partial(lambda call, s: (call * per_call + s, 0, 0), call))
        partial.append(
            pl.pallas_call(
                functools.partial(collect_kernel, planes, height, unroll),
                grid=(per_call,),
                in_specs=[slab_spec, steps_spec, set_spec, set_spec],
                out_specs=pl.BlockSpec((1, 2 * rows, CHUNK), lambda s: (s, 0, 0)),
                out_shape=jax.ShapeDtypeStruct((per_call, 2 * rows, CHUNK), F32),
                scratch_shapes=point_scratch
                + [
                    pltpu.VMEM((planes, 8 * height, LANES), BF),
                    pltpu.VMEM((rows, 4 * height, CHUNK), F32),
                ],
                compiler_params=params(24),
                cost_estimate=cost(8e9),
                name="collect_points",
            )(table, table, keep, other)
        )
    if half <= 4:
        arrived = [partial[0]] + [swap(partial[j], 2 * j) for j in range(1, half)]
    else:
        ids = jnp.arange(slabs)
        blocks = jnp.take(partial[0], (ids ^ me) // 2, axis=0)
        blocks = jnp.where(((ids ^ me) % 2 == 0)[:, None, None], blocks, 0.0)
        arrived = [lax.all_to_all(blocks, "grid", split_axis=0, concat_axis=0, tiled=True)]
    applied, part = pl.pallas_call(
        functools.partial(unsort_kernel, len(arrived), bands),
        out_shape=(
            jax.ShapeDtypeStruct((2, 2 * rows, LANES), F32),
            jax.ShapeDtypeStruct((slabs, 2 * bands, LANES), F32),
        ),
        scratch_shapes=[pltpu.VMEM((4 * rows, CHUNK), BF), pltpu.VMEM((2, rows, CHUNK), F32)],
        compiler_params=params(12),
        cost_estimate=cost(6e9),
        name="unsort_points",
    )(*arrived, dest, *coefs)
    sums = lax.all_to_all(part, "grid", split_axis=0, concat_axis=0, tiled=True)
    resid, sub = pl.pallas_call(
        functools.partial(residual_kernel, 1.0 / (count * slabs), bands),
        out_shape=(
            jax.ShapeDtypeStruct((2, 2 * rows, LANES), F32),
            jax.ShapeDtypeStruct((2, 1, bands), F32),
        ),
        compiler_params=params(8),
        cost_estimate=cost(2e9),
        name="residual",
    )(sums, applied, *coefs)
    return sub.transpose(0, 2, 1), resid.reshape(2, 1, count)


def solution(mesh):
    return jax.shard_map(
        local,
        mesh=mesh,
        in_specs=(P(None, "band", "grid"), P("grid"), P("grid", None)),
        out_specs=(P(None, None, "band"), P(None, "band", "grid")),
        check_vma=False,
    )
```

```python
import functools
import math

import jax
import jax.numpy as jnp
import numpy as np
from jax import lax
from jax.experimental import pallas as pl
from jax.experimental.pallas import tpu as pltpu
from jax.sharding import PartitionSpec as P

N = 192
CHUNK = 256
LANES = 128
BF = jnp.bfloat16
F32 = jnp.float32
NT = (((1,), (1,)), ((), ()))


def split(x):
    high = x.astype(BF)
    low = (x - high.astype(F32)).astype(BF)
    return high, low


def mm(a, b):
    return jnp.dot(a, b, preferred_element_type=F32)


def split_table(table):
    table = table.astype(np.float32)
    high = table.astype(BF)
    low = (table - high.astype(np.float32)).astype(BF)
    return high, low


@functools.cache
def tables():
    pos = np.arange(N)
    angle = 2.0 * math.pi * ((pos[:, None] * pos[None, :]) % N) / N
    cb, sb = np.cos(angle), np.sin(angle)
    order = np.concatenate([pos[0::2], pos[1::2]])
    co, so = cb[order], sb[order]
    b_fwd = np.block([[co, -so], [so, co]])
    b_inv = np.block([[co.T, so.T], [-so.T, co.T]])
    freq = np.arange(LANES)
    freq = np.where(freq < 64, freq, freq - LANES)
    keep = (np.abs(freq) < 48)[:, None]
    angle = 2.0 * math.pi * ((freq[:, None] * pos[None, :]) % N) / N
    cc, sc = np.cos(angle) * keep, np.sin(angle) * keep
    c_fwd = np.block([[cc, sc], [-sc, cc]])
    c_inv = np.block([[cc.T, -sc.T], [sc.T, cc.T]]) / float(N) ** 3
    bf_h, bf_l = split_table(b_fwd)
    bi_h, bi_l = split_table(b_inv)
    cf_h, cf_l = split_table(c_fwd)
    ci_h, ci_l = split_table(c_inv)
    return (
        np.concatenate([bf_h, bf_l, bf_h], axis=1),
        np.concatenate([cf_h, cf_l, cf_h], axis=0),
        np.concatenate([ci_h, ci_l, ci_h], axis=0),
        np.concatenate([bi_h, bi_l, bi_h], axis=1),
    )


def fold(x):
    half = x.shape[0] // 2
    return jnp.concatenate([x[:half], x[half:]], axis=1)


def unfold(x):
    return jnp.concatenate([x[:, :LANES], x[:, LANES:]], axis=0)


def wide(row, count):
    tile = jnp.broadcast_to(row, (16, row.shape[1])).astype(BF)
    return jnp.concatenate([tile] * (count // 16), axis=0)


def ident(count):
    return lax.broadcasted_iota(jnp.int32, (count, LANES), 0).astype(F32).astype(BF)


def equal(row, ids):
    code = wide(row, ids.shape[0])
    return code == jnp.concatenate([ids, ids], axis=1)


def one_hot(row, ids):
    one = jnp.ones((ids.shape[0], CHUNK), BF)
    return jnp.where(equal(row, ids), one, jnp.zeros_like(one))


def floor_div(x, divisor):
    return jnp.floor((x + 0.5) * (1.0 / divisor))


def sort_kernel(planes, m_ref, c_ref, out_ref, d_ref, acc_ref, val_ref, gb_ref, cum_ref, tot_ref, lane_ref):
    rows = gb_ref.shape[0]
    m = fold(m_ref[...]).astype(F32)
    line = floor_div(m, N)
    gc = m - N * line
    ga = floor_div(line, planes)
    gb = line - planes * ga
    ga = jnp.where(ga < 96, ga, ga - 96)
    gc = jnp.where(gc < 96, gc, gc - 64)
    gb_ref[...] = gb
    lane_r = lax.broadcasted_iota(jnp.int32, (CHUNK, 2 * CHUNK), 0)
    lane_c = lax.broadcasted_iota(jnp.int32, (CHUNK, 2 * CHUNK), 1)
    tri = jnp.where((lane_r < lane_c) | (lane_c >= CHUNK), 1.0, 0.0).astype(BF)
    row_r = lax.broadcasted_iota(jnp.int32, (rows + 16, rows), 0)
    row_c = lax.broadcasted_iota(jnp.int32, (rows + 16, rows), 1)
    below = jnp.where(row_c < row_r, 1.0, 0.0).astype(BF)
    masks = [jnp.where(gb == float(g), 1.0, 0.0).astype(BF) for g in range(planes)]
    cum_ref[...] = mm(below, jnp.concatenate(masks, axis=1))
    tot_ref[...] = jnp.zeros_like(tot_ref)
    step = 3 if planes % 3 == 0 and planes > 3 else 1

    def at(g):
        return pl.ds(pl.multiple_of(g * CHUNK, CHUNK), CHUNK)

    def gather(i, carry):
        for j in range(step):
            g = i * step + j
            tot_ref[pl.ds(g, 1), :] = cum_ref[rows : rows + 8, at(g)][0:1]
        return carry

    lax.fori_loop(0, planes // step, gather, 0)
    lane_ref[...] = mm(tot_ref[...].astype(BF), tri)
    step_id = lax.broadcasted_iota(jnp.int32, (8, CHUNK), 1).astype(F32)

    def rank(i, carry):
        base, place, plane_of = carry
        for j in range(step):
            g = i * step + j
            gf = g.astype(F32)
            lanes = lane_ref[pl.ds(g, 1), :]
            here = cum_ref[0:rows, at(g)] + (lanes[:, :CHUNK] + base)
            place = jnp.where(gb_ref[...] == gf, here, place)
            base = base + lanes[:, CHUNK:]
            end = gf + jnp.floor((jnp.maximum(base, 1.0) - 1.0) * (1.0 / CHUNK))
            end = jnp.where(gf < planes - 1.0, end, 1e6)
            plane_of = plane_of + jnp.where(end < step_id, 1.0, 0.0)
        return base, place, plane_of

    _, place, plane_of = lax.fori_loop(
        0,
        planes // step,
        rank,
        (jnp.zeros((1, CHUNK), F32), jnp.zeros((rows, CHUNK), F32), jnp.zeros((8, CHUNK), F32)),
    )
    d_ref[...] = place
    re_h, re_l = split(fold(c_ref[0]))
    im_h, im_l = split(fold(c_ref[1]))
    for q, value in enumerate((re_h, re_l, im_h, im_l, ga, gb, gc)):
        val_ref[q] = value.astype(F32)
    acc_ref[...] = jnp.zeros_like(acc_ref)
    hi_id, lo_id = ident(rows), ident(CHUNK)
    zero = jnp.zeros((rows, CHUNK), BF)

    def body(i, carry):
        part = pl.ds(pl.multiple_of(i * 8, 8), 8)
        d = d_ref[part, :]
        hi = jnp.floor(d * (1.0 / CHUNK))
        lo = d - CHUNK * hi
        values = [val_ref[q, part, :] for q in range(7)]
        left, right = [], []
        for j in range(8):
            at_hi = equal(hi[j : j + 1], hi_id)
            left.append(
                jnp.concatenate([jnp.where(at_hi, wide(v[j : j + 1], rows), zero) for v in values], axis=0)
            )
            right.append(one_hot(lo[j : j + 1], lo_id))
        acc_ref[...] += lax.dot_general(
            jnp.concatenate(left, axis=1), jnp.concatenate(right, axis=1), NT, preferred_element_type=F32
        )
        return carry

    lax.fori_loop(0, rows // 8, body, 0)
    got = [acc_ref[q * rows : (q + 1) * rows] for q in range(7)]
    out_ref[0:rows] = got[0] + got[1]
    out_ref[rows : 2 * rows] = got[2] + got[3]
    out_ref[2 * rows : 3 * rows] = (got[4] * planes + got[5]) * LANES + got[6]
    out_ref[3 * rows : 3 * rows + 8] = plane_of


def sin_cos(x):
    y = x * x
    s = -1.0 / 39916800.0 + y * (1.0 / 6227020800.0)
    s = 1.0 / 362880.0 + y * s
    s = -1.0 / 5040.0 + y * s
    s = 1.0 / 120.0 + y * s
    s = -1.0 / 6.0 + y * s
    s = x + x * y * s
    c = 1.0 / 479001600.0 - y * (1.0 / 87178291200.0)
    c = -1.0 / 3628800.0 + y * c
    c = 1.0 / 40320.0 + y * c
    c = -1.0 / 720.0 + y * c
    c = 1.0 / 24.0 + y * c
    c = -0.5 + y * c
    c = 1.0 + y * c
    return s, c


def decode(cell, planes):
    line = jnp.floor(cell * (1.0 / LANES))
    gc = cell - LANES * line
    ga = floor_div(line, planes)
    gb = line - planes * ga
    freq = jnp.where(ga < 48, ga, ga - 96)
    return freq, gb, gc


def phase(freq, first):
    turn = freq * first
    turn = turn - N * jnp.floor(turn * (1.0 / N) + 0.5)
    s, c = sin_cos(turn * (math.pi / N))
    return 1.0 - 2.0 * s * s, 2.0 * s * c


def powers(freq, w_ref):
    s, c = sin_cos(freq * (2.0 * math.pi / N))
    for q in range(4):
        w_ref[4 + 2 * q] = c
        w_ref[5 + 2 * q] = s
        s, c = 2.0 * s * c, c * c - s * s


def firsts(planes):
    me = lax.axis_index("grid")
    return (me * planes).astype(F32), ((me ^ 1) * planes).astype(F32)


def pair_code(planes, steps_ref, code_ref, rows, step):
    g = steps_ref[0, step].astype(jnp.int32)
    c = jnp.minimum(step - g, rows - 1)
    wanted = jnp.where(step < rows + planes - 1, g, -1).astype(F32)
    code = jnp.where(code_ref[0, pl.ds(c, 1), :] == wanted, code_ref[1, pl.ds(c, 1), :], -1.0)
    return g, c, code


def row_of(ref, index, c):
    return jnp.broadcast_to(ref[index, pl.ds(c, 1), :], (8, CHUNK))


def rise(w_ref, c):
    k = lax.broadcasted_iota(jnp.int32, (8, CHUNK), 0)
    er = ei = None
    for bit in range(3):
        on = (k & (1 << bit)) != 0
        fr = jnp.where(on, row_of(w_ref, 4 + 2 * bit, c), 1.0)
        fi = jnp.where(on, row_of(w_ref, 5 + 2 * bit, c), 0.0)
        if er is None:
            er, ei = fr, fi
        else:
            er, ei = er * fr - ei * fi, er * fi + ei * fr
    return er, ei


def prepare(planes, cell, w_ref, code_ref, id_ref):
    freq, gb, gc = decode(cell, planes)
    code_ref[0] = gb
    code_ref[1] = gc
    id_ref[...] = ident(LANES)
    for q, first in enumerate(firsts(planes)):
        w_ref[2 * q], w_ref[2 * q + 1] = phase(freq, first)
    powers(freq, w_ref)


def spread_kernel(planes, height, unroll, slab_ref, steps_ref, own_ref, sib_ref, w_ref, code_ref, id_ref):
    rows = w_ref.shape[1]
    prepare(planes, slab_ref[0, 2 * rows : 3 * rows], w_ref, code_ref, id_ref)
    re, im = slab_ref[0, 0:rows], slab_ref[0, rows : 2 * rows]
    for q in range(2):
        sr, si = w_ref[2 * q], w_ref[2 * q + 1]
        w_ref[2 * q] = re * sr - im * si
        w_ref[2 * q + 1] = re * si + im * sr
    own_ref[...] = jnp.zeros_like(own_ref)
    sib_ref[...] = jnp.zeros_like(sib_ref)

    def visit(i, carry):
        ids = id_ref[...]
        for j in range(unroll):
            g, c, code = pair_code(planes, steps_ref, code_ref, rows, i * unroll + j)
            er, ei = rise(w_ref, c)
            jr, ji = row_of(w_ref, 10, c), row_of(w_ref, 11, c)
            lines = []
            for q in range(2):
                zr, zi = row_of(w_ref, 2 * q, c), row_of(w_ref, 2 * q + 1, c)
                zr, zi = er * zr - ei * zi, er * zi + ei * zr
                real, imag = [zr], [zi]
                for _ in range(height // 8 - 1):
                    zr, zi = zr * jr - zi * ji, zr * ji + zi * jr
                    real.append(zr)
                    imag.append(zi)
                lines += real + imag
            high, low = split(jnp.concatenate(lines, axis=0))
            got = lax.dot_general(
                jnp.concatenate([high, low], axis=0), one_hot(code, ids), NT, preferred_element_type=F32
            )
            got = got[: 4 * height] + got[4 * height :]
            where = pl.ds(pl.multiple_of(g * (2 * height), 8), 2 * height)
            own_ref[0, where, :] += got[: 2 * height]
            sib_ref[0, where, :] += got[2 * height :]
        return carry

    lax.fori_loop(0, -(-(rows + planes - 1) // unroll), visit, 0)


def collect_kernel(
    planes, height, unroll, slab_ref, steps_ref, own_ref, sib_ref, h_ref, w_ref, code_ref, id_ref, u2_ref
):
    rows = w_ref.shape[1]
    prepare(planes, slab_ref[0, 2 * rows : 3 * rows], w_ref, code_ref, id_ref)
    for g in range(planes):
        where = slice(g * 2 * height, (g + 1) * 2 * height)
        high, low = split(jnp.concatenate([own_ref[0, where, :], sib_ref[0, where, :]], axis=0))
        u2_ref[g] = jnp.concatenate([high, low], axis=0)
    h_ref[...] = jnp.zeros_like(h_ref)

    def visit(i, carry):
        ids = id_ref[...]
        for j in range(unroll):
            g, c, code = pair_code(planes, steps_ref, code_ref, rows, i * unroll + j)
            got = mm(u2_ref[g], one_hot(code, ids))
            got = got[: 4 * height] + got[4 * height :]
            jr, ji = row_of(w_ref, 10, c), row_of(w_ref, 11, c)
            hr = hi = 0.0
            for q in range(2):
                value = got[q * 2 * height : (q + 1) * 2 * height]
                ar = value[height - 8 : height]
                ai = value[2 * height - 8 : 2 * height]
                for t in range(height // 8 - 2, -1, -1):
                    ar, ai = (
                        ar * jr + ai * ji + value[8 * t : 8 * t + 8],
                        ai * jr - ar * ji + value[height + 8 * t : height + 8 * t + 8],
                    )
                zr, zi = row_of(w_ref, 2 * q, c), row_of(w_ref, 2 * q + 1, c)
                hr, hi = hr + ar * zr + ai * zi, hi + ai * zr - ar * zi
            er, ei = rise(w_ref, c)
            h_ref[0, pl.ds(c, 1), :] += jnp.sum(hr * er + hi * ei, axis=0, keepdims=True)
            h_ref[0, pl.ds(rows + c, 1), :] += jnp.sum(hi * er - hr * ei, axis=0, keepdims=True)
        return carry

    lax.fori_loop(0, -(-(rows + planes - 1) // unroll), visit, 0)


def potential_kernel(group, height, planes, calls, *refs):
    own, sib = refs[:calls], refs[calls : 2 * calls]
    v_ref, bf_ref, cf_ref, ci_ref, bi_ref = refs[2 * calls : 2 * calls + 5]
    keep_ref, send_ref, t_ref, u_ref, sems = refs[-5:]
    step = pl.program_id(0)
    me = lax.axis_index("grid")
    lines = planes * 2 * height

    def place(j, mine):
        slab = me ^ (2 * j) if mine else me ^ (2 * j + 1)
        return pl.ds(pl.multiple_of(slab * lines, 8), lines)

    half = keep_ref.shape[0]
    per_call = half // calls

    def arrivals(j):
        for q, blocks in enumerate((own, sib)):
            yield pltpu.make_async_copy(
                blocks[j // per_call].at[j % per_call], t_ref.at[place(j, q == 0)], sems.at[q, j]
            )

    def departures(j):
        for q, block in enumerate((keep_ref, send_ref)):
            yield pltpu.make_async_copy(u_ref.at[place(j, q == 0)], block.at[j], sems.at[q, j])

    @pl.when(step == 0)
    def _():
        for j in range(half):
            for copy in arrivals(j):
                copy.start()
        for j in range(half):
            for copy in arrivals(j):
                copy.wait()

    if height > planes:

        @pl.when(step == 0)
        def _():
            u_ref[...] = jnp.zeros_like(u_ref)

    stride = 2 * height
    real, imag = [], []
    for j in range(group):
        k = step * group + j
        real.append(t_ref[pl.ds(k, N, stride=stride), :])
        imag.append(t_ref[pl.ds(k + height, N, stride=stride), :])
    x = jnp.concatenate([jnp.concatenate(real, axis=1), jnp.concatenate(imag, axis=1)], axis=0)
    high, low = split(x)
    x = mm(bf_ref[...], jnp.concatenate([high, high, low], axis=0))
    x = jnp.concatenate(
        [
            jnp.concatenate([x[:N, j * LANES : (j + 1) * LANES], x[N:, j * LANES : (j + 1) * LANES]], axis=1)
            for j in range(group)
        ],
        axis=0,
    )
    high, low = split(x)
    x = mm(jnp.concatenate([high, high, low], axis=1), cf_ref[...])
    v = []
    for j in range(group):
        line = (step * group + j) % 8
        t = [v_ref[0, pl.ds(8 * q + line, N // 2, stride=24), :] for q in range(3)]
        v.append(jnp.concatenate([t[0], t[1][:, :64]], axis=1))
        v.append(jnp.concatenate([t[1][:, 64:], t[2]], axis=1))
    v = jnp.concatenate(v, axis=0)
    x = x * jnp.concatenate([v, v], axis=1)
    high, low = split(x)
    x = mm(jnp.concatenate([high, high, low], axis=1), ci_ref[...])
    x = jnp.concatenate(
        [
            jnp.concatenate([x[j * N : (j + 1) * N, q * LANES : (q + 1) * LANES] for j in range(group)], axis=1)
            for q in range(2)
        ],
        axis=0,
    )
    high, low = split(x)
    x = mm(bi_ref[...], jnp.concatenate([high, high, low], axis=0))
    for j in range(group):
        k = step * group + j
        u_ref[pl.ds(k, N, stride=stride), :] = x[:N, j * LANES : (j + 1) * LANES]
        u_ref[pl.ds(k + height, N, stride=stride), :] = x[N:, j * LANES : (j + 1) * LANES]

    @pl.when(step == pl.num_programs(0) - 1)
    def _():
        for j in range(half):
            for copy in departures(j):
                copy.start()
        for j in range(half):
            for copy in departures(j):
                copy.wait()


def unsort_kernel(arrivals, bands, *refs):
    recv_refs = refs[:arrivals]
    d_ref, *coef_refs = refs[arrivals : arrivals + 1 + bands]
    h_ref, part_ref, hl_ref, wide_ref = refs[arrivals + 1 + bands :]
    rows = d_ref.shape[0]
    total = None
    for recv in recv_refs:
        for s in range(recv.shape[0]):
            total = recv[s] if total is None else total + recv[s]
    high, low = split(total)
    hl_ref[0 : 2 * rows] = high
    hl_ref[2 * rows :] = low
    hi_id = lax.broadcasted_iota(jnp.int32, (rows, CHUNK), 0).astype(F32)
    lo_id = ident(CHUNK)

    def body(i, carry):
        part = pl.ds(pl.multiple_of(i * 8, 8), 8)
        d = d_ref[part, :]
        hi = jnp.floor(d * (1.0 / CHUNK))
        lo = d - CHUNK * hi
        real, imag = [], []
        for j in range(8):
            got = mm(hl_ref[...], one_hot(lo[j : j + 1], lo_id))
            got = got[: 2 * rows] + got[2 * rows :]
            at_hi = jnp.broadcast_to(hi[j : j + 1], (rows, CHUNK)) == hi_id
            real.append(jnp.sum(jnp.where(at_hi, got[:rows], 0.0), axis=0, keepdims=True))
            imag.append(jnp.sum(jnp.where(at_hi, got[rows:], 0.0), axis=0, keepdims=True))
        wide_ref[0, part, :] = jnp.concatenate(real, axis=0)
        wide_ref[1, part, :] = jnp.concatenate(imag, axis=0)
        return carry

    lax.fori_loop(0, rows // 8, body, 0)
    hr, hi = unfold(wide_ref[0]), unfold(wide_ref[1])
    h_ref[0] = hr
    h_ref[1] = hi
    real, imag = [], []
    for coef in coef_refs:
        cr, ci = coef[0], coef[1]
        real.append(jnp.sum(cr * hr + ci * hi, axis=0, keepdims=True))
        imag.append(jnp.sum(cr * hi - ci * hr, axis=0, keepdims=True))
    sums = jnp.concatenate(real + imag, axis=0)
    for s in range(part_ref.shape[0]):
        part_ref[s] = sums


def residual_kernel(scale, bands, sum_ref, h_ref, *refs):
    coef_refs, (out_ref, sub_ref) = refs[:bands], refs[bands:]
    band = lax.axis_index("band")
    sub = sum_ref[0]
    for s in range(1, sum_ref.shape[0]):
        sub = sub + sum_ref[s]
    sub = jnp.sum(sub, axis=1, keepdims=True) * scale
    lane = lax.broadcasted_iota(jnp.int32, (1, LANES), 1)
    hr, hi = h_ref[0], h_ref[1]
    line_re = line_im = jnp.zeros((1, LANES), F32)
    for shift, coef in enumerate(coef_refs):
        sr, si = sub[shift : shift + 1], sub[bands + shift : bands + shift + 1]
        here = lane == lax.rem(band + bands - shift, bands)
        line_re = jnp.where(here, sr, line_re)
        line_im = jnp.where(here, si, line_im)
        cr, ci = coef[0], coef[1]
        hr = hr - (sr * cr - si * ci)
        hi = hi - (si * cr + sr * ci)
    out_ref[0] = hr
    out_ref[1] = hi
    sub_ref[0] = line_re[:, :bands]
    sub_ref[1] = line_im[:, :bands]


def params(mib):
    return pltpu.CompilerParams(vmem_limit_bytes=mib * 1024 * 1024)


def cost(flops):
    return pl.CostEstimate(flops=int(flops), bytes_accessed=0, transcendentals=0)


def whole(shape):
    return pl.BlockSpec(shape, lambda *_: (0,) * len(shape))


def local(coefficients, index_map, potential):
    slabs = lax.axis_size("grid")
    bands = lax.axis_size("band")
    planes = potential.shape[0]
    count = coefficients.shape[2]
    rows = count // CHUNK
    height = -(-planes // 8) * 8
    group = 8 if planes % 8 == 0 else 1
    unroll = 22
    me = lax.axis_index("grid")
    half = slabs // 2
    coef = coefficients.reshape(2, 2 * rows, LANES)
    table_rows = 3 * rows + 8
    sorted_pts, dest = pl.pallas_call(
        functools.partial(sort_kernel, planes),
        out_shape=(
            jax.ShapeDtypeStruct((table_rows, CHUNK), F32),
            jax.ShapeDtypeStruct((rows, CHUNK), F32),
        ),
        scratch_shapes=[
            pltpu.VMEM((7 * rows, CHUNK), F32),
            pltpu.VMEM((7, rows, CHUNK), F32),
            pltpu.VMEM((rows, CHUNK), F32),
            pltpu.VMEM((rows + 16, planes * CHUNK), F32),
            pltpu.VMEM((-(-planes // 16) * 16, CHUNK), F32),
            pltpu.VMEM((-(-planes // 16) * 16, 2 * CHUNK), F32),
        ],
        compiler_params=params(16),
        cost_estimate=cost(1e10),
        name="sort_points",
    )(index_map.reshape(2 * rows, LANES), coef)

    def swap(x, bits):
        return lax.ppermute(x, "grid", [(i, i ^ bits) for i in range(slabs)])

    if half <= 4:
        points = [sorted_pts[None]] + [swap(sorted_pts, 2 * j)[None] for j in range(1, half)]
    else:
        everything = lax.all_gather(sorted_pts, "grid")
        points = [jnp.take(everything, me ^ (2 * jnp.arange(half)), axis=0)]
    calls = len(points)
    per_call = half // calls
    lines = planes * 2 * height
    slab_spec = pl.BlockSpec((1, table_rows, CHUNK), lambda s: (s, 0, 0))
    steps_spec = pl.BlockSpec((None, 8, CHUNK), lambda s: (s, table_rows // 8 - 1, 0), memory_space=pltpu.SMEM)
    block_spec = pl.BlockSpec((1, lines, LANES), lambda s: (s, 0, 0))
    point_scratch = [pltpu.VMEM((12, rows, CHUNK), F32), pltpu.VMEM((2, rows, CHUNK), F32), pltpu.VMEM((LANES, LANES), BF)]
    spread = pl.pallas_call(
        functools.partial(spread_kernel, planes, height, unroll),
        grid=(per_call,),
        in_specs=[slab_spec, steps_spec],
        out_specs=(block_spec, block_spec),
        out_shape=(jax.ShapeDtypeStruct((per_call, lines, LANES), F32),) * 2,
        scratch_shapes=point_scratch,
        compiler_params=params(20),
        cost_estimate=cost(8e9),
        name="spread_points",
    )
    own, sib = [], []
    for table in points:
        mine, theirs = spread(table, table)
        own.append(mine)
        sib.append(swap(theirs, 1))
    cells = potential if height == planes else jnp.pad(potential, ((0, height - planes), (0, 0)))
    cells = cells.reshape(height // 8, 8, N * N // LANES, LANES).transpose(0, 2, 1, 3)
    cells = cells.reshape(height // 8, N * N // 16, LANES)
    *sib, mine = lax.optimization_barrier((*sib, coef))
    coefs = [coef]
    for shift in range(1, bands):
        coefs.append(lax.ppermute(mine, "band", [(i, (i + shift) % bands) for i in range(bands)]))
    constants = [jnp.asarray(t) for t in tables()]
    anywhere = pl.BlockSpec(memory_space=pl.ANY)
    keep, send = pl.pallas_call(
        functools.partial(potential_kernel, group, height, planes, calls),
        grid=(planes // group,),
        in_specs=[anywhere] * (2 * calls)
        + [pl.BlockSpec((1, N * N // 16, LANES), lambda i: (i * group // 8, 0, 0))]
        + [whole(t.shape) for t in constants],
        out_specs=(anywhere, anywhere),
        out_shape=(jax.ShapeDtypeStruct((half, lines, LANES), F32),) * 2,
        scratch_shapes=[
            pltpu.VMEM((slabs * lines, LANES), F32),
            pltpu.VMEM((slabs * lines, LANES), F32),
            pltpu.SemaphoreType.DMA((2, half)),
        ],
        compiler_params=params(40),
        cost_estimate=cost(4e10),
        name="apply_potential",
    )(*own, *sib, cells, *constants)
    send, *coefs = lax.optimization_barrier((send, *coefs))
    other = swap(send, 1)
    partial = []
    for call, table in enumerate(points):
        set_spec = pl.BlockSpec((1, lines, LANES), functools.partial(lambda call, s: (call * per_call + s, 0, 0), call))
        partial.append(
            pl.pallas_call(
                functools.partial(collect_kernel, planes, height, unroll),
                grid=(per_call,),
                in_specs=[slab_spec, steps_spec, set_spec, set_spec],
                out_specs=pl.BlockSpec((1, 2 * rows, CHUNK), lambda s: (s, 0, 0)),
                out_shape=jax.ShapeDtypeStruct((per_call, 2 * rows, CHUNK), F32),
                scratch_shapes=point_scratch + [pltpu.VMEM((planes, 8 * height, LANES), BF)],
                compiler_params=params(24),
                cost_estimate=cost(8e9),
                name="collect_points",
            )(table, table, keep, other)
        )
    if half <= 4:
        arrived = [partial[0]] + [swap(partial[j], 2 * j) for j in range(1, half)]
    else:
        ids = jnp.arange(slabs)
        blocks = jnp.take(partial[0], (ids ^ me) // 2, axis=0)
        blocks = jnp.where(((ids ^ me) % 2 == 0)[:, None, None], blocks, 0.0)
        arrived = [lax.all_to_all(blocks, "grid", split_axis=0, concat_axis=0, tiled=True)]
    applied, part = pl.pallas_call(
        functools.partial(unsort_kernel, len(arrived), bands),
        out_shape=(
            jax.ShapeDtypeStruct((2, 2 * rows, LANES), F32),
            jax.ShapeDtypeStruct((slabs, 2 * bands, LANES), F32),
        ),
        scratch_shapes=[pltpu.VMEM((4 * rows, CHUNK), BF), pltpu.VMEM((2, rows, CHUNK), F32)],
        compiler_params=params(12),
        cost_estimate=cost(6e9),
        name="unsort_points",
    )(*arrived, dest, *coefs)
    sums = lax.all_to_all(part, "grid", split_axis=0, concat_axis=0, tiled=True)
    resid, sub = pl.pallas_call(
        functools.partial(residual_kernel, 1.0 / (count * slabs), bands),
        out_shape=(
            jax.ShapeDtypeStruct((2, 2 * rows, LANES), F32),
            jax.ShapeDtypeStruct((2, 1, bands), F32),
        ),
        compiler_params=params(8),
        cost_estimate=cost(2e9),
        name="residual",
    )(sums, applied, *coefs)
    return sub.transpose(0, 2, 1), resid.reshape(2, 1, count)


def solution(mesh):
    return jax.shard_map(
        local,
        mesh=mesh,
        in_specs=(P(None, "band", "grid"), P("grid"), P("grid", None)),
        out_specs=(P(None, None, "band"), P(None, "band", "grid")),
        check_vma=False,
    )
```

```python
import functools
import math

import jax
import jax.numpy as jnp
import numpy as np
from jax import lax
from jax.experimental import pallas as pl
from jax.experimental.pallas import tpu as pltpu
from jax.sharding import PartitionSpec as P

N = 192
CHUNK = 256
LANES = 128
BF = jnp.bfloat16
F32 = jnp.float32
NT = (((1,), (1,)), ((), ()))


def split(x):
    high = x.astype(BF)
    low = (x - high.astype(F32)).astype(BF)
    return high, low


def mm(a, b):
    return jnp.dot(a, b, preferred_element_type=F32)


def split_table(table):
    table = table.astype(np.float32)
    high = table.astype(BF)
    low = (table - high.astype(np.float32)).astype(BF)
    return high, low


@functools.cache
def tables():
    pos = np.arange(N)
    angle = 2.0 * math.pi * ((pos[:, None] * pos[None, :]) % N) / N
    cb, sb = np.cos(angle), np.sin(angle)
    order = np.concatenate([pos[0::2], pos[1::2]])
    co, so = cb[order], sb[order]
    b_fwd = np.block([[co, -so], [so, co]])
    b_inv = np.block([[co.T, so.T], [-so.T, co.T]])
    freq = np.arange(LANES)
    freq = np.where(freq < 64, freq, freq - LANES)
    keep = (np.abs(freq) < 48)[:, None]
    angle = 2.0 * math.pi * ((freq[:, None] * pos[None, :]) % N) / N
    cc, sc = np.cos(angle) * keep, np.sin(angle) * keep
    c_fwd = np.block([[cc, sc], [-sc, cc]])
    c_inv = np.block([[cc.T, -sc.T], [sc.T, cc.T]]) / float(N) ** 3
    bf_h, bf_l = split_table(b_fwd)
    bi_h, bi_l = split_table(b_inv)
    cf_h, cf_l = split_table(c_fwd)
    ci_h, ci_l = split_table(c_inv)
    return (
        np.concatenate([bf_h, bf_l, bf_h], axis=1),
        np.concatenate([cf_h, cf_l, cf_h], axis=0),
        np.concatenate([ci_h, ci_l, ci_h], axis=0),
        np.concatenate([bi_h, bi_l, bi_h], axis=1),
    )


def fold(x):
    half = x.shape[0] // 2
    return jnp.concatenate([x[:half], x[half:]], axis=1)


def unfold(x):
    return jnp.concatenate([x[:, :LANES], x[:, LANES:]], axis=0)


def wide(row, count):
    tile = jnp.broadcast_to(row, (16, row.shape[1])).astype(BF)
    return jnp.concatenate([tile] * (count // 16), axis=0)


def ident(count):
    return lax.broadcasted_iota(jnp.int32, (count, LANES), 0).astype(F32).astype(BF)


def equal(row, ids):
    code = wide(row, ids.shape[0])
    return code == jnp.concatenate([ids, ids], axis=1)


def one_hot(row, ids):
    one = jnp.ones((ids.shape[0], CHUNK), BF)
    return jnp.where(equal(row, ids), one, jnp.zeros_like(one))


def floor_div(x, divisor):
    return jnp.floor((x + 0.5) * (1.0 / divisor))


def sort_kernel(
    planes, m_hbm, c_hbm, out_ref, d_ref, acc_ref, val_ref, gb_ref, cum_ref, tot_ref, lane_ref, m_ref, c_ref, sems
):
    rows = gb_ref.shape[0]
    fetch_m = pltpu.make_async_copy(m_hbm, m_ref, sems.at[0])
    fetch_c = pltpu.make_async_copy(c_hbm, c_ref, sems.at[1])
    fetch_m.start()
    fetch_c.start()
    fetch_m.wait()
    m = fold(m_ref[...]).astype(F32)
    line = floor_div(m, N)
    gc = m - N * line
    ga = floor_div(line, planes)
    gb = line - planes * ga
    ga = jnp.where(ga < 96, ga, ga - 96)
    gc = jnp.where(gc < 96, gc, gc - 64)
    gb_ref[...] = gb
    lane_r = lax.broadcasted_iota(jnp.int32, (CHUNK, 2 * CHUNK), 0)
    lane_c = lax.broadcasted_iota(jnp.int32, (CHUNK, 2 * CHUNK), 1)
    tri = jnp.where((lane_r < lane_c) | (lane_c >= CHUNK), 1.0, 0.0).astype(BF)
    row_r = lax.broadcasted_iota(jnp.int32, (rows + 16, rows), 0)
    row_c = lax.broadcasted_iota(jnp.int32, (rows + 16, rows), 1)
    below = jnp.where(row_c < row_r, 1.0, 0.0).astype(BF)
    masks = [jnp.where(gb == float(g), 1.0, 0.0).astype(BF) for g in range(planes)]
    cum_ref[...] = mm(below, jnp.concatenate(masks, axis=1))
    tot_ref[...] = jnp.zeros_like(tot_ref)
    step = 3 if planes % 3 == 0 and planes > 3 else 1

    def at(g):
        return pl.ds(pl.multiple_of(g * CHUNK, CHUNK), CHUNK)

    def gather(i, carry):
        for j in range(step):
            g = i * step + j
            tot_ref[pl.ds(g, 1), :] = cum_ref[rows : rows + 8, at(g)][0:1]
        return carry

    lax.fori_loop(0, planes // step, gather, 0)
    lane_ref[...] = mm(tot_ref[...].astype(BF), tri)
    step_id = lax.broadcasted_iota(jnp.int32, (8, CHUNK), 1).astype(F32)

    def rank(i, carry):
        base, place, plane_of = carry
        for j in range(step):
            g = i * step + j
            gf = g.astype(F32)
            lanes = lane_ref[pl.ds(g, 1), :]
            here = cum_ref[0:rows, at(g)] + (lanes[:, :CHUNK] + base)
            place = jnp.where(gb_ref[...] == gf, here, place)
            base = base + lanes[:, CHUNK:]
            end = gf + jnp.floor((jnp.maximum(base, 1.0) - 1.0) * (1.0 / CHUNK))
            end = jnp.where(gf < planes - 1.0, end, 1e6)
            plane_of = plane_of + jnp.where(end < step_id, 1.0, 0.0)
        return base, place, plane_of

    _, place, plane_of = lax.fori_loop(
        0,
        planes // step,
        rank,
        (jnp.zeros((1, CHUNK), F32), jnp.zeros((rows, CHUNK), F32), jnp.zeros((8, CHUNK), F32)),
    )
    d_ref[...] = place
    fetch_c.wait()
    re_h, re_l = split(fold(c_ref[0]))
    im_h, im_l = split(fold(c_ref[1]))
    for q, value in enumerate((re_h, re_l, im_h, im_l, ga, gb, gc)):
        val_ref[q] = value.astype(F32)
    acc_ref[...] = jnp.zeros_like(acc_ref)
    hi_id, lo_id = ident(rows), ident(CHUNK)
    zero = jnp.zeros((rows, CHUNK), BF)

    def body(i, carry):
        part = pl.ds(pl.multiple_of(i * 8, 8), 8)
        d = d_ref[part, :]
        hi = jnp.floor(d * (1.0 / CHUNK))
        lo = d - CHUNK * hi
        values = [val_ref[q, part, :] for q in range(7)]
        left, right = [], []
        for j in range(8):
            at_hi = equal(hi[j : j + 1], hi_id)
            left.append(
                jnp.concatenate([jnp.where(at_hi, wide(v[j : j + 1], rows), zero) for v in values], axis=0)
            )
            right.append(one_hot(lo[j : j + 1], lo_id))
        acc_ref[...] += lax.dot_general(
            jnp.concatenate(left, axis=1), jnp.concatenate(right, axis=1), NT, preferred_element_type=F32
        )
        return carry

    lax.fori_loop(0, rows // 8, body, 0)
    got = [acc_ref[q * rows : (q + 1) * rows] for q in range(7)]
    out_ref[0:rows] = got[0] + got[1]
    out_ref[rows : 2 * rows] = got[2] + got[3]
    out_ref[2 * rows : 3 * rows] = (got[4] * planes + got[5]) * LANES + got[6]
    out_ref[3 * rows : 3 * rows + 8] = plane_of


def sin_cos(x):
    y = x * x
    s = -1.0 / 39916800.0 + y * (1.0 / 6227020800.0)
    s = 1.0 / 362880.0 + y * s
    s = -1.0 / 5040.0 + y * s
    s = 1.0 / 120.0 + y * s
    s = -1.0 / 6.0 + y * s
    s = x + x * y * s
    c = 1.0 / 479001600.0 - y * (1.0 / 87178291200.0)
    c = -1.0 / 3628800.0 + y * c
    c = 1.0 / 40320.0 + y * c
    c = -1.0 / 720.0 + y * c
    c = 1.0 / 24.0 + y * c
    c = -0.5 + y * c
    c = 1.0 + y * c
    return s, c


def decode(cell, planes):
    line = jnp.floor(cell * (1.0 / LANES))
    gc = cell - LANES * line
    ga = floor_div(line, planes)
    gb = line - planes * ga
    freq = jnp.where(ga < 48, ga, ga - 96)
    return freq, gb, gc


def phase(freq, first):
    turn = freq * first
    turn = turn - N * jnp.floor(turn * (1.0 / N) + 0.5)
    s, c = sin_cos(turn * (math.pi / N))
    return 1.0 - 2.0 * s * s, 2.0 * s * c


def powers(freq, w_ref):
    s, c = sin_cos(freq * (2.0 * math.pi / N))
    for q in range(4):
        w_ref[4 + 2 * q] = c
        w_ref[5 + 2 * q] = s
        s, c = 2.0 * s * c, c * c - s * s


def firsts(planes):
    me = lax.axis_index("grid")
    return (me * planes).astype(F32), ((me ^ 1) * planes).astype(F32)


def pair_code(planes, steps_ref, code_ref, rows, step):
    g = steps_ref[0, step].astype(jnp.int32)
    c = jnp.minimum(step - g, rows - 1)
    wanted = jnp.where(step < rows + planes - 1, g, -1).astype(F32)
    code = jnp.where(code_ref[0, pl.ds(c, 1), :] == wanted, code_ref[1, pl.ds(c, 1), :], -1.0)
    return g, c, code


def row_of(ref, index, c):
    return jnp.broadcast_to(ref[index, pl.ds(c, 1), :], (8, CHUNK))


def rise(w_ref, c):
    k = lax.broadcasted_iota(jnp.int32, (8, CHUNK), 0)
    er = ei = None
    for bit in range(3):
        on = (k & (1 << bit)) != 0
        fr = jnp.where(on, row_of(w_ref, 4 + 2 * bit, c), 1.0)
        fi = jnp.where(on, row_of(w_ref, 5 + 2 * bit, c), 0.0)
        if er is None:
            er, ei = fr, fi
        else:
            er, ei = er * fr - ei * fi, er * fi + ei * fr
    return er, ei


def prepare(planes, cell, w_ref, code_ref, id_ref):
    freq, gb, gc = decode(cell, planes)
    code_ref[0] = gb
    code_ref[1] = gc
    id_ref[...] = ident(LANES)
    for q, first in enumerate(firsts(planes)):
        w_ref[2 * q], w_ref[2 * q + 1] = phase(freq, first)
    powers(freq, w_ref)


def spread_kernel(planes, height, unroll, slab_ref, steps_ref, own_ref, sib_ref, w_ref, code_ref, id_ref):
    rows = w_ref.shape[1]
    prepare(planes, slab_ref[0, 2 * rows : 3 * rows], w_ref, code_ref, id_ref)
    re, im = slab_ref[0, 0:rows], slab_ref[0, rows : 2 * rows]
    for q in range(2):
        sr, si = w_ref[2 * q], w_ref[2 * q + 1]
        w_ref[2 * q] = re * sr - im * si
        w_ref[2 * q + 1] = re * si + im * sr
    own_ref[...] = jnp.zeros_like(own_ref)
    sib_ref[...] = jnp.zeros_like(sib_ref)

    def visit(i, carry):
        ids = id_ref[...]
        for j in range(unroll):
            g, c, code = pair_code(planes, steps_ref, code_ref, rows, i * unroll + j)
            er, ei = rise(w_ref, c)
            jr, ji = row_of(w_ref, 10, c), row_of(w_ref, 11, c)
            lines = []
            for q in range(2):
                zr, zi = row_of(w_ref, 2 * q, c), row_of(w_ref, 2 * q + 1, c)
                zr, zi = er * zr - ei * zi, er * zi + ei * zr
                real, imag = [zr], [zi]
                for _ in range(height // 8 - 1):
                    zr, zi = zr * jr - zi * ji, zr * ji + zi * jr
                    real.append(zr)
                    imag.append(zi)
                lines += real + imag
            high, low = split(jnp.concatenate(lines, axis=0))
            got = lax.dot_general(
                jnp.concatenate([high, low], axis=0), one_hot(code, ids), NT, preferred_element_type=F32
            )
            got = got[: 4 * height] + got[4 * height :]
            where = pl.ds(pl.multiple_of(g * (2 * height), 8), 2 * height)
            own_ref[0, where, :] += got[: 2 * height]
            sib_ref[0, where, :] += got[2 * height :]
        return carry

    lax.fori_loop(0, -(-(rows + planes - 1) // unroll), visit, 0)


def collect_kernel(
    planes, height, unroll, slab_ref, steps_ref, own_ref, sib_ref, h_ref, w_ref, code_ref, id_ref, u2_ref
):
    rows = w_ref.shape[1]
    prepare(planes, slab_ref[0, 2 * rows : 3 * rows], w_ref, code_ref, id_ref)
    for g in range(planes):
        where = slice(g * 2 * height, (g + 1) * 2 * height)
        high, low = split(jnp.concatenate([own_ref[0, where, :], sib_ref[0, where, :]], axis=0))
        u2_ref[g] = jnp.concatenate([high, low], axis=0)
    h_ref[...] = jnp.zeros_like(h_ref)

    def visit(i, carry):
        ids = id_ref[...]
        for j in range(unroll):
            g, c, code = pair_code(planes, steps_ref, code_ref, rows, i * unroll + j)
            got = mm(u2_ref[g], one_hot(code, ids))
            got = got[: 4 * height] + got[4 * height :]
            jr, ji = row_of(w_ref, 10, c), row_of(w_ref, 11, c)
            hr = hi = 0.0
            for q in range(2):
                value = got[q * 2 * height : (q + 1) * 2 * height]
                ar = value[height - 8 : height]
                ai = value[2 * height - 8 : 2 * height]
                for t in range(height // 8 - 2, -1, -1):
                    ar, ai = (
                        ar * jr + ai * ji + value[8 * t : 8 * t + 8],
                        ai * jr - ar * ji + value[height + 8 * t : height + 8 * t + 8],
                    )
                zr, zi = row_of(w_ref, 2 * q, c), row_of(w_ref, 2 * q + 1, c)
                hr, hi = hr + ar * zr + ai * zi, hi + ai * zr - ar * zi
            er, ei = rise(w_ref, c)
            h_ref[0, pl.ds(c, 1), :] += jnp.sum(hr * er + hi * ei, axis=0, keepdims=True)
            h_ref[0, pl.ds(rows + c, 1), :] += jnp.sum(hi * er - hr * ei, axis=0, keepdims=True)
        return carry

    lax.fori_loop(0, -(-(rows + planes - 1) // unroll), visit, 0)


def potential_kernel(group, height, planes, calls, parts, *refs):
    own, sib = refs[:calls], refs[calls : 2 * calls]
    v_ref, *tables_hbm = refs[2 * calls : 2 * calls + 5]
    keep_ref = refs[2 * calls + 5]
    send_refs = refs[2 * calls + 6 : 2 * calls + 6 + len(parts)]
    t_ref, u_ref, bf_ref, cf_ref, ci_ref, bi_ref, in_sems, out_sems, table_sems = refs[2 * calls + 6 + len(parts) :]
    step = pl.program_id(0)
    me = lax.axis_index("grid")
    half = keep_ref.shape[0]
    per_call = half // calls
    tiles = height // 8
    shape = (N, 2, tiles, 8, LANES)
    t_tiles, u_tiles = t_ref.reshape(shape), u_ref.reshape(shape)
    last = planes // group - 1

    def place(j, q):
        return pl.ds((me ^ (2 * j + q)) * planes, planes)

    def arrivals(t):
        for q, blocks in enumerate((own, sib)):
            for j in range(half):
                yield pltpu.make_async_copy(
                    blocks[j // per_call].at[j % per_call, :, :, t], t_tiles.at[place(j, q), :, t], in_sems.at[t, q, j]
                )

    def departures(t):
        for j in range(half):
            yield pltpu.make_async_copy(
                u_tiles.at[place(j, 0), :, t], keep_ref.at[j, :, :, t], out_sems.at[t, 0, j]
            )
        for ref, part in zip(send_refs, parts):
            for i, j in enumerate(part):
                yield pltpu.make_async_copy(
                    u_tiles.at[place(j, 1), :, t], ref.at[i, :, :, t], out_sems.at[t, 1, j]
                )

    def fetches():
        for q, (source, target) in enumerate(zip(tables_hbm, (bf_ref, cf_ref, ci_ref, bi_ref))):
            yield pltpu.make_async_copy(source, target, table_sems.at[q])

    @pl.when(step == 0)
    def _():
        for copies in (arrivals(0), fetches(), *(arrivals(t) for t in range(1, tiles))):
            for copy in copies:
                copy.start()
        for copies in (arrivals(0), fetches()):
            for copy in copies:
                copy.wait()
        if height > planes:
            u_ref[...] = jnp.zeros_like(u_ref)

    for t in range(1, tiles):

        @pl.when(step == t * 8 // group)
        def _(t=t):
            for copy in arrivals(t):
                copy.wait()

    stride = 2 * height
    real, imag = [], []
    for j in range(group):
        k = step * group + j
        real.append(t_ref[pl.ds(k, N, stride=stride), :])
        imag.append(t_ref[pl.ds(k + height, N, stride=stride), :])
    x = jnp.concatenate([jnp.concatenate(real, axis=1), jnp.concatenate(imag, axis=1)], axis=0)
    high, low = split(x)
    x = mm(bf_ref[...], jnp.concatenate([high, high, low], axis=0))
    x = jnp.concatenate(
        [
            jnp.concatenate([x[:N, j * LANES : (j + 1) * LANES], x[N:, j * LANES : (j + 1) * LANES]], axis=1)
            for j in range(group)
        ],
        axis=0,
    )
    high, low = split(x)
    x = mm(jnp.concatenate([high, high, low], axis=1), cf_ref[...])
    v = []
    for j in range(group):
        line = (step * group + j) % 8
        t = [v_ref[0, pl.ds(8 * q + line, N // 2, stride=24), :] for q in range(3)]
        v.append(jnp.concatenate([t[0], t[1][:, :64]], axis=1))
        v.append(jnp.concatenate([t[1][:, 64:], t[2]], axis=1))
    v = jnp.concatenate(v, axis=0)
    x = x * jnp.concatenate([v, v], axis=1)
    high, low = split(x)
    x = mm(jnp.concatenate([high, high, low], axis=1), ci_ref[...])
    x = jnp.concatenate(
        [
            jnp.concatenate([x[j * N : (j + 1) * N, q * LANES : (q + 1) * LANES] for j in range(group)], axis=1)
            for q in range(2)
        ],
        axis=0,
    )
    high, low = split(x)
    x = mm(bi_ref[...], jnp.concatenate([high, high, low], axis=0))
    for j in range(group):
        k = step * group + j
        u_ref[pl.ds(k, N, stride=stride), :] = x[:N, j * LANES : (j + 1) * LANES]
        u_ref[pl.ds(k + height, N, stride=stride), :] = x[N:, j * LANES : (j + 1) * LANES]

    for t in range(tiles):

        @pl.when(step == min((t + 1) * 8 // group - 1, last))
        def _(t=t):
            for copy in departures(t):
                copy.start()

    @pl.when(step == last)
    def _():
        for t in range(tiles):
            for copy in departures(t):
                copy.wait()


def unsort_kernel(arrivals, bands, *refs):
    recv_refs = refs[:arrivals]
    d_ref, *coef_refs = refs[arrivals : arrivals + 1 + bands]
    h_ref, part_ref, hl_ref, wide_ref = refs[arrivals + 1 + bands :]
    rows = d_ref.shape[0]
    total = None
    for recv in recv_refs:
        for s in range(recv.shape[0]):
            total = recv[s] if total is None else total + recv[s]
    high, low = split(total)
    hl_ref[0 : 2 * rows] = high
    hl_ref[2 * rows :] = low
    hi_id = lax.broadcasted_iota(jnp.int32, (rows, CHUNK), 0).astype(F32)
    lo_id = ident(CHUNK)

    def body(i, carry):
        part = pl.ds(pl.multiple_of(i * 8, 8), 8)
        d = d_ref[part, :]
        hi = jnp.floor(d * (1.0 / CHUNK))
        lo = d - CHUNK * hi
        real, imag = [], []
        for j in range(8):
            got = mm(hl_ref[...], one_hot(lo[j : j + 1], lo_id))
            got = got[: 2 * rows] + got[2 * rows :]
            at_hi = jnp.broadcast_to(hi[j : j + 1], (rows, CHUNK)) == hi_id
            real.append(jnp.sum(jnp.where(at_hi, got[:rows], 0.0), axis=0, keepdims=True))
            imag.append(jnp.sum(jnp.where(at_hi, got[rows:], 0.0), axis=0, keepdims=True))
        wide_ref[0, part, :] = jnp.concatenate(real, axis=0)
        wide_ref[1, part, :] = jnp.concatenate(imag, axis=0)
        return carry

    lax.fori_loop(0, rows // 8, body, 0)
    hr, hi = unfold(wide_ref[0]), unfold(wide_ref[1])
    h_ref[0] = hr
    h_ref[1] = hi
    real, imag = [], []
    for coef in coef_refs:
        cr, ci = coef[0], coef[1]
        real.append(jnp.sum(cr * hr + ci * hi, axis=0, keepdims=True))
        imag.append(jnp.sum(cr * hi - ci * hr, axis=0, keepdims=True))
    sums = jnp.concatenate(real + imag, axis=0)
    for s in range(part_ref.shape[0]):
        part_ref[s] = sums


def residual_kernel(scale, bands, sum_ref, h_ref, *refs):
    coef_refs, (out_ref, sub_ref) = refs[:bands], refs[bands:]
    band = lax.axis_index("band")
    sub = sum_ref[0]
    for s in range(1, sum_ref.shape[0]):
        sub = sub + sum_ref[s]
    sub = jnp.sum(sub, axis=1, keepdims=True) * scale
    lane = lax.broadcasted_iota(jnp.int32, (1, LANES), 1)
    hr, hi = h_ref[0], h_ref[1]
    line_re = line_im = jnp.zeros((1, LANES), F32)
    for shift, coef in enumerate(coef_refs):
        sr, si = sub[shift : shift + 1], sub[bands + shift : bands + shift + 1]
        here = lane == lax.rem(band + bands - shift, bands)
        line_re = jnp.where(here, sr, line_re)
        line_im = jnp.where(here, si, line_im)
        cr, ci = coef[0], coef[1]
        hr = hr - (sr * cr - si * ci)
        hi = hi - (si * cr + sr * ci)
    out_ref[0] = hr
    out_ref[1] = hi
    sub_ref[0] = line_re[:, :bands]
    sub_ref[1] = line_im[:, :bands]


def params(mib):
    return pltpu.CompilerParams(vmem_limit_bytes=mib * 1024 * 1024)


def cost(flops):
    return pl.CostEstimate(flops=int(flops), bytes_accessed=0, transcendentals=0)


def whole(shape):
    return pl.BlockSpec(shape, lambda *_: (0,) * len(shape))


def local(coefficients, index_map, potential):
    slabs = lax.axis_size("grid")
    bands = lax.axis_size("band")
    planes = potential.shape[0]
    count = coefficients.shape[2]
    rows = count // CHUNK
    height = -(-planes // 8) * 8
    group = 8 if planes % 8 == 0 else 1
    unroll = 44
    me = lax.axis_index("grid")
    half = slabs // 2
    anywhere = pl.BlockSpec(memory_space=pl.ANY)
    coef = coefficients.reshape(2, 2 * rows, LANES)
    table_rows = 3 * rows + 8
    sorted_pts, dest = pl.pallas_call(
        functools.partial(sort_kernel, planes),
        in_specs=[pl.BlockSpec(memory_space=pltpu.HBM)] * 2,
        out_shape=(
            jax.ShapeDtypeStruct((table_rows, CHUNK), F32),
            jax.ShapeDtypeStruct((rows, CHUNK), F32),
        ),
        scratch_shapes=[
            pltpu.VMEM((7 * rows, CHUNK), F32),
            pltpu.VMEM((7, rows, CHUNK), F32),
            pltpu.VMEM((rows, CHUNK), F32),
            pltpu.VMEM((rows + 16, planes * CHUNK), F32),
            pltpu.VMEM((-(-planes // 16) * 16, CHUNK), F32),
            pltpu.VMEM((-(-planes // 16) * 16, 2 * CHUNK), F32),
            pltpu.VMEM((2 * rows, LANES), jnp.int32),
            pltpu.VMEM((2, 2 * rows, LANES), F32),
            pltpu.SemaphoreType.DMA((2,)),
        ],
        compiler_params=params(58),
        cost_estimate=cost(1e10),
        name="sort_points",
    )(index_map.reshape(2 * rows, LANES), coef)

    def swap(x, bits):
        return lax.ppermute(x, "grid", [(i, i ^ bits) for i in range(slabs)])

    if half <= 4:
        points = [sorted_pts[None]] + [swap(sorted_pts, 2 * j)[None] for j in range(1, min(half, 3))]
    else:
        everything = lax.all_gather(sorted_pts, "grid")
        points = [jnp.take(everything, me ^ (2 * jnp.arange(half)), axis=0)]
    calls = half if half <= 4 else 1
    per_call = half // calls
    lines = planes * 2 * height
    slab_spec = pl.BlockSpec((1, table_rows, CHUNK), lambda s: (s, 0, 0))
    steps_spec = pl.BlockSpec((None, 8, CHUNK), lambda s: (s, table_rows // 8 - 1, 0), memory_space=pltpu.SMEM)
    block_spec = pl.BlockSpec((1, lines, LANES), lambda s: (s, 0, 0))
    point_scratch = [pltpu.VMEM((12, rows, CHUNK), F32), pltpu.VMEM((2, rows, CHUNK), F32), pltpu.VMEM((LANES, LANES), BF)]
    spread = pl.pallas_call(
        functools.partial(spread_kernel, planes, height, unroll),
        grid=(per_call,),
        in_specs=[slab_spec, steps_spec],
        out_specs=(block_spec, block_spec),
        out_shape=(jax.ShapeDtypeStruct((per_call, lines, LANES), F32),) * 2,
        scratch_shapes=point_scratch,
        compiler_params=params(20),
        cost_estimate=cost(8e9),
        name="spread_points",
    )
    own, sib = [], []
    for call in range(calls):
        mine, theirs = spread(points[call], points[call])
        if call == 0 and half == 4:
            sorted_pts, theirs = lax.optimization_barrier((sorted_pts, theirs))
            points.append(swap(sorted_pts, 6)[None])
        own.append(mine)
        sib.append(swap(theirs, 1))
    cells = potential if height == planes else jnp.pad(potential, ((0, height - planes), (0, 0)))
    cells = cells.reshape(height // 8, 8, N * N // LANES, LANES).transpose(0, 2, 1, 3)
    cells = cells.reshape(height // 8, N * N // 16, LANES)
    *sib, mine = lax.optimization_barrier((*sib, coef))
    coefs = [coef]
    for shift in range(1, bands):
        coefs.append(lax.ppermute(mine, "band", [(i, (i + shift) % bands) for i in range(bands)]))
    constants = [jnp.asarray(t) for t in tables()]
    parts = [[1], [0, *range(2, half)]] if 2 <= half <= 4 else [list(range(half))]
    cube = (planes, 2, height // 8, 8, LANES)
    keep, *send = pl.pallas_call(
        functools.partial(potential_kernel, group, height, planes, calls, parts),
        grid=(planes // group,),
        in_specs=[anywhere] * (2 * calls)
        + [pl.BlockSpec((1, N * N // 16, LANES), lambda i: (i * group // 8, 0, 0))]
        + [anywhere] * 4,
        out_specs=[anywhere] * (1 + len(parts)),
        out_shape=[jax.ShapeDtypeStruct((count_of, *cube), F32) for count_of in (half, *map(len, parts))],
        scratch_shapes=[
            pltpu.VMEM((slabs * lines, LANES), F32),
            pltpu.VMEM((slabs * lines, LANES), F32),
            *(pltpu.VMEM(t.shape, BF) for t in constants),
            pltpu.SemaphoreType.DMA((height // 8, 2, half)),
            pltpu.SemaphoreType.DMA((height // 8, 2, half)),
            pltpu.SemaphoreType.DMA((4,)),
        ],
        compiler_params=params(40),
        cost_estimate=cost(4e10),
        name="apply_potential",
    )(*(x.reshape(per_call, *cube) for x in (*own, *sib)), cells, *constants)
    tied = lax.optimization_barrier((*send, *coefs))
    coefs = tied[len(parts) :]
    keep = keep.reshape(half, lines, LANES)
    other = []
    for x in tied[: len(parts)]:
        if other:
            other[-1], x = lax.optimization_barrier((other[-1], x))
        other.append(swap(x, 1))
    other = [x.reshape(-1, lines, LANES) for x in other]

    def block_at(first):
        return pl.BlockSpec((1, lines, LANES), lambda s: (first + s, 0, 0))

    partial = []
    for call, table in enumerate(points):
        first = call * per_call
        number, part = next((i, part) for i, part in enumerate(parts) if first in part)
        partial.append(
            pl.pallas_call(
                functools.partial(collect_kernel, planes, height, unroll),
                grid=(per_call,),
                in_specs=[slab_spec, steps_spec, block_at(first), block_at(part.index(first))],
                out_specs=pl.BlockSpec((1, 2 * rows, CHUNK), lambda s: (s, 0, 0)),
                out_shape=jax.ShapeDtypeStruct((per_call, 2 * rows, CHUNK), F32),
                scratch_shapes=point_scratch + [pltpu.VMEM((planes, 8 * height, LANES), BF)],
                compiler_params=params(24),
                cost_estimate=cost(8e9),
                name="collect_points",
            )(table, table, keep, other[number])
        )
    if half <= 4:
        arrived = [partial[0]] + [swap(partial[j], 2 * j) for j in range(1, half)]
    else:
        ids = jnp.arange(slabs)
        blocks = jnp.take(partial[0], (ids ^ me) // 2, axis=0)
        blocks = jnp.where(((ids ^ me) % 2 == 0)[:, None, None], blocks, 0.0)
        arrived = [lax.all_to_all(blocks, "grid", split_axis=0, concat_axis=0, tiled=True)]
    applied, part = pl.pallas_call(
        functools.partial(unsort_kernel, len(arrived), bands),
        out_shape=(
            jax.ShapeDtypeStruct((2, 2 * rows, LANES), F32),
            jax.ShapeDtypeStruct((slabs, 2 * bands, LANES), F32),
        ),
        scratch_shapes=[pltpu.VMEM((4 * rows, CHUNK), BF), pltpu.VMEM((2, rows, CHUNK), F32)],
        compiler_params=params(12),
        cost_estimate=cost(6e9),
        name="unsort_points",
    )(*arrived, dest, *coefs)
    sums = lax.all_to_all(part, "grid", split_axis=0, concat_axis=0, tiled=True)
    resid, sub = pl.pallas_call(
        functools.partial(residual_kernel, 1.0 / (count * slabs), bands),
        out_shape=(
            jax.ShapeDtypeStruct((2, 2 * rows, LANES), F32),
            jax.ShapeDtypeStruct((2, 1, bands), F32),
        ),
        compiler_params=params(8),
        cost_estimate=cost(2e9),
        name="residual",
    )(sums, applied, *coefs)
    return sub.transpose(0, 2, 1), resid.reshape(2, 1, count)


def solution(mesh):
    return jax.shard_map(
        local,
        mesh=mesh,
        in_specs=(P(None, "band", "grid"), P("grid"), P("grid", None)),
        out_specs=(P(None, None, "band"), P(None, "band", "grid")),
        check_vma=False,
    )
```

```python
import functools
import math

import jax
import jax.numpy as jnp
import numpy as np
from jax import lax
from jax.experimental import pallas as pl
from jax.experimental.pallas import tpu as pltpu
from jax.sharding import PartitionSpec as P

N = 192
CHUNK = 256
LANES = 128
BF = jnp.bfloat16
F32 = jnp.float32
NT = (((1,), (1,)), ((), ()))


def split(x):
    high = x.astype(BF)
    low = (x - high.astype(F32)).astype(BF)
    return high, low


def mm(a, b):
    return jnp.dot(a, b, preferred_element_type=F32)


def split_table(table):
    table = table.astype(np.float32)
    high = table.astype(BF)
    low = (table - high.astype(np.float32)).astype(BF)
    return high, low


@functools.cache
def tables():
    pos = np.arange(N)
    angle = 2.0 * math.pi * ((pos[:, None] * pos[None, :]) % N) / N
    cb, sb = np.cos(angle), np.sin(angle)
    order = np.concatenate([pos[0::2], pos[1::2]])
    co, so = cb[order], sb[order]
    b_fwd = np.block([[co, -so], [so, co]])
    b_inv = np.block([[co.T, so.T], [-so.T, co.T]])
    freq = np.arange(LANES)
    freq = np.where(freq < 64, freq, freq - LANES)
    keep = (np.abs(freq) < 48)[:, None]
    angle = 2.0 * math.pi * ((freq[:, None] * pos[None, :]) % N) / N
    cc, sc = np.cos(angle) * keep, np.sin(angle) * keep
    c_fwd = np.block([[cc, sc], [-sc, cc]])
    c_inv = np.block([[cc.T, -sc.T], [sc.T, cc.T]]) / float(N) ** 3
    bf_h, bf_l = split_table(b_fwd)
    bi_h, bi_l = split_table(b_inv)
    cf_h, cf_l = split_table(c_fwd)
    ci_h, ci_l = split_table(c_inv)
    return (
        np.concatenate([bf_h, bf_l, bf_h], axis=1),
        np.concatenate([cf_h, cf_l, cf_h], axis=0),
        np.concatenate([ci_h, ci_l, ci_h], axis=0),
        np.concatenate([bi_h, bi_l, bi_h], axis=1),
    )


def fold(x):
    half = x.shape[0] // 2
    return jnp.concatenate([x[:half], x[half:]], axis=1)


def unfold(x):
    return jnp.concatenate([x[:, :LANES], x[:, LANES:]], axis=0)


def wide(row, count):
    tile = jnp.broadcast_to(row, (16, row.shape[1])).astype(BF)
    return jnp.concatenate([tile] * (count // 16), axis=0)


def ident(count):
    return lax.broadcasted_iota(jnp.int32, (count, LANES), 0).astype(F32).astype(BF)


def equal(row, ids):
    code = wide(row, ids.shape[0])
    return code == jnp.concatenate([ids, ids], axis=1)


def one_hot(row, ids):
    one = jnp.ones((ids.shape[0], CHUNK), BF)
    return jnp.where(equal(row, ids), one, jnp.zeros_like(one))


def floor_div(x, divisor):
    return jnp.floor((x + 0.5) * (1.0 / divisor))


def sort_kernel(
    planes, m_hbm, c_hbm, out_ref, d_ref, acc_ref, val_ref, gb_ref, cum_ref, tot_ref, lane_ref, m_ref, c_ref, sems
):
    rows = gb_ref.shape[0]
    fetch_m = pltpu.make_async_copy(m_hbm, m_ref, sems.at[0])
    fetch_c = pltpu.make_async_copy(c_hbm, c_ref, sems.at[1])
    fetch_m.start()
    fetch_c.start()
    fetch_m.wait()
    m = fold(m_ref[...]).astype(F32)
    line = floor_div(m, N)
    gc = m - N * line
    ga = floor_div(line, planes)
    gb = line - planes * ga
    ga = jnp.where(ga < 96, ga, ga - 96)
    gc = jnp.where(gc < 96, gc, gc - 64)
    gb_ref[...] = gb
    lane_r = lax.broadcasted_iota(jnp.int32, (CHUNK, 2 * CHUNK), 0)
    lane_c = lax.broadcasted_iota(jnp.int32, (CHUNK, 2 * CHUNK), 1)
    tri = jnp.where((lane_r < lane_c) | (lane_c >= CHUNK), 1.0, 0.0).astype(BF)
    row_r = lax.broadcasted_iota(jnp.int32, (rows + 16, rows), 0)
    row_c = lax.broadcasted_iota(jnp.int32, (rows + 16, rows), 1)
    below = jnp.where(row_c < row_r, 1.0, 0.0).astype(BF)
    masks = [jnp.where(gb == float(g), 1.0, 0.0).astype(BF) for g in range(planes)]
    cum_ref[...] = mm(below, jnp.concatenate(masks, axis=1))
    tot_ref[...] = jnp.zeros_like(tot_ref)
    step = 3 if planes % 3 == 0 and planes > 3 else 1

    def at(g):
        return pl.ds(pl.multiple_of(g * CHUNK, CHUNK), CHUNK)

    def gather(i, carry):
        for j in range(step):
            g = i * step + j
            tot_ref[pl.ds(g, 1), :] = cum_ref[rows : rows + 8, at(g)][0:1]
        return carry

    lax.fori_loop(0, planes // step, gather, 0)
    lane_ref[...] = mm(tot_ref[...].astype(BF), tri)
    step_id = lax.broadcasted_iota(jnp.int32, (8, CHUNK), 1).astype(F32)

    def rank(i, carry):
        base, place, plane_of = carry
        for j in range(step):
            g = i * step + j
            gf = g.astype(F32)
            lanes = lane_ref[pl.ds(g, 1), :]
            here = cum_ref[0:rows, at(g)] + (lanes[:, :CHUNK] + base)
            place = jnp.where(gb_ref[...] == gf, here, place)
            base = base + lanes[:, CHUNK:]
            end = gf + jnp.floor((jnp.maximum(base, 1.0) - 1.0) * (1.0 / CHUNK))
            end = jnp.where(gf < planes - 1.0, end, 1e6)
            plane_of = plane_of + jnp.where(end < step_id, 1.0, 0.0)
        return base, place, plane_of

    _, place, plane_of = lax.fori_loop(
        0,
        planes // step,
        rank,
        (jnp.zeros((1, CHUNK), F32), jnp.zeros((rows, CHUNK), F32), jnp.zeros((8, CHUNK), F32)),
    )
    d_ref[...] = place
    fetch_c.wait()
    re_h, re_l = split(fold(c_ref[0]))
    im_h, im_l = split(fold(c_ref[1]))
    for q, value in enumerate((re_h, re_l, im_h, im_l, ga, gb, gc)):
        val_ref[q] = value.astype(F32)
    acc_ref[...] = jnp.zeros_like(acc_ref)
    hi_id, lo_id = ident(rows), ident(CHUNK)
    zero = jnp.zeros((rows, CHUNK), BF)

    def body(i, carry):
        part = pl.ds(pl.multiple_of(i * 8, 8), 8)
        d = d_ref[part, :]
        hi = jnp.floor(d * (1.0 / CHUNK))
        lo = d - CHUNK * hi
        values = [val_ref[q, part, :] for q in range(7)]
        left, right = [], []
        for j in range(8):
            at_hi = equal(hi[j : j + 1], hi_id)
            left.append(
                jnp.concatenate([jnp.where(at_hi, wide(v[j : j + 1], rows), zero) for v in values], axis=0)
            )
            right.append(one_hot(lo[j : j + 1], lo_id))
        acc_ref[...] += lax.dot_general(
            jnp.concatenate(left, axis=1), jnp.concatenate(right, axis=1), NT, preferred_element_type=F32
        )
        return carry

    lax.fori_loop(0, rows // 8, body, 0)
    got = [acc_ref[q * rows : (q + 1) * rows] for q in range(7)]
    out_ref[0:rows] = got[0] + got[1]
    out_ref[rows : 2 * rows] = got[2] + got[3]
    out_ref[2 * rows : 3 * rows] = (got[4] * planes + got[5]) * LANES + got[6]
    out_ref[3 * rows : 3 * rows + 8] = plane_of


def sin_cos(x):
    y = x * x
    s = -1.0 / 39916800.0 + y * (1.0 / 6227020800.0)
    s = 1.0 / 362880.0 + y * s
    s = -1.0 / 5040.0 + y * s
    s = 1.0 / 120.0 + y * s
    s = -1.0 / 6.0 + y * s
    s = x + x * y * s
    c = 1.0 / 479001600.0 - y * (1.0 / 87178291200.0)
    c = -1.0 / 3628800.0 + y * c
    c = 1.0 / 40320.0 + y * c
    c = -1.0 / 720.0 + y * c
    c = 1.0 / 24.0 + y * c
    c = -0.5 + y * c
    c = 1.0 + y * c
    return s, c


def decode(cell, planes):
    line = jnp.floor(cell * (1.0 / LANES))
    gc = cell - LANES * line
    ga = floor_div(line, planes)
    gb = line - planes * ga
    freq = jnp.where(ga < 48, ga, ga - 96)
    return freq, gb, gc


def phase(freq, first):
    turn = freq * first
    turn = turn - N * jnp.floor(turn * (1.0 / N) + 0.5)
    s, c = sin_cos(turn * (math.pi / N))
    return 1.0 - 2.0 * s * s, 2.0 * s * c


def powers(freq, w_ref):
    s, c = sin_cos(freq * (2.0 * math.pi / N))
    for q in range(4):
        w_ref[4 + 2 * q] = c
        w_ref[5 + 2 * q] = s
        s, c = 2.0 * s * c, c * c - s * s


def firsts(planes):
    me = lax.axis_index("grid")
    return (me * planes).astype(F32), ((me ^ 1) * planes).astype(F32)


def pair_code(planes, steps_ref, code_ref, rows, step):
    g = steps_ref[0, step].astype(jnp.int32)
    c = jnp.minimum(step - g, rows - 1)
    wanted = jnp.where(step < rows + planes - 1, g, -1).astype(F32)
    code = jnp.where(code_ref[0, pl.ds(c, 1), :] == wanted, code_ref[1, pl.ds(c, 1), :], -1.0)
    return g, c, code


def row_of(ref, index, c):
    return jnp.broadcast_to(ref[index, pl.ds(c, 1), :], (8, CHUNK))


def rise(w_ref, c):
    k = lax.broadcasted_iota(jnp.int32, (8, CHUNK), 0)
    er = ei = None
    for bit in range(3):
        on = (k & (1 << bit)) != 0
        fr = jnp.where(on, row_of(w_ref, 4 + 2 * bit, c), 1.0)
        fi = jnp.where(on, row_of(w_ref, 5 + 2 * bit, c), 0.0)
        if er is None:
            er, ei = fr, fi
        else:
            er, ei = er * fr - ei * fi, er * fi + ei * fr
    return er, ei


def prepare(planes, cell, w_ref, code_ref, id_ref):
    freq, gb, gc = decode(cell, planes)
    code_ref[0] = gb
    code_ref[1] = gc
    id_ref[...] = ident(LANES)
    for q, first in enumerate(firsts(planes)):
        w_ref[2 * q], w_ref[2 * q + 1] = phase(freq, first)
    powers(freq, w_ref)


def spread_kernel(planes, height, unroll, slab_ref, steps_ref, own_ref, sib_ref, w_ref, code_ref, id_ref):
    rows = w_ref.shape[1]
    prepare(planes, slab_ref[0, 2 * rows : 3 * rows], w_ref, code_ref, id_ref)
    re, im = slab_ref[0, 0:rows], slab_ref[0, rows : 2 * rows]
    for q in range(2):
        sr, si = w_ref[2 * q], w_ref[2 * q + 1]
        w_ref[2 * q] = re * sr - im * si
        w_ref[2 * q + 1] = re * si + im * sr
    own_ref[...] = jnp.zeros_like(own_ref)
    sib_ref[...] = jnp.zeros_like(sib_ref)

    def visit(i, carry):
        ids = id_ref[...]
        for j in range(unroll):
            g, c, code = pair_code(planes, steps_ref, code_ref, rows, i * unroll + j)
            er, ei = rise(w_ref, c)
            jr, ji = row_of(w_ref, 10, c), row_of(w_ref, 11, c)
            lines = []
            for q in range(2):
                zr, zi = row_of(w_ref, 2 * q, c), row_of(w_ref, 2 * q + 1, c)
                zr, zi = er * zr - ei * zi, er * zi + ei * zr
                real, imag = [zr], [zi]
                for _ in range(height // 8 - 1):
                    zr, zi = zr * jr - zi * ji, zr * ji + zi * jr
                    real.append(zr)
                    imag.append(zi)
                lines += real + imag
            high, low = split(jnp.concatenate(lines, axis=0))
            got = lax.dot_general(
                jnp.concatenate([high, low], axis=0), one_hot(code, ids), NT, preferred_element_type=F32
            )
            got = got[: 4 * height] + got[4 * height :]
            where = pl.ds(pl.multiple_of(g * (2 * height), 8), 2 * height)
            own_ref[0, where, :] += got[: 2 * height]
            sib_ref[0, where, :] += got[2 * height :]
        return carry

    lax.fori_loop(0, -(-(rows + planes - 1) // unroll), visit, 0)


def collect_kernel(
    planes, height, unroll, slab_ref, steps_ref, own_ref, sib_ref, h_ref, w_ref, code_ref, id_ref, u2_ref
):
    rows = w_ref.shape[1]
    prepare(planes, slab_ref[0, 2 * rows : 3 * rows], w_ref, code_ref, id_ref)
    for g in range(planes):
        where = slice(g * 2 * height, (g + 1) * 2 * height)
        high, low = split(jnp.concatenate([own_ref[0, where, :], sib_ref[0, where, :]], axis=0))
        u2_ref[g] = jnp.concatenate([high, low], axis=0)
    h_ref[...] = jnp.zeros_like(h_ref)

    def visit(i, carry):
        ids = id_ref[...]
        for j in range(unroll):
            g, c, code = pair_code(planes, steps_ref, code_ref, rows, i * unroll + j)
            got = mm(u2_ref[g], one_hot(code, ids))
            got = got[: 4 * height] + got[4 * height :]
            jr, ji = row_of(w_ref, 10, c), row_of(w_ref, 11, c)
            hr = hi = 0.0
            for q in range(2):
                value = got[q * 2 * height : (q + 1) * 2 * height]
                ar = value[height - 8 : height]
                ai = value[2 * height - 8 : 2 * height]
                for t in range(height // 8 - 2, -1, -1):
                    ar, ai = (
                        ar * jr + ai * ji + value[8 * t : 8 * t + 8],
                        ai * jr - ar * ji + value[height + 8 * t : height + 8 * t + 8],
                    )
                zr, zi = row_of(w_ref, 2 * q, c), row_of(w_ref, 2 * q + 1, c)
                hr, hi = hr + ar * zr + ai * zi, hi + ai * zr - ar * zi
            er, ei = rise(w_ref, c)
            h_ref[0, pl.ds(c, 1), :] += jnp.sum(hr * er + hi * ei, axis=0, keepdims=True)
            h_ref[0, pl.ds(rows + c, 1), :] += jnp.sum(hi * er - hr * ei, axis=0, keepdims=True)
        return carry

    lax.fori_loop(0, -(-(rows + planes - 1) // unroll), visit, 0)


def potential_kernel(planes, calls, parts, *refs):
    own, sib = refs[:calls], refs[calls : 2 * calls]
    v_ref, *tables_hbm = refs[2 * calls : 2 * calls + 5]
    keep_ref = refs[2 * calls + 5]
    send_refs = refs[2 * calls + 6 : 2 * calls + 6 + len(parts)]
    t_ref, u_ref, bf_ref, cf_ref, ci_ref, bi_ref, in_sems, out_sems, table_sems = refs[2 * calls + 6 + len(parts) :]
    step = pl.program_id(0)
    me = lax.axis_index("grid")
    half = keep_ref.shape[0]
    per_call = half // calls
    tiles = t_ref.shape[2]
    last = tiles - 1

    def place(j, q):
        return pl.ds((me ^ (2 * j + q)) * planes, planes)

    def arrivals(t):
        for q, blocks in enumerate((own, sib)):
            for j in range(half):
                yield pltpu.make_async_copy(
                    blocks[j // per_call].at[j % per_call, :, :, t], t_ref.at[place(j, q), :, t], in_sems.at[t, q, j]
                )

    def departures(t):
        for j in range(half):
            yield pltpu.make_async_copy(
                u_ref.at[place(j, 0), :, t], keep_ref.at[j, :, :, t], out_sems.at[t, 0, j]
            )
        for ref, part in zip(send_refs, parts):
            for i, j in enumerate(part):
                yield pltpu.make_async_copy(
                    u_ref.at[place(j, 1), :, t], ref.at[i, :, :, t], out_sems.at[t, 1, j]
                )

    def fetches():
        for q, (source, target) in enumerate(zip(tables_hbm, (bf_ref, cf_ref, ci_ref, bi_ref))):
            yield pltpu.make_async_copy(source, target, table_sems.at[q])

    @pl.when(step == 0)
    def _():
        for copies in (arrivals(0), fetches(), *(arrivals(t) for t in range(1, tiles))):
            for copy in copies:
                copy.start()
        for copies in (arrivals(0), fetches()):
            for copy in copies:
                copy.wait()

    for t in range(1, tiles):

        @pl.when(step == t)
        def _(t=t):
            for copy in arrivals(t):
                copy.wait()

    group = 8

    def turn(x):
        return jnp.transpose(x, (1, 0, 2))

    def abreast(x):
        return jnp.concatenate([x[j] for j in range(group)], axis=1)

    x = jnp.concatenate([abreast(turn(t_ref[:, q, step])) for q in range(2)], axis=0)
    high, low = split(x)
    x = mm(bf_ref[...], jnp.concatenate([high, high, low], axis=0))
    x = jnp.concatenate(
        [
            jnp.concatenate([x[:N, j * LANES : (j + 1) * LANES], x[N:, j * LANES : (j + 1) * LANES]], axis=1)
            for j in range(group)
        ],
        axis=0,
    )
    high, low = split(x)
    x = mm(jnp.concatenate([high, high, low], axis=1), cf_ref[...])
    cells = [turn(v_ref[0, :, q]) for q in range(3)]
    v = []
    for j in range(group):
        t = [cell[j] for cell in cells]
        v.append(jnp.concatenate([t[0], t[1][:, :64]], axis=1))
        v.append(jnp.concatenate([t[1][:, 64:], t[2]], axis=1))
    v = jnp.concatenate(v, axis=0)
    x = x * jnp.concatenate([v, v], axis=1)
    high, low = split(x)
    x = mm(jnp.concatenate([high, high, low], axis=1), ci_ref[...])
    x = jnp.concatenate(
        [
            jnp.concatenate([x[j * N : (j + 1) * N, q * LANES : (q + 1) * LANES] for j in range(group)], axis=1)
            for q in range(2)
        ],
        axis=0,
    )
    high, low = split(x)
    x = mm(bi_ref[...], jnp.concatenate([high, high, low], axis=0))
    for q in range(2):
        part = x[q * N : (q + 1) * N]
        u_ref[:, q, step] = turn(jnp.stack([part[:, j * LANES : (j + 1) * LANES] for j in range(group)]))

    for t in range(tiles):

        @pl.when(step == t)
        def _(t=t):
            for copy in departures(t):
                copy.start()

    @pl.when(step == last)
    def _():
        for t in range(tiles):
            for copy in departures(t):
                copy.wait()


def unsort_kernel(arrivals, bands, *refs):
    recv_refs = refs[:arrivals]
    d_ref, *coef_refs = refs[arrivals : arrivals + 1 + bands]
    h_ref, part_ref, hl_ref, wide_ref = refs[arrivals + 1 + bands :]
    rows = d_ref.shape[0]
    total = None
    for recv in recv_refs:
        for s in range(recv.shape[0]):
            total = recv[s] if total is None else total + recv[s]
    high, low = split(total)
    hl_ref[0 : 2 * rows] = high
    hl_ref[2 * rows :] = low
    hi_id = lax.broadcasted_iota(jnp.int32, (rows, CHUNK), 0).astype(F32)
    lo_id = ident(CHUNK)

    def body(i, carry):
        part = pl.ds(pl.multiple_of(i * 8, 8), 8)
        d = d_ref[part, :]
        hi = jnp.floor(d * (1.0 / CHUNK))
        lo = d - CHUNK * hi
        real, imag = [], []
        for j in range(8):
            got = mm(hl_ref[...], one_hot(lo[j : j + 1], lo_id))
            got = got[: 2 * rows] + got[2 * rows :]
            at_hi = jnp.broadcast_to(hi[j : j + 1], (rows, CHUNK)) == hi_id
            real.append(jnp.sum(jnp.where(at_hi, got[:rows], 0.0), axis=0, keepdims=True))
            imag.append(jnp.sum(jnp.where(at_hi, got[rows:], 0.0), axis=0, keepdims=True))
        wide_ref[0, part, :] = jnp.concatenate(real, axis=0)
        wide_ref[1, part, :] = jnp.concatenate(imag, axis=0)
        return carry

    lax.fori_loop(0, rows // 8, body, 0)
    hr, hi = unfold(wide_ref[0]), unfold(wide_ref[1])
    h_ref[0] = hr
    h_ref[1] = hi
    real, imag = [], []
    for coef in coef_refs:
        cr, ci = coef[0], coef[1]
        real.append(jnp.sum(cr * hr + ci * hi, axis=0, keepdims=True))
        imag.append(jnp.sum(cr * hi - ci * hr, axis=0, keepdims=True))
    sums = jnp.concatenate(real + imag, axis=0)
    for s in range(part_ref.shape[0]):
        part_ref[s] = sums


def residual_kernel(scale, bands, sum_ref, h_ref, *refs):
    coef_refs, (out_ref, sub_ref) = refs[:bands], refs[bands:]
    band = lax.axis_index("band")
    sub = sum_ref[0]
    for s in range(1, sum_ref.shape[0]):
        sub = sub + sum_ref[s]
    sub = jnp.sum(sub, axis=1, keepdims=True) * scale
    lane = lax.broadcasted_iota(jnp.int32, (1, LANES), 1)
    hr, hi = h_ref[0], h_ref[1]
    line_re = line_im = jnp.zeros((1, LANES), F32)
    for shift, coef in enumerate(coef_refs):
        sr, si = sub[shift : shift + 1], sub[bands + shift : bands + shift + 1]
        here = lane == lax.rem(band + bands - shift, bands)
        line_re = jnp.where(here, sr, line_re)
        line_im = jnp.where(here, si, line_im)
        cr, ci = coef[0], coef[1]
        hr = hr - (sr * cr - si * ci)
        hi = hi - (si * cr + sr * ci)
    out_ref[0] = hr
    out_ref[1] = hi
    sub_ref[0] = line_re[:, :bands]
    sub_ref[1] = line_im[:, :bands]


def params(mib):
    return pltpu.CompilerParams(vmem_limit_bytes=mib * 1024 * 1024)


def cost(flops):
    return pl.CostEstimate(flops=int(flops), bytes_accessed=0, transcendentals=0)


def whole(shape):
    return pl.BlockSpec(shape, lambda *_: (0,) * len(shape))


def local(coefficients, index_map, potential):
    slabs = lax.axis_size("grid")
    bands = lax.axis_size("band")
    planes = potential.shape[0]
    count = coefficients.shape[2]
    rows = count // CHUNK
    height = -(-planes // 8) * 8
    unroll = 44
    me = lax.axis_index("grid")
    half = slabs // 2
    anywhere = pl.BlockSpec(memory_space=pl.ANY)
    coef = coefficients.reshape(2, 2 * rows, LANES)
    table_rows = 3 * rows + 8
    sorted_pts, dest = pl.pallas_call(
        functools.partial(sort_kernel, planes),
        in_specs=[pl.BlockSpec(memory_space=pltpu.HBM)] * 2,
        out_shape=(
            jax.ShapeDtypeStruct((table_rows, CHUNK), F32),
            jax.ShapeDtypeStruct((rows, CHUNK), F32),
        ),
        scratch_shapes=[
            pltpu.VMEM((7 * rows, CHUNK), F32),
            pltpu.VMEM((7, rows, CHUNK), F32),
            pltpu.VMEM((rows, CHUNK), F32),
            pltpu.VMEM((rows + 16, planes * CHUNK), F32),
            pltpu.VMEM((-(-planes // 16) * 16, CHUNK), F32),
            pltpu.VMEM((-(-planes // 16) * 16, 2 * CHUNK), F32),
            pltpu.VMEM((2 * rows, LANES), jnp.int32),
            pltpu.VMEM((2, 2 * rows, LANES), F32),
            pltpu.SemaphoreType.DMA((2,)),
        ],
        compiler_params=params(58),
        cost_estimate=cost(1e10),
        name="sort_points",
    )(index_map.reshape(2 * rows, LANES), coef)

    def swap(x, bits):
        return lax.ppermute(x, "grid", [(i, i ^ bits) for i in range(slabs)])

    if half <= 4:
        points = [sorted_pts[None]] + [swap(sorted_pts, 2 * j)[None] for j in range(1, min(half, 3))]
    else:
        everything = lax.all_gather(sorted_pts, "grid")
        points = [jnp.take(everything, me ^ (2 * jnp.arange(half)), axis=0)]
    calls = half if half <= 4 else 1
    per_call = half // calls
    lines = planes * 2 * height
    slab_spec = pl.BlockSpec((1, table_rows, CHUNK), lambda s: (s, 0, 0))
    steps_spec = pl.BlockSpec((None, 8, CHUNK), lambda s: (s, table_rows // 8 - 1, 0), memory_space=pltpu.SMEM)
    block_spec = pl.BlockSpec((1, lines, LANES), lambda s: (s, 0, 0))
    point_scratch = [pltpu.VMEM((12, rows, CHUNK), F32), pltpu.VMEM((2, rows, CHUNK), F32), pltpu.VMEM((LANES, LANES), BF)]
    spread = pl.pallas_call(
        functools.partial(spread_kernel, planes, height, unroll),
        grid=(per_call,),
        in_specs=[slab_spec, steps_spec],
        out_specs=(block_spec, block_spec),
        out_shape=(jax.ShapeDtypeStruct((per_call, lines, LANES), F32),) * 2,
        scratch_shapes=point_scratch,
        compiler_params=params(20),
        cost_estimate=cost(8e9),
        name="spread_points",
    )
    own, sib = [], []
    for call in range(calls):
        mine, theirs = spread(points[call], points[call])
        if call == 0 and half == 4:
            sorted_pts, theirs = lax.optimization_barrier((sorted_pts, theirs))
            points.append(swap(sorted_pts, 6)[None])
        own.append(mine)
        sib.append(swap(theirs, 1))
    cells = potential if height == planes else jnp.pad(potential, ((0, height - planes), (0, 0)))
    cells = cells.reshape(height // 8, 8, N * N // LANES, LANES).transpose(0, 2, 1, 3)
    cells = cells.reshape(height // 8, N // 2, 3, 8, LANES)
    *sib, mine = lax.optimization_barrier((*sib, coef))
    coefs = [coef]
    for shift in range(1, bands):
        coefs.append(lax.ppermute(mine, "band", [(i, (i + shift) % bands) for i in range(bands)]))
    constants = [jnp.asarray(t) for t in tables()]
    parts = [[1], [0, *range(2, half)]] if 2 <= half <= 4 else [list(range(half))]
    cube = (planes, 2, height // 8, 8, LANES)
    keep, *send = pl.pallas_call(
        functools.partial(potential_kernel, planes, calls, parts),
        grid=(height // 8,),
        in_specs=[anywhere] * (2 * calls)
        + [pl.BlockSpec((1, N // 2, 3, 8, LANES), lambda i: (i, 0, 0, 0, 0))]
        + [anywhere] * 4,
        out_specs=[anywhere] * (1 + len(parts)),
        out_shape=[jax.ShapeDtypeStruct((count_of, *cube), F32) for count_of in (half, *map(len, parts))],
        scratch_shapes=[
            pltpu.VMEM((N, *cube[1:]), F32),
            pltpu.VMEM((N, *cube[1:]), F32),
            *(pltpu.VMEM(t.shape, BF) for t in constants),
            pltpu.SemaphoreType.DMA((height // 8, 2, half)),
            pltpu.SemaphoreType.DMA((height // 8, 2, half)),
            pltpu.SemaphoreType.DMA((4,)),
        ],
        compiler_params=params(40),
        cost_estimate=cost(4e10),
        name="apply_potential",
    )(*(x.reshape(per_call, *cube) for x in (*own, *sib)), cells, *constants)
    tied = lax.optimization_barrier((*send, *coefs))
    coefs = tied[len(parts) :]
    keep = keep.reshape(half, lines, LANES)
    other = []
    for x in tied[: len(parts)]:
        if other:
            other[-1], x = lax.optimization_barrier((other[-1], x))
        other.append(swap(x, 1))
    other = [x.reshape(-1, lines, LANES) for x in other]

    def block_at(first):
        return pl.BlockSpec((1, lines, LANES), lambda s: (first + s, 0, 0))

    partial = []
    for call, table in enumerate(points):
        first = call * per_call
        number, part = next((i, part) for i, part in enumerate(parts) if first in part)
        partial.append(
            pl.pallas_call(
                functools.partial(collect_kernel, planes, height, unroll),
                grid=(per_call,),
                in_specs=[slab_spec, steps_spec, block_at(first), block_at(part.index(first))],
                out_specs=pl.BlockSpec((1, 2 * rows, CHUNK), lambda s: (s, 0, 0)),
                out_shape=jax.ShapeDtypeStruct((per_call, 2 * rows, CHUNK), F32),
                scratch_shapes=point_scratch + [pltpu.VMEM((planes, 8 * height, LANES), BF)],
                compiler_params=params(24),
                cost_estimate=cost(8e9),
                name="collect_points",
            )(table, table, keep, other[number])
        )
    if half <= 4:
        arrived = [partial[0]] + [swap(partial[j], 2 * j) for j in range(1, half)]
    else:
        ids = jnp.arange(slabs)
        blocks = jnp.take(partial[0], (ids ^ me) // 2, axis=0)
        blocks = jnp.where(((ids ^ me) % 2 == 0)[:, None, None], blocks, 0.0)
        arrived = [lax.all_to_all(blocks, "grid", split_axis=0, concat_axis=0, tiled=True)]
    applied, part = pl.pallas_call(
        functools.partial(unsort_kernel, len(arrived), bands),
        out_shape=(
            jax.ShapeDtypeStruct((2, 2 * rows, LANES), F32),
            jax.ShapeDtypeStruct((slabs, 2 * bands, LANES), F32),
        ),
        scratch_shapes=[pltpu.VMEM((4 * rows, CHUNK), BF), pltpu.VMEM((2, rows, CHUNK), F32)],
        compiler_params=params(12),
        cost_estimate=cost(6e9),
        name="unsort_points",
    )(*arrived, dest, *coefs)
    sums = lax.all_to_all(part, "grid", split_axis=0, concat_axis=0, tiled=True)
    resid, sub = pl.pallas_call(
        functools.partial(residual_kernel, 1.0 / (count * slabs), bands),
        out_shape=(
            jax.ShapeDtypeStruct((2, 2 * rows, LANES), F32),
            jax.ShapeDtypeStruct((2, 1, bands), F32),
        ),
        compiler_params=params(8),
        cost_estimate=cost(2e9),
        name="residual",
    )(sums, applied, *coefs)
    return sub.transpose(0, 2, 1), resid.reshape(2, 1, count)


def solution(mesh):
    return jax.shard_map(
        local,
        mesh=mesh,
        in_specs=(P(None, "band", "grid"), P("grid"), P("grid", None)),
        out_specs=(P(None, None, "band"), P(None, "band", "grid")),
        check_vma=False,
    )
```

```python
import functools
import math

import jax
import jax.numpy as jnp
import numpy as np
from jax import lax
from jax.experimental import pallas as pl
from jax.experimental.pallas import tpu as pltpu
from jax.sharding import PartitionSpec as P

N = 192
CHUNK = 256
LANES = 128
BF = jnp.bfloat16
F32 = jnp.float32
NT = (((1,), (1,)), ((), ()))


def split(x):
    high = x.astype(BF)
    low = (x - high.astype(F32)).astype(BF)
    return high, low


def mm(a, b):
    return jnp.dot(a, b, preferred_element_type=F32)


def split_table(table):
    table = table.astype(np.float32)
    high = table.astype(BF)
    low = (table - high.astype(np.float32)).astype(BF)
    return high, low


@functools.cache
def tables():
    pos = np.arange(N)
    angle = 2.0 * math.pi * ((pos[:, None] * pos[None, :]) % N) / N
    cb, sb = np.cos(angle), np.sin(angle)
    order = np.concatenate([pos[0::2], pos[1::2]])
    co, so = cb[order], sb[order]
    b_fwd = np.block([[co, -so], [so, co]])
    b_inv = np.block([[co.T, so.T], [-so.T, co.T]])
    freq = np.arange(LANES)
    freq = np.where(freq < 64, freq, freq - LANES)
    keep = (np.abs(freq) < 48)[:, None]
    angle = 2.0 * math.pi * ((freq[:, None] * pos[None, :]) % N) / N
    cc, sc = np.cos(angle) * keep, np.sin(angle) * keep
    c_fwd = np.block([[cc, sc], [-sc, cc]])
    c_inv = np.block([[cc.T, -sc.T], [sc.T, cc.T]]) / float(N) ** 3
    bf_h, bf_l = split_table(b_fwd)
    bi_h, bi_l = split_table(b_inv)
    cf_h, cf_l = split_table(c_fwd)
    ci_h, ci_l = split_table(c_inv)
    return (
        np.concatenate([bf_h, bf_l, bf_h], axis=1),
        np.concatenate([cf_h, cf_l, cf_h], axis=0),
        np.concatenate([ci_h, ci_l, ci_h], axis=0),
        np.concatenate([bi_h, bi_l, bi_h], axis=1),
    )


def fold(x):
    half = x.shape[0] // 2
    return jnp.concatenate([x[:half], x[half:]], axis=1)


def unfold(x):
    return jnp.concatenate([x[:, :LANES], x[:, LANES:]], axis=0)


def wide(row, count):
    tile = jnp.broadcast_to(row, (16, row.shape[1])).astype(BF)
    return jnp.concatenate([tile] * (count // 16), axis=0)


def ident(count):
    return lax.broadcasted_iota(jnp.int32, (count, LANES), 0).astype(F32).astype(BF)


def equal(row, ids):
    code = wide(row, ids.shape[0])
    return code == jnp.concatenate([ids, ids], axis=1)


def one_hot(row, ids):
    one = jnp.ones((ids.shape[0], CHUNK), BF)
    return jnp.where(equal(row, ids), one, jnp.zeros_like(one))


def floor_div(x, divisor):
    return jnp.floor((x + 0.5) * (1.0 / divisor))


def sort_kernel(
    planes, m_hbm, c_hbm, out_ref, d_ref, both_ref, acc_ref, val_ref, gb_ref, cum_ref, tot_ref, lane_ref, m_ref, c_ref, sems
):
    rows = gb_ref.shape[0]
    fetch_m = pltpu.make_async_copy(m_hbm, m_ref, sems.at[0])
    fetch_c = pltpu.make_async_copy(c_hbm, c_ref, sems.at[1])
    fetch_m.start()
    fetch_c.start()
    fetch_m.wait()
    m = fold(m_ref[...]).astype(F32)
    line = floor_div(m, N)
    gc = m - N * line
    ga = floor_div(line, planes)
    gb = line - planes * ga
    ga = jnp.where(ga < 96, ga, ga - 96)
    gc = jnp.where(gc < 96, gc, gc - 64)
    gb_ref[...] = gb
    lane_r = lax.broadcasted_iota(jnp.int32, (CHUNK, 2 * CHUNK), 0)
    lane_c = lax.broadcasted_iota(jnp.int32, (CHUNK, 2 * CHUNK), 1)
    tri = jnp.where((lane_r < lane_c) | (lane_c >= CHUNK), 1.0, 0.0).astype(BF)
    row_r = lax.broadcasted_iota(jnp.int32, (rows + 16, rows), 0)
    row_c = lax.broadcasted_iota(jnp.int32, (rows + 16, rows), 1)
    below = jnp.where(row_c < row_r, 1.0, 0.0).astype(BF)
    masks = [jnp.where(gb == float(g), 1.0, 0.0).astype(BF) for g in range(planes)]
    cum_ref[...] = mm(below, jnp.concatenate(masks, axis=1))
    tot_ref[...] = jnp.zeros_like(tot_ref)
    step = 3 if planes % 3 == 0 and planes > 3 else 1

    def at(g):
        return pl.ds(pl.multiple_of(g * CHUNK, CHUNK), CHUNK)

    def gather(i, carry):
        for j in range(step):
            g = i * step + j
            tot_ref[pl.ds(g, 1), :] = cum_ref[rows : rows + 8, at(g)][0:1]
        return carry

    lax.fori_loop(0, planes // step, gather, 0)
    lane_ref[...] = mm(tot_ref[...].astype(BF), tri)
    step_id = lax.broadcasted_iota(jnp.int32, (8, CHUNK), 1).astype(F32)

    def rank(i, carry):
        base, place, plane_of = carry
        for j in range(step):
            g = i * step + j
            gf = g.astype(F32)
            lanes = lane_ref[pl.ds(g, 1), :]
            here = cum_ref[0:rows, at(g)] + (lanes[:, :CHUNK] + base)
            place = jnp.where(gb_ref[...] == gf, here, place)
            base = base + lanes[:, CHUNK:]
            end = gf + jnp.floor((jnp.maximum(base, 1.0) - 1.0) * (1.0 / CHUNK))
            end = jnp.where(gf < planes - 1.0, end, 1e6)
            plane_of = plane_of + jnp.where(end < step_id, 1.0, 0.0)
        return base, place, plane_of

    _, place, plane_of = lax.fori_loop(
        0,
        planes // step,
        rank,
        (jnp.zeros((1, CHUNK), F32), jnp.zeros((rows, CHUNK), F32), jnp.zeros((8, CHUNK), F32)),
    )
    d_ref[...] = place
    fetch_c.wait()
    re_h, re_l = split(fold(c_ref[0]))
    im_h, im_l = split(fold(c_ref[1]))
    for q, value in enumerate((re_h, re_l, im_h, im_l, ga, gb, gc)):
        val_ref[q] = value.astype(F32)
    acc_ref[...] = jnp.zeros_like(acc_ref)
    hi_id, lo_id = ident(rows), ident(CHUNK)
    zero = jnp.zeros((rows, CHUNK), BF)

    def body(i, carry):
        part = pl.ds(pl.multiple_of(i * 8, 8), 8)
        d = d_ref[part, :]
        hi = jnp.floor(d * (1.0 / CHUNK))
        lo = d - CHUNK * hi
        values = [val_ref[q, part, :] for q in range(7)]
        left, right = [], []
        for j in range(8):
            at_hi = equal(hi[j : j + 1], hi_id)
            left.append(
                jnp.concatenate([jnp.where(at_hi, wide(v[j : j + 1], rows), zero) for v in values], axis=0)
            )
            right.append(one_hot(lo[j : j + 1], lo_id))
        acc_ref[...] += lax.dot_general(
            jnp.concatenate(left, axis=1), jnp.concatenate(right, axis=1), NT, preferred_element_type=F32
        )
        return carry

    lax.fori_loop(0, rows // 8, body, 0)
    got = [acc_ref[q * rows : (q + 1) * rows] for q in range(7)]
    both_ref[0:2] = c_ref[...]
    for q in range(2):
        value = got[2 * q] + got[2 * q + 1]
        out_ref[q * rows : (q + 1) * rows] = value
        both_ref[2 + q] = unfold(value)
    out_ref[2 * rows : 3 * rows] = (got[4] * planes + got[5]) * LANES + got[6]
    out_ref[3 * rows : 3 * rows + 8] = plane_of


def sin_cos(x):
    y = x * x
    s = -1.0 / 39916800.0 + y * (1.0 / 6227020800.0)
    s = 1.0 / 362880.0 + y * s
    s = -1.0 / 5040.0 + y * s
    s = 1.0 / 120.0 + y * s
    s = -1.0 / 6.0 + y * s
    s = x + x * y * s
    c = 1.0 / 479001600.0 - y * (1.0 / 87178291200.0)
    c = -1.0 / 3628800.0 + y * c
    c = 1.0 / 40320.0 + y * c
    c = -1.0 / 720.0 + y * c
    c = 1.0 / 24.0 + y * c
    c = -0.5 + y * c
    c = 1.0 + y * c
    return s, c


def decode(cell, planes):
    line = jnp.floor(cell * (1.0 / LANES))
    gc = cell - LANES * line
    ga = floor_div(line, planes)
    gb = line - planes * ga
    freq = jnp.where(ga < 48, ga, ga - 96)
    return freq, gb, gc


def phase(freq, first):
    turn = freq * first
    turn = turn - N * jnp.floor(turn * (1.0 / N) + 0.5)
    s, c = sin_cos(turn * (math.pi / N))
    return 1.0 - 2.0 * s * s, 2.0 * s * c


def times(a, b):
    return a[0] * b[0] - a[1] * b[1], a[0] * b[1] + a[1] * b[0]


def firsts(planes):
    me = lax.axis_index("grid")
    return (me * planes).astype(F32), ((me ^ 1) * planes).astype(F32)


def pair_code(planes, steps_ref, code_ref, rows, step):
    g = steps_ref[0, step].astype(jnp.int32)
    c = jnp.minimum(step - g, rows - 1)
    wanted = jnp.where(step < rows + planes - 1, g, -1).astype(F32)
    code = jnp.where(code_ref[0, pl.ds(c, 1), :] == wanted, code_ref[1, pl.ds(c, 1), :], -1.0)
    return g, c, code


def row_of(ref, index, c):
    return jnp.broadcast_to(ref[index, pl.ds(c, 1), :], (8, CHUNK))


def rise(e_ref, start, turn):
    rows = turn[0].shape[0]
    value = start
    for k in range(8):
        for p in range(2):
            for q in range(2):
                e_ref[p, q, pl.ds(k, rows, stride=8), :] = value[p][:, q * LANES : (q + 1) * LANES]
        if k < 7:
            value = times(value, turn)


def risen(e_ref, c):
    where = pl.ds(pl.multiple_of(c * 8, 8), 8)
    return tuple(jnp.concatenate([e_ref[p, 0, where, :], e_ref[p, 1, where, :]], axis=1) for p in range(2))


def prepare(planes, cell, w_ref, code_ref, id_ref):
    freq, gb, gc = decode(cell, planes)
    code_ref[0] = gb
    code_ref[1] = gc
    id_ref[...] = ident(LANES)
    s, c = sin_cos(freq * (2.0 * math.pi / N))
    turn = eight = (c, s)
    for _ in range(3):
        eight = times(eight, eight)
    w_ref[0], w_ref[1] = eight
    return turn, [phase(freq, first) for first in firsts(planes)]


def spread_kernel(
    planes, height, unroll, slab_ref, steps_ref, own_ref, sib_ref, w_ref, code_ref, id_ref, e0_ref, e1_ref
):
    rows = w_ref.shape[1]
    turn, starts = prepare(planes, slab_ref[0, 2 * rows : 3 * rows], w_ref, code_ref, id_ref)
    value = slab_ref[0, 0:rows], slab_ref[0, rows : 2 * rows]
    for e_ref, start in zip((e0_ref, e1_ref), starts):
        rise(e_ref, times(value, start), turn)
    own_ref[...] = jnp.zeros_like(own_ref)
    sib_ref[...] = jnp.zeros_like(sib_ref)

    def visit(i, carry):
        ids = id_ref[...]
        for j in range(unroll):
            g, c, code = pair_code(planes, steps_ref, code_ref, rows, i * unroll + j)
            eight = row_of(w_ref, 0, c), row_of(w_ref, 1, c)
            lines = []
            for e_ref in (e0_ref, e1_ref):
                z = risen(e_ref, c)
                real, imag = [z[0]], [z[1]]
                for _ in range(height // 8 - 1):
                    z = times(z, eight)
                    real.append(z[0])
                    imag.append(z[1])
                lines += real + imag
            high, low = split(jnp.concatenate(lines, axis=0))
            got = lax.dot_general(
                jnp.concatenate([high, low], axis=0), one_hot(code, ids), NT, preferred_element_type=F32
            )
            got = got[: 4 * height] + got[4 * height :]
            where = pl.ds(pl.multiple_of(g * (2 * height), 8), 2 * height)
            own_ref[0, where, :] += got[: 2 * height]
            sib_ref[0, where, :] += got[2 * height :]
        return carry

    lax.fori_loop(0, -(-(rows + planes - 1) // unroll), visit, 0)


def collect_kernel(
    planes, height, unroll, slab_ref, steps_ref, own_ref, sib_ref, h_ref, w_ref, code_ref, id_ref, e_ref, u2_ref
):
    rows = w_ref.shape[1]
    turn, starts = prepare(planes, slab_ref[0, 2 * rows : 3 * rows], w_ref, code_ref, id_ref)
    for q, start in enumerate(starts):
        w_ref[2 + 2 * q], w_ref[3 + 2 * q] = start
    rise(e_ref, (jnp.ones_like(turn[0]), jnp.zeros_like(turn[0])), turn)
    for g in range(planes):
        where = slice(g * 2 * height, (g + 1) * 2 * height)
        high, low = split(jnp.concatenate([own_ref[0, where, :], sib_ref[0, where, :]], axis=0))
        u2_ref[g] = jnp.concatenate([high, low], axis=0)
    h_ref[...] = jnp.zeros_like(h_ref)

    def visit(i, carry):
        ids = id_ref[...]
        for j in range(unroll):
            g, c, code = pair_code(planes, steps_ref, code_ref, rows, i * unroll + j)
            got = mm(u2_ref[g], one_hot(code, ids))
            got = got[: 4 * height] + got[4 * height :]
            jr, ji = row_of(w_ref, 0, c), row_of(w_ref, 1, c)
            hr = hi = 0.0
            for q in range(2):
                value = got[q * 2 * height : (q + 1) * 2 * height]
                ar = value[height - 8 : height]
                ai = value[2 * height - 8 : 2 * height]
                for t in range(height // 8 - 2, -1, -1):
                    ar, ai = (
                        ar * jr + ai * ji + value[8 * t : 8 * t + 8],
                        ai * jr - ar * ji + value[height + 8 * t : height + 8 * t + 8],
                    )
                zr, zi = row_of(w_ref, 2 + 2 * q, c), row_of(w_ref, 3 + 2 * q, c)
                hr, hi = hr + ar * zr + ai * zi, hi + ai * zr - ar * zi
            er, ei = risen(e_ref, c)
            h_ref[0, pl.ds(c, 1), :] += jnp.sum(hr * er + hi * ei, axis=0, keepdims=True)
            h_ref[0, pl.ds(rows + c, 1), :] += jnp.sum(hi * er - hr * ei, axis=0, keepdims=True)
        return carry

    lax.fori_loop(0, -(-(rows + planes - 1) // unroll), visit, 0)


def potential_kernel(planes, calls, parts, *refs):
    own, sib = refs[:calls], refs[calls : 2 * calls]
    v_ref, *tables_hbm = refs[2 * calls : 2 * calls + 5]
    keep_ref = refs[2 * calls + 5]
    send_refs = refs[2 * calls + 6 : 2 * calls + 6 + len(parts)]
    t_ref, u_ref, bf_ref, cf_ref, ci_ref, bi_ref, in_sems, out_sems, table_sems = refs[2 * calls + 6 + len(parts) :]
    step = pl.program_id(0)
    me = lax.axis_index("grid")
    half = keep_ref.shape[0]
    per_call = half // calls
    tiles = t_ref.shape[2]
    last = tiles - 1

    def place(j, q):
        return pl.ds((me ^ (2 * j + q)) * planes, planes)

    def arrivals(t):
        for q, blocks in enumerate((own, sib)):
            for j in range(half):
                yield pltpu.make_async_copy(
                    blocks[j // per_call].at[j % per_call, :, :, t], t_ref.at[place(j, q), :, t], in_sems.at[t, q, j]
                )

    def departures(t):
        for j in range(half):
            yield pltpu.make_async_copy(
                u_ref.at[place(j, 0), :, t], keep_ref.at[j, :, :, t], out_sems.at[t, 0, j]
            )
        for ref, part in zip(send_refs, parts):
            for i, j in enumerate(part):
                yield pltpu.make_async_copy(
                    u_ref.at[place(j, 1), :, t], ref.at[i, :, :, t], out_sems.at[t, 1, j]
                )

    def fetches():
        for q, (source, target) in enumerate(zip(tables_hbm, (bf_ref, cf_ref, ci_ref, bi_ref))):
            yield pltpu.make_async_copy(source, target, table_sems.at[q])

    @pl.when(step == 0)
    def _():
        for copies in (arrivals(0), fetches(), *(arrivals(t) for t in range(1, tiles))):
            for copy in copies:
                copy.start()
        for copies in (arrivals(0), fetches()):
            for copy in copies:
                copy.wait()

    for t in range(1, tiles):

        @pl.when(step == t)
        def _(t=t):
            for copy in arrivals(t):
                copy.wait()

    group = 8

    def turn(x):
        return jnp.transpose(x, (1, 0, 2))

    def abreast(x):
        return jnp.concatenate([x[j] for j in range(group)], axis=1)

    x = jnp.concatenate([abreast(turn(t_ref[:, q, step])) for q in range(2)], axis=0)
    high, low = split(x)
    x = mm(bf_ref[...], jnp.concatenate([high, high, low], axis=0))
    x = jnp.concatenate(
        [
            jnp.concatenate([x[:N, j * LANES : (j + 1) * LANES], x[N:, j * LANES : (j + 1) * LANES]], axis=1)
            for j in range(group)
        ],
        axis=0,
    )
    high, low = split(x)
    x = mm(jnp.concatenate([high, high, low], axis=1), cf_ref[...])
    cells = [turn(v_ref[0, :, q]) for q in range(3)]
    v = []
    for j in range(group):
        t = [cell[j] for cell in cells]
        v.append(jnp.concatenate([t[0], t[1][:, :64]], axis=1))
        v.append(jnp.concatenate([t[1][:, 64:], t[2]], axis=1))
    v = jnp.concatenate(v, axis=0)
    x = x * jnp.concatenate([v, v], axis=1)
    high, low = split(x)
    x = mm(jnp.concatenate([high, high, low], axis=1), ci_ref[...])
    x = jnp.concatenate(
        [
            jnp.concatenate([x[j * N : (j + 1) * N, q * LANES : (q + 1) * LANES] for j in range(group)], axis=1)
            for q in range(2)
        ],
        axis=0,
    )
    high, low = split(x)
    x = mm(bi_ref[...], jnp.concatenate([high, high, low], axis=0))
    for q in range(2):
        part = x[q * N : (q + 1) * N]
        u_ref[:, q, step] = turn(jnp.stack([part[:, j * LANES : (j + 1) * LANES] for j in range(group)]))

    for t in range(tiles):

        @pl.when(step == t)
        def _(t=t):
            for copy in departures(t):
                copy.start()

    @pl.when(step == last)
    def _():
        for t in range(tiles):
            for copy in departures(t):
                copy.wait()


def sum_kernel(arrivals, *refs):
    recv_refs, coef_refs, (total_ref, part_ref) = refs[:arrivals], refs[arrivals:-2], refs[-2:]
    total = None
    for recv in recv_refs:
        for s in range(recv.shape[0]):
            total = recv[s] if total is None else total + recv[s]
    total_ref[...] = total
    rows = total.shape[0] // 2
    hr, hi = unfold(total[:rows]), unfold(total[rows:])
    real, imag = [], []
    for coef in coef_refs:
        cr, ci = coef[2], coef[3]
        real.append(jnp.sum(cr * hr + ci * hi, axis=0, keepdims=True))
        imag.append(jnp.sum(cr * hi - ci * hr, axis=0, keepdims=True))
    sums = jnp.concatenate(real + imag, axis=0)
    for s in range(part_ref.shape[0]):
        part_ref[s] = sums


def unsort_kernel(total_ref, d_ref, h_ref, hl_ref, wide_ref):
    rows = d_ref.shape[0]
    high, low = split(total_ref[...])
    hl_ref[0 : 2 * rows] = high
    hl_ref[2 * rows :] = low
    hi_id = lax.broadcasted_iota(jnp.int32, (rows, CHUNK), 0).astype(F32)
    lo_id = ident(CHUNK)

    def body(i, carry):
        part = pl.ds(pl.multiple_of(i * 8, 8), 8)
        d = d_ref[part, :]
        hi = jnp.floor(d * (1.0 / CHUNK))
        lo = d - CHUNK * hi
        real, imag = [], []
        for j in range(8):
            got = mm(hl_ref[...], one_hot(lo[j : j + 1], lo_id))
            got = got[: 2 * rows] + got[2 * rows :]
            at_hi = jnp.broadcast_to(hi[j : j + 1], (rows, CHUNK)) == hi_id
            real.append(jnp.sum(jnp.where(at_hi, got[:rows], 0.0), axis=0, keepdims=True))
            imag.append(jnp.sum(jnp.where(at_hi, got[rows:], 0.0), axis=0, keepdims=True))
        wide_ref[0, part, :] = jnp.concatenate(real, axis=0)
        wide_ref[1, part, :] = jnp.concatenate(imag, axis=0)
        return carry

    lax.fori_loop(0, rows // 8, body, 0)
    h_ref[0] = unfold(wide_ref[0])
    h_ref[1] = unfold(wide_ref[1])


def residual_kernel(scale, bands, h_ref, *refs):
    coef_refs, sum_refs, (out_ref, sub_ref, all_ref) = refs[:bands], refs[bands:-3], refs[-3:]
    band = lax.axis_index("band")
    me = lax.axis_index("grid")
    if len(sum_refs) > 1:
        for bits, part in enumerate(sum_refs):
            all_ref[me ^ bits] = part[0]
    else:
        all_ref[...] = sum_refs[0][...]
    sub = all_ref[0]
    for s in range(1, all_ref.shape[0]):
        sub = sub + all_ref[s]
    sub = jnp.sum(sub, axis=1, keepdims=True) * scale
    lane = lax.broadcasted_iota(jnp.int32, (1, LANES), 1)
    hr, hi = h_ref[0], h_ref[1]
    line_re = line_im = jnp.zeros((1, LANES), F32)
    for shift, coef in enumerate(coef_refs):
        sr, si = sub[shift : shift + 1], sub[bands + shift : bands + shift + 1]
        here = lane == lax.rem(band + bands - shift, bands)
        line_re = jnp.where(here, sr, line_re)
        line_im = jnp.where(here, si, line_im)
        cr, ci = coef[0], coef[1]
        hr = hr - (sr * cr - si * ci)
        hi = hi - (si * cr + sr * ci)
    out_ref[0] = hr
    out_ref[1] = hi
    sub_ref[0] = line_re[:, :bands]
    sub_ref[1] = line_im[:, :bands]


def params(mib):
    return pltpu.CompilerParams(vmem_limit_bytes=mib * 1024 * 1024)


def cost(flops):
    return pl.CostEstimate(flops=int(flops), bytes_accessed=0, transcendentals=0)


def whole(shape):
    return pl.BlockSpec(shape, lambda *_: (0,) * len(shape))


def local(coefficients, index_map, potential):
    slabs = lax.axis_size("grid")
    bands = lax.axis_size("band")
    planes = potential.shape[0]
    count = coefficients.shape[2]
    rows = count // CHUNK
    height = -(-planes // 8) * 8
    unroll = 44
    me = lax.axis_index("grid")
    half = slabs // 2
    anywhere = pl.BlockSpec(memory_space=pl.ANY)
    coef = coefficients.reshape(2, 2 * rows, LANES)
    table_rows = 3 * rows + 8
    sorted_pts, dest, both = pl.pallas_call(
        functools.partial(sort_kernel, planes),
        in_specs=[pl.BlockSpec(memory_space=pltpu.HBM)] * 2,
        out_shape=(
            jax.ShapeDtypeStruct((table_rows, CHUNK), F32),
            jax.ShapeDtypeStruct((rows, CHUNK), F32),
            jax.ShapeDtypeStruct((4, 2 * rows, LANES), F32),
        ),
        scratch_shapes=[
            pltpu.VMEM((7 * rows, CHUNK), F32),
            pltpu.VMEM((7, rows, CHUNK), F32),
            pltpu.VMEM((rows, CHUNK), F32),
            pltpu.VMEM((rows + 16, planes * CHUNK), F32),
            pltpu.VMEM((-(-planes // 16) * 16, CHUNK), F32),
            pltpu.VMEM((-(-planes // 16) * 16, 2 * CHUNK), F32),
            pltpu.VMEM((2 * rows, LANES), jnp.int32),
            pltpu.VMEM((2, 2 * rows, LANES), F32),
            pltpu.SemaphoreType.DMA((2,)),
        ],
        compiler_params=params(58),
        cost_estimate=cost(1e10),
        name="sort_points",
    )(index_map.reshape(2 * rows, LANES), coef)

    def swap(x, bits):
        return lax.ppermute(x, "grid", [(i, i ^ bits) for i in range(slabs)])

    if half <= 4:
        points = [sorted_pts[None]] + [swap(sorted_pts, 2 * j)[None] for j in range(1, min(half, 3))]
    else:
        everything = lax.all_gather(sorted_pts, "grid")
        points = [jnp.take(everything, me ^ (2 * jnp.arange(half)), axis=0)]
    calls = half if half <= 4 else 1
    per_call = half // calls
    lines = planes * 2 * height
    slab_spec = pl.BlockSpec((1, table_rows, CHUNK), lambda s: (s, 0, 0))
    steps_spec = pl.BlockSpec((None, 8, CHUNK), lambda s: (s, table_rows // 8 - 1, 0), memory_space=pltpu.SMEM)
    block_spec = pl.BlockSpec((1, lines, LANES), lambda s: (s, 0, 0))
    point_scratch = [pltpu.VMEM((6, rows, CHUNK), F32), pltpu.VMEM((2, rows, CHUNK), F32), pltpu.VMEM((LANES, LANES), BF)]
    risen_scratch = pltpu.VMEM((2, 2, 8 * rows, LANES), F32)
    spread = pl.pallas_call(
        functools.partial(spread_kernel, planes, height, unroll),
        grid=(per_call,),
        in_specs=[slab_spec, steps_spec],
        out_specs=(block_spec, block_spec),
        out_shape=(jax.ShapeDtypeStruct((per_call, lines, LANES), F32),) * 2,
        scratch_shapes=point_scratch + [risen_scratch] * 2,
        compiler_params=params(20),
        cost_estimate=cost(8e9),
        name="spread_points",
    )
    own, sib = [], []
    for call in range(calls):
        mine, theirs = spread(points[call], points[call])
        if call == 0 and half == 4:
            sorted_pts, theirs = lax.optimization_barrier((sorted_pts, theirs))
            points.append(swap(sorted_pts, 6)[None])
        own.append(mine)
        sib.append(swap(theirs, 1))
    cells = potential if height == planes else jnp.pad(potential, ((0, height - planes), (0, 0)))
    cells = cells.reshape(height // 8, 8, N * N // LANES, LANES).transpose(0, 2, 1, 3)
    cells = cells.reshape(height // 8, N // 2, 3, 8, LANES)
    *sib, mine = lax.optimization_barrier((*sib, both))
    coefs = [both]
    for shift in range(1, bands):
        coefs.append(lax.ppermute(mine, "band", [(i, (i + shift) % bands) for i in range(bands)]))
    constants = [jnp.asarray(t) for t in tables()]
    parts = [[1], [0, *range(2, half)]] if 2 <= half <= 4 else [list(range(half))]
    cube = (planes, 2, height // 8, 8, LANES)
    keep, *send = pl.pallas_call(
        functools.partial(potential_kernel, planes, calls, parts),
        grid=(height // 8,),
        in_specs=[anywhere] * (2 * calls)
        + [pl.BlockSpec((1, N // 2, 3, 8, LANES), lambda i: (i, 0, 0, 0, 0))]
        + [anywhere] * 4,
        out_specs=[anywhere] * (1 + len(parts)),
        out_shape=[jax.ShapeDtypeStruct((count_of, *cube), F32) for count_of in (half, *map(len, parts))],
        scratch_shapes=[
            pltpu.VMEM((N, *cube[1:]), F32),
            pltpu.VMEM((N, *cube[1:]), F32),
            *(pltpu.VMEM(t.shape, BF) for t in constants),
            pltpu.SemaphoreType.DMA((height // 8, 2, half)),
            pltpu.SemaphoreType.DMA((height // 8, 2, half)),
            pltpu.SemaphoreType.DMA((4,)),
        ],
        compiler_params=params(40),
        cost_estimate=cost(4e10),
        name="apply_potential",
    )(*(x.reshape(per_call, *cube) for x in (*own, *sib)), cells, *constants)
    tied = lax.optimization_barrier((*send, *coefs))
    coefs = tied[len(parts) :]
    keep = keep.reshape(half, lines, LANES)
    other = []
    for x in tied[: len(parts)]:
        if other:
            other[-1], x = lax.optimization_barrier((other[-1], x))
        other.append(swap(x, 1))
    other = [x.reshape(-1, lines, LANES) for x in other]

    def block_at(first):
        return pl.BlockSpec((1, lines, LANES), lambda s: (first + s, 0, 0))

    partial = []
    for call, table in enumerate(points):
        first = call * per_call
        number, part = next((i, part) for i, part in enumerate(parts) if first in part)
        partial.append(
            pl.pallas_call(
                functools.partial(collect_kernel, planes, height, unroll),
                grid=(per_call,),
                in_specs=[slab_spec, steps_spec, block_at(first), block_at(part.index(first))],
                out_specs=pl.BlockSpec((1, 2 * rows, CHUNK), lambda s: (s, 0, 0)),
                out_shape=jax.ShapeDtypeStruct((per_call, 2 * rows, CHUNK), F32),
                scratch_shapes=point_scratch + [risen_scratch, pltpu.VMEM((planes, 8 * height, LANES), BF)],
                compiler_params=params(24),
                cost_estimate=cost(8e9),
                name="collect_points",
            )(table, table, keep, other[number])
        )
    if half <= 4:
        arrived = [partial[0]] + [swap(partial[j], 2 * j) for j in range(1, half)]
    else:
        ids = jnp.arange(slabs)
        blocks = jnp.take(partial[0], (ids ^ me) // 2, axis=0)
        blocks = jnp.where(((ids ^ me) % 2 == 0)[:, None, None], blocks, 0.0)
        arrived = [lax.all_to_all(blocks, "grid", split_axis=0, concat_axis=0, tiled=True)]
    direct = slabs <= 8
    total, part = pl.pallas_call(
        functools.partial(sum_kernel, len(arrived)),
        out_shape=(
            jax.ShapeDtypeStruct((2 * rows, CHUNK), F32),
            jax.ShapeDtypeStruct((1 if direct else slabs, 2 * bands, LANES), F32),
        ),
        compiler_params=params(16),
        cost_estimate=cost(1e9),
        name="sum_points",
    )(*arrived, *coefs)
    if direct:
        sums = [part] + [swap(part, bits) for bits in range(1, slabs)]
    else:
        sums = [lax.all_to_all(part, "grid", split_axis=0, concat_axis=0, tiled=True)]
    applied = pl.pallas_call(
        unsort_kernel,
        out_shape=jax.ShapeDtypeStruct((2, 2 * rows, LANES), F32),
        scratch_shapes=[pltpu.VMEM((4 * rows, CHUNK), BF), pltpu.VMEM((2, rows, CHUNK), F32)],
        compiler_params=params(12),
        cost_estimate=cost(6e9),
        name="unsort_points",
    )(total, dest)
    resid, sub = pl.pallas_call(
        functools.partial(residual_kernel, 1.0 / (count * slabs), bands),
        out_shape=(
            jax.ShapeDtypeStruct((2, 2 * rows, LANES), F32),
            jax.ShapeDtypeStruct((2, 1, bands), F32),
        ),
        scratch_shapes=[pltpu.VMEM((slabs, 2 * bands, LANES), F32)],
        compiler_params=params(8),
        cost_estimate=cost(2e9),
        name="residual",
    )(applied, *coefs, *sums)
    return sub.transpose(0, 2, 1), resid.reshape(2, 1, count)


def solution(mesh):
    return jax.shard_map(
        local,
        mesh=mesh,
        in_specs=(P(None, "band", "grid"), P("grid"), P("grid", None)),
        out_specs=(P(None, None, "band"), P(None, "band", "grid")),
        check_vma=False,
    )
```

```python
import functools
import math

import jax
import jax.numpy as jnp
import numpy as np
from jax import lax
from jax.experimental import pallas as pl
from jax.experimental.pallas import tpu as pltpu
from jax.sharding import PartitionSpec as P

N = 192
CHUNK = 256
LANES = 128
BF = jnp.bfloat16
F32 = jnp.float32
NT = (((1,), (1,)), ((), ()))


def split(x):
    high = x.astype(BF)
    low = (x - high.astype(F32)).astype(BF)
    return high, low


def mm(a, b):
    return jnp.dot(a, b, preferred_element_type=F32)


def split_table(table):
    table = table.astype(np.float32)
    high = table.astype(BF)
    low = (table - high.astype(np.float32)).astype(BF)
    return high, low


@functools.cache
def tables():
    pos = np.arange(N)
    angle = 2.0 * math.pi * ((pos[:, None] * pos[None, :]) % N) / N
    cb, sb = np.cos(angle), np.sin(angle)
    order = np.concatenate([pos[0::2], pos[1::2]])
    co, so = cb[order], sb[order]
    b_fwd = np.block([[co, -so], [so, co]])
    b_inv = np.block([[co.T, so.T], [-so.T, co.T]])
    freq = np.arange(LANES)
    freq = np.where(freq < 64, freq, freq - LANES)
    keep = (np.abs(freq) < 48)[:, None]
    angle = 2.0 * math.pi * ((freq[:, None] * pos[None, :]) % N) / N
    cc, sc = np.cos(angle) * keep, np.sin(angle) * keep
    c_fwd = np.block([[cc, sc], [-sc, cc]])
    c_inv = np.block([[cc.T, -sc.T], [sc.T, cc.T]]) / float(N) ** 3
    bf_h, bf_l = split_table(b_fwd)
    bi_h, bi_l = split_table(b_inv)
    cf_h, cf_l = split_table(c_fwd)
    ci_h, ci_l = split_table(c_inv)
    return (
        np.concatenate([bf_h, bf_l, bf_h], axis=1),
        np.concatenate([cf_h, cf_l, cf_h], axis=0),
        np.concatenate([ci_h, ci_l, ci_h], axis=0),
        np.concatenate([bi_h, bi_l, bi_h], axis=1),
    )


def fold(x):
    half = x.shape[0] // 2
    return jnp.concatenate([x[:half], x[half:]], axis=1)


def unfold(x):
    return jnp.concatenate([x[:, :LANES], x[:, LANES:]], axis=0)


def wide(row, count):
    tile = jnp.broadcast_to(row, (16, row.shape[1])).astype(BF)
    return jnp.concatenate([tile] * (count // 16), axis=0)


def ident(count):
    return lax.broadcasted_iota(jnp.int32, (count, LANES), 0).astype(F32).astype(BF)


def equal(row, ids):
    code = wide(row, ids.shape[0])
    return code == jnp.concatenate([ids, ids], axis=1)


def one_hot(row, ids):
    one = jnp.ones((ids.shape[0], CHUNK), BF)
    return jnp.where(equal(row, ids), one, jnp.zeros_like(one))


def floor_div(x, divisor):
    return jnp.floor((x + 0.5) * (1.0 / divisor))


def sort_kernel(
    planes, m_hbm, c_hbm, out_ref, d_ref, both_ref, acc_ref, val_ref, gb_ref, cum_ref, tot_ref, lane_ref, m_ref, c_ref, sems
):
    rows = gb_ref.shape[0]
    fetch_m = pltpu.make_async_copy(m_hbm, m_ref, sems.at[0])
    fetch_c = pltpu.make_async_copy(c_hbm, c_ref, sems.at[1])
    fetch_m.start()
    fetch_c.start()
    fetch_m.wait()
    m = fold(m_ref[...]).astype(F32)
    line = floor_div(m, N)
    gc = m - N * line
    ga = floor_div(line, planes)
    gb = line - planes * ga
    ga = jnp.where(ga < 96, ga, ga - 96)
    gc = jnp.where(gc < 96, gc, gc - 64)
    gb_ref[...] = gb
    lane_r = lax.broadcasted_iota(jnp.int32, (CHUNK, 2 * CHUNK), 0)
    lane_c = lax.broadcasted_iota(jnp.int32, (CHUNK, 2 * CHUNK), 1)
    tri = jnp.where((lane_r < lane_c) | (lane_c >= CHUNK), 1.0, 0.0).astype(BF)
    row_r = lax.broadcasted_iota(jnp.int32, (rows + 16, rows), 0)
    row_c = lax.broadcasted_iota(jnp.int32, (rows + 16, rows), 1)
    below = jnp.where(row_c < row_r, 1.0, 0.0).astype(BF)
    masks = [jnp.where(gb == float(g), 1.0, 0.0).astype(BF) for g in range(planes)]
    cum_ref[...] = mm(below, jnp.concatenate(masks, axis=1))
    tot_ref[...] = jnp.zeros_like(tot_ref)
    step = 3 if planes % 3 == 0 and planes > 3 else 1

    def at(g):
        return pl.ds(pl.multiple_of(g * CHUNK, CHUNK), CHUNK)

    def gather(i, carry):
        for j in range(step):
            g = i * step + j
            tot_ref[pl.ds(g, 1), :] = cum_ref[rows : rows + 8, at(g)][0:1]
        return carry

    lax.fori_loop(0, planes // step, gather, 0)
    lane_ref[...] = mm(tot_ref[...].astype(BF), tri)
    step_id = lax.broadcasted_iota(jnp.int32, (8, CHUNK), 1).astype(F32)

    def rank(i, carry):
        base, place, plane_of = carry
        for j in range(step):
            g = i * step + j
            gf = g.astype(F32)
            lanes = lane_ref[pl.ds(g, 1), :]
            here = cum_ref[0:rows, at(g)] + (lanes[:, :CHUNK] + base)
            place = jnp.where(gb_ref[...] == gf, here, place)
            base = base + lanes[:, CHUNK:]
            end = gf + jnp.floor((jnp.maximum(base, 1.0) - 1.0) * (1.0 / CHUNK))
            end = jnp.where(gf < planes - 1.0, end, 1e6)
            plane_of = plane_of + jnp.where(end < step_id, 1.0, 0.0)
        return base, place, plane_of

    _, place, plane_of = lax.fori_loop(
        0,
        planes // step,
        rank,
        (jnp.zeros((1, CHUNK), F32), jnp.zeros((rows, CHUNK), F32), jnp.zeros((8, CHUNK), F32)),
    )
    d_ref[...] = place
    fetch_c.wait()
    re_h, re_l = split(fold(c_ref[0]))
    im_h, im_l = split(fold(c_ref[1]))
    for q, value in enumerate((re_h, re_l, im_h, im_l, ga, gb, gc)):
        val_ref[q] = value.astype(F32)
    acc_ref[...] = jnp.zeros_like(acc_ref)
    hi_id, lo_id = ident(rows), ident(CHUNK)
    zero = jnp.zeros((rows, CHUNK), BF)

    def body(i, carry):
        part = pl.ds(pl.multiple_of(i * 8, 8), 8)
        d = d_ref[part, :]
        hi = jnp.floor(d * (1.0 / CHUNK))
        lo = d - CHUNK * hi
        values = [val_ref[q, part, :] for q in range(7)]
        left, right = [], []
        for j in range(8):
            at_hi = equal(hi[j : j + 1], hi_id)
            left.append(
                jnp.concatenate([jnp.where(at_hi, wide(v[j : j + 1], rows), zero) for v in values], axis=0)
            )
            right.append(one_hot(lo[j : j + 1], lo_id))
        acc_ref[...] += lax.dot_general(
            jnp.concatenate(left, axis=1), jnp.concatenate(right, axis=1), NT, preferred_element_type=F32
        )
        return carry

    lax.fori_loop(0, rows // 8, body, 0)
    got = [acc_ref[q * rows : (q + 1) * rows] for q in range(7)]
    both_ref[0:2] = c_ref[...]
    for q in range(2):
        value = got[2 * q] + got[2 * q + 1]
        out_ref[q * rows : (q + 1) * rows] = value
        both_ref[2 + q] = unfold(value)
    out_ref[2 * rows : 3 * rows] = (got[4] * planes + got[5]) * LANES + got[6]
    out_ref[3 * rows : 3 * rows + 8] = plane_of


def sin_cos(x):
    y = x * x
    s = -1.0 / 39916800.0 + y * (1.0 / 6227020800.0)
    s = 1.0 / 362880.0 + y * s
    s = -1.0 / 5040.0 + y * s
    s = 1.0 / 120.0 + y * s
    s = -1.0 / 6.0 + y * s
    s = x + x * y * s
    c = 1.0 / 479001600.0 - y * (1.0 / 87178291200.0)
    c = -1.0 / 3628800.0 + y * c
    c = 1.0 / 40320.0 + y * c
    c = -1.0 / 720.0 + y * c
    c = 1.0 / 24.0 + y * c
    c = -0.5 + y * c
    c = 1.0 + y * c
    return s, c


def decode(cell, planes):
    line = jnp.floor(cell * (1.0 / LANES))
    gc = cell - LANES * line
    ga = floor_div(line, planes)
    gb = line - planes * ga
    freq = jnp.where(ga < 48, ga, ga - 96)
    return freq, gb, gc


def phase(freq, first):
    turn = freq * first
    turn = turn - N * jnp.floor(turn * (1.0 / N) + 0.5)
    s, c = sin_cos(turn * (math.pi / N))
    return 1.0 - 2.0 * s * s, 2.0 * s * c


def powers(freq, w_ref):
    s, c = sin_cos(freq * (2.0 * math.pi / N))
    for q in range(4):
        w_ref[4 + 2 * q] = c
        w_ref[5 + 2 * q] = s
        s, c = 2.0 * s * c, c * c - s * s


def firsts(planes):
    me = lax.axis_index("grid")
    return (me * planes).astype(F32), ((me ^ 1) * planes).astype(F32)


def pair_code(planes, steps_ref, code_ref, rows, step):
    g = steps_ref[0, step].astype(jnp.int32)
    c = jnp.minimum(step - g, rows - 1)
    wanted = jnp.where(step < rows + planes - 1, g, -1).astype(F32)
    code = jnp.where(code_ref[0, pl.ds(c, 1), :] == wanted, code_ref[1, pl.ds(c, 1), :], -1.0)
    return g, c, code


def row_of(ref, index, c):
    return jnp.broadcast_to(ref[index, pl.ds(c, 1), :], (8, CHUNK))


def rise(w_ref, c):
    k = lax.broadcasted_iota(jnp.int32, (8, CHUNK), 0)
    er = ei = None
    for bit in range(3):
        on = (k & (1 << bit)) != 0
        fr = jnp.where(on, row_of(w_ref, 4 + 2 * bit, c), 1.0)
        fi = jnp.where(on, row_of(w_ref, 5 + 2 * bit, c), 0.0)
        if er is None:
            er, ei = fr, fi
        else:
            er, ei = er * fr - ei * fi, er * fi + ei * fr
    return er, ei


def prepare(planes, cell, w_ref, code_ref, id_ref):
    freq, gb, gc = decode(cell, planes)
    code_ref[0] = gb
    code_ref[1] = gc
    id_ref[...] = ident(LANES)
    for q, first in enumerate(firsts(planes)):
        w_ref[2 * q], w_ref[2 * q + 1] = phase(freq, first)
    powers(freq, w_ref)


def spread_kernel(planes, height, unroll, slab_ref, steps_ref, own_ref, sib_ref, w_ref, code_ref, id_ref):
    rows = w_ref.shape[1]
    prepare(planes, slab_ref[0, 2 * rows : 3 * rows], w_ref, code_ref, id_ref)
    re, im = slab_ref[0, 0:rows], slab_ref[0, rows : 2 * rows]
    for q in range(2):
        sr, si = w_ref[2 * q], w_ref[2 * q + 1]
        w_ref[2 * q] = re * sr - im * si
        w_ref[2 * q + 1] = re * si + im * sr
    own_ref[...] = jnp.zeros_like(own_ref)
    sib_ref[...] = jnp.zeros_like(sib_ref)

    def visit(i, carry):
        ids = id_ref[...]
        for j in range(unroll):
            g, c, code = pair_code(planes, steps_ref, code_ref, rows, i * unroll + j)
            er, ei = rise(w_ref, c)
            jr, ji = row_of(w_ref, 10, c), row_of(w_ref, 11, c)
            lines = []
            for q in range(2):
                zr, zi = row_of(w_ref, 2 * q, c), row_of(w_ref, 2 * q + 1, c)
                zr, zi = er * zr - ei * zi, er * zi + ei * zr
                real, imag = [zr], [zi]
                for _ in range(height // 8 - 1):
                    zr, zi = zr * jr - zi * ji, zr * ji + zi * jr
                    real.append(zr)
                    imag.append(zi)
                lines += real + imag
            high, low = split(jnp.concatenate(lines, axis=0))
            got = lax.dot_general(
                jnp.concatenate([high, low], axis=0), one_hot(code, ids), NT, preferred_element_type=F32
            )
            got = got[: 4 * height] + got[4 * height :]
            where = pl.ds(pl.multiple_of(g * (2 * height), 8), 2 * height)
            own_ref[0, where, :] += got[: 2 * height]
            sib_ref[0, where, :] += got[2 * height :]
        return carry

    lax.fori_loop(0, -(-(rows + planes - 1) // unroll), visit, 0)


def collect_kernel(
    planes, height, unroll, slab_ref, steps_ref, own_ref, sib_ref, h_ref, w_ref, code_ref, id_ref, u2_ref
):
    rows = w_ref.shape[1]
    prepare(planes, slab_ref[0, 2 * rows : 3 * rows], w_ref, code_ref, id_ref)
    for g in range(planes):
        where = slice(g * 2 * height, (g + 1) * 2 * height)
        high, low = split(jnp.concatenate([own_ref[0, where, :], sib_ref[0, where, :]], axis=0))
        u2_ref[g] = jnp.concatenate([high, low], axis=0)
    h_ref[...] = jnp.zeros_like(h_ref)

    def visit(i, carry):
        ids = id_ref[...]
        for j in range(unroll):
            g, c, code = pair_code(planes, steps_ref, code_ref, rows, i * unroll + j)
            got = mm(u2_ref[g], one_hot(code, ids))
            got = got[: 4 * height] + got[4 * height :]
            jr, ji = row_of(w_ref, 10, c), row_of(w_ref, 11, c)
            hr = hi = 0.0
            for q in range(2):
                value = got[q * 2 * height : (q + 1) * 2 * height]
                ar = value[height - 8 : height]
                ai = value[2 * height - 8 : 2 * height]
                for t in range(height // 8 - 2, -1, -1):
                    ar, ai = (
                        ar * jr + ai * ji + value[8 * t : 8 * t + 8],
                        ai * jr - ar * ji + value[height + 8 * t : height + 8 * t + 8],
                    )
                zr, zi = row_of(w_ref, 2 * q, c), row_of(w_ref, 2 * q + 1, c)
                hr, hi = hr + ar * zr + ai * zi, hi + ai * zr - ar * zi
            er, ei = rise(w_ref, c)
            h_ref[0, pl.ds(c, 1), :] += jnp.sum(hr * er + hi * ei, axis=0, keepdims=True)
            h_ref[0, pl.ds(rows + c, 1), :] += jnp.sum(hi * er - hr * ei, axis=0, keepdims=True)
        return carry

    lax.fori_loop(0, -(-(rows + planes - 1) // unroll), visit, 0)


def potential_kernel(planes, calls, parts, *refs):
    own, sib = refs[:calls], refs[calls : 2 * calls]
    v_ref, *tables_hbm = refs[2 * calls : 2 * calls + 5]
    keep_ref = refs[2 * calls + 5]
    send_refs = refs[2 * calls + 6 : 2 * calls + 6 + len(parts)]
    t_ref, u_ref, bf_ref, cf_ref, ci_ref, bi_ref, in_sems, out_sems, table_sems = refs[2 * calls + 6 + len(parts) :]
    step = pl.program_id(0)
    me = lax.axis_index("grid")
    half = keep_ref.shape[0]
    per_call = half // calls
    tiles = t_ref.shape[2]
    last = tiles - 1

    def place(j, q):
        return pl.ds((me ^ (2 * j + q)) * planes, planes)

    def arrivals(t):
        for q, blocks in enumerate((own, sib)):
            for j in range(half):
                yield pltpu.make_async_copy(
                    blocks[j // per_call].at[j % per_call, :, :, t], t_ref.at[place(j, q), :, t], in_sems.at[t, q, j]
                )

    def departures(t):
        for j in range(half):
            yield pltpu.make_async_copy(
                u_ref.at[place(j, 0), :, t], keep_ref.at[j, :, :, t], out_sems.at[t, 0, j]
            )
        for ref, part in zip(send_refs, parts):
            for i, j in enumerate(part):
                yield pltpu.make_async_copy(
                    u_ref.at[place(j, 1), :, t], ref.at[i, :, :, t], out_sems.at[t, 1, j]
                )

    def fetches():
        for q, (source, target) in enumerate(zip(tables_hbm, (bf_ref, cf_ref, ci_ref, bi_ref))):
            yield pltpu.make_async_copy(source, target, table_sems.at[q])

    @pl.when(step == 0)
    def _():
        for copies in (arrivals(0), fetches(), *(arrivals(t) for t in range(1, tiles))):
            for copy in copies:
                copy.start()
        for copies in (arrivals(0), fetches()):
            for copy in copies:
                copy.wait()

    for t in range(1, tiles):

        @pl.when(step == t)
        def _(t=t):
            for copy in arrivals(t):
                copy.wait()

    group = 8

    def turn(x):
        return jnp.transpose(x, (1, 0, 2))

    def abreast(x):
        return jnp.concatenate([x[j] for j in range(group)], axis=1)

    x = jnp.concatenate([abreast(turn(t_ref[:, q, step])) for q in range(2)], axis=0)
    high, low = split(x)
    x = mm(bf_ref[...], jnp.concatenate([high, high, low], axis=0))
    x = jnp.concatenate(
        [
            jnp.concatenate([x[:N, j * LANES : (j + 1) * LANES], x[N:, j * LANES : (j + 1) * LANES]], axis=1)
            for j in range(group)
        ],
        axis=0,
    )
    high, low = split(x)
    x = mm(jnp.concatenate([high, high, low], axis=1), cf_ref[...])
    cells = [turn(v_ref[0, :, q]) for q in range(3)]
    v = []
    for j in range(group):
        t = [cell[j] for cell in cells]
        v.append(jnp.concatenate([t[0], t[1][:, :64]], axis=1))
        v.append(jnp.concatenate([t[1][:, 64:], t[2]], axis=1))
    v = jnp.concatenate(v, axis=0)
    x = x * jnp.concatenate([v, v], axis=1)
    high, low = split(x)
    x = mm(jnp.concatenate([high, high, low], axis=1), ci_ref[...])
    x = jnp.concatenate(
        [
            jnp.concatenate([x[j * N : (j + 1) * N, q * LANES : (q + 1) * LANES] for j in range(group)], axis=1)
            for q in range(2)
        ],
        axis=0,
    )
    high, low = split(x)
    x = mm(bi_ref[...], jnp.concatenate([high, high, low], axis=0))
    for q in range(2):
        part = x[q * N : (q + 1) * N]
        u_ref[:, q, step] = turn(jnp.stack([part[:, j * LANES : (j + 1) * LANES] for j in range(group)]))

    for t in range(tiles):

        @pl.when(step == t)
        def _(t=t):
            for copy in departures(t):
                copy.start()

    @pl.when(step == last)
    def _():
        for t in range(tiles):
            for copy in departures(t):
                copy.wait()


def sum_kernel(arrivals, *refs):
    recv_refs, coef_refs, (total_ref, part_ref) = refs[:arrivals], refs[arrivals:-2], refs[-2:]
    total = None
    for recv in recv_refs:
        for s in range(recv.shape[0]):
            total = recv[s] if total is None else total + recv[s]
    total_ref[...] = total
    rows = total.shape[0] // 2
    hr, hi = unfold(total[:rows]), unfold(total[rows:])
    real, imag = [], []
    for coef in coef_refs:
        cr, ci = coef[2], coef[3]
        real.append(jnp.sum(cr * hr + ci * hi, axis=0, keepdims=True))
        imag.append(jnp.sum(cr * hi - ci * hr, axis=0, keepdims=True))
    sums = jnp.concatenate(real + imag, axis=0)
    for s in range(part_ref.shape[0]):
        part_ref[s] = sums


def unsort_kernel(total_ref, d_ref, h_ref, hl_ref, wide_ref):
    rows = d_ref.shape[0]
    high, low = split(total_ref[...])
    hl_ref[0 : 2 * rows] = high
    hl_ref[2 * rows :] = low
    hi_id = lax.broadcasted_iota(jnp.int32, (rows, CHUNK), 0).astype(F32)
    lo_id = ident(CHUNK)

    def body(i, carry):
        part = pl.ds(pl.multiple_of(i * 8, 8), 8)
        d = d_ref[part, :]
        hi = jnp.floor(d * (1.0 / CHUNK))
        lo = d - CHUNK * hi
        real, imag = [], []
        for j in range(8):
            got = mm(hl_ref[...], one_hot(lo[j : j + 1], lo_id))
            got = got[: 2 * rows] + got[2 * rows :]
            at_hi = jnp.broadcast_to(hi[j : j + 1], (rows, CHUNK)) == hi_id
            real.append(jnp.sum(jnp.where(at_hi, got[:rows], 0.0), axis=0, keepdims=True))
            imag.append(jnp.sum(jnp.where(at_hi, got[rows:], 0.0), axis=0, keepdims=True))
        wide_ref[0, part, :] = jnp.concatenate(real, axis=0)
        wide_ref[1, part, :] = jnp.concatenate(imag, axis=0)
        return carry

    lax.fori_loop(0, rows // 8, body, 0)
    h_ref[0] = unfold(wide_ref[0])
    h_ref[1] = unfold(wide_ref[1])


def residual_kernel(scale, bands, h_ref, *refs):
    coef_refs, sum_refs, (out_ref, sub_ref, all_ref) = refs[:bands], refs[bands:-3], refs[-3:]
    band = lax.axis_index("band")
    me = lax.axis_index("grid")
    if len(sum_refs) > 1:
        for j, part in enumerate(sum_refs):
            all_ref[lax.div(me, 2) ^ j] = part[0]
    else:
        all_ref[...] = sum_refs[0][...]
    sub = all_ref[0]
    for s in range(1, all_ref.shape[0]):
        sub = sub + all_ref[s]
    sub = jnp.sum(sub, axis=1, keepdims=True) * scale
    lane = lax.broadcasted_iota(jnp.int32, (1, LANES), 1)
    hr, hi = h_ref[0], h_ref[1]
    line_re = line_im = jnp.zeros((1, LANES), F32)
    for shift, coef in enumerate(coef_refs):
        sr, si = sub[shift : shift + 1], sub[bands + shift : bands + shift + 1]
        here = lane == lax.rem(band + bands - shift, bands)
        line_re = jnp.where(here, sr, line_re)
        line_im = jnp.where(here, si, line_im)
        cr, ci = coef[0], coef[1]
        hr = hr - (sr * cr - si * ci)
        hi = hi - (si * cr + sr * ci)
    out_ref[0] = hr
    out_ref[1] = hi
    sub_ref[0] = line_re[:, :bands]
    sub_ref[1] = line_im[:, :bands]


def params(mib):
    return pltpu.CompilerParams(vmem_limit_bytes=mib * 1024 * 1024)


def cost(flops):
    return pl.CostEstimate(flops=int(flops), bytes_accessed=0, transcendentals=0)


def whole(shape):
    return pl.BlockSpec(shape, lambda *_: (0,) * len(shape))


def local(coefficients, index_map, potential):
    slabs = lax.axis_size("grid")
    bands = lax.axis_size("band")
    planes = potential.shape[0]
    count = coefficients.shape[2]
    rows = count // CHUNK
    height = -(-planes // 8) * 8
    unroll = 44
    me = lax.axis_index("grid")
    half = slabs // 2
    anywhere = pl.BlockSpec(memory_space=pl.ANY)
    coef = coefficients.reshape(2, 2 * rows, LANES)
    table_rows = 3 * rows + 8
    sorted_pts, dest, both = pl.pallas_call(
        functools.partial(sort_kernel, planes),
        in_specs=[pl.BlockSpec(memory_space=pltpu.HBM)] * 2,
        out_shape=(
            jax.ShapeDtypeStruct((table_rows, CHUNK), F32),
            jax.ShapeDtypeStruct((rows, CHUNK), F32),
            jax.ShapeDtypeStruct((4, 2 * rows, LANES), F32),
        ),
        scratch_shapes=[
            pltpu.VMEM((7 * rows, CHUNK), F32),
            pltpu.VMEM((7, rows, CHUNK), F32),
            pltpu.VMEM((rows, CHUNK), F32),
            pltpu.VMEM((rows + 16, planes * CHUNK), F32),
            pltpu.VMEM((-(-planes // 16) * 16, CHUNK), F32),
            pltpu.VMEM((-(-planes // 16) * 16, 2 * CHUNK), F32),
            pltpu.VMEM((2 * rows, LANES), jnp.int32),
            pltpu.VMEM((2, 2 * rows, LANES), F32),
            pltpu.SemaphoreType.DMA((2,)),
        ],
        compiler_params=params(58),
        cost_estimate=cost(1e10),
        name="sort_points",
    )(index_map.reshape(2 * rows, LANES), coef)

    def swap(x, bits):
        return lax.ppermute(x, "grid", [(i, i ^ bits) for i in range(slabs)])

    if half <= 4:
        points = [sorted_pts[None]] + [swap(sorted_pts, 2 * j)[None] for j in range(1, min(half, 3))]
    else:
        everything = lax.all_gather(sorted_pts, "grid")
        points = [jnp.take(everything, me ^ (2 * jnp.arange(half)), axis=0)]
    calls = half if half <= 4 else 1
    per_call = half // calls
    lines = planes * 2 * height
    slab_spec = pl.BlockSpec((1, table_rows, CHUNK), lambda s: (s, 0, 0))
    steps_spec = pl.BlockSpec((None, 8, CHUNK), lambda s: (s, table_rows // 8 - 1, 0), memory_space=pltpu.SMEM)
    block_spec = pl.BlockSpec((1, lines, LANES), lambda s: (s, 0, 0))
    point_scratch = [pltpu.VMEM((12, rows, CHUNK), F32), pltpu.VMEM((2, rows, CHUNK), F32), pltpu.VMEM((LANES, LANES), BF)]
    spread = pl.pallas_call(
        functools.partial(spread_kernel, planes, height, unroll),
        grid=(per_call,),
        in_specs=[slab_spec, steps_spec],
        out_specs=(block_spec, block_spec),
        out_shape=(jax.ShapeDtypeStruct((per_call, lines, LANES), F32),) * 2,
        scratch_shapes=point_scratch,
        compiler_params=params(20),
        cost_estimate=cost(8e9),
        name="spread_points",
    )
    own, sib = [], []
    for call in range(calls):
        mine, theirs = spread(points[call], points[call])
        if call == 0 and half == 4:
            sorted_pts, theirs = lax.optimization_barrier((sorted_pts, theirs))
            points.append(swap(sorted_pts, 6)[None])
        own.append(mine)
        if call < calls - 1:
            sib.append(swap(theirs, 1))
    sent = theirs
    cells = potential if height == planes else jnp.pad(potential, ((0, height - planes), (0, 0)))
    cells = cells.reshape(height // 8, 8, N * N // LANES, LANES).transpose(0, 2, 1, 3)
    cells = cells.reshape(height // 8, N // 2, 3, 8, LANES)
    *sib, sent, mine = lax.optimization_barrier((*sib, sent, both))
    sib.append(swap(sent, 1))
    coefs = [both]
    for shift in range(1, bands):
        coefs.append(lax.ppermute(mine, "band", [(i, (i + shift) % bands) for i in range(bands)]))
    constants = [jnp.asarray(t) for t in tables()]
    parts = [[1], [0, *range(2, half)]] if 2 <= half <= 4 else [list(range(half))]
    cube = (planes, 2, height // 8, 8, LANES)
    keep, *send = pl.pallas_call(
        functools.partial(potential_kernel, planes, calls, parts),
        grid=(height // 8,),
        in_specs=[anywhere] * (2 * calls)
        + [pl.BlockSpec((1, N // 2, 3, 8, LANES), lambda i: (i, 0, 0, 0, 0))]
        + [anywhere] * 4,
        out_specs=[anywhere] * (1 + len(parts)),
        out_shape=[jax.ShapeDtypeStruct((count_of, *cube), F32) for count_of in (half, *map(len, parts))],
        scratch_shapes=[
            pltpu.VMEM((N, *cube[1:]), F32),
            pltpu.VMEM((N, *cube[1:]), F32),
            *(pltpu.VMEM(t.shape, BF) for t in constants),
            pltpu.SemaphoreType.DMA((height // 8, 2, half)),
            pltpu.SemaphoreType.DMA((height // 8, 2, half)),
            pltpu.SemaphoreType.DMA((4,)),
        ],
        compiler_params=params(40),
        cost_estimate=cost(4e10),
        name="apply_potential",
    )(*(x.reshape(per_call, *cube) for x in (*own, *sib)), cells, *constants)
    tied = lax.optimization_barrier((*send, *coefs))
    coefs = tied[len(parts) :]
    keep = keep.reshape(half, lines, LANES)
    other = []
    for x in tied[: len(parts)]:
        if other:
            other[-1], x = lax.optimization_barrier((other[-1], x))
        other.append(swap(x, 1))
    other = [x.reshape(-1, lines, LANES) for x in other]

    def block_at(first):
        return pl.BlockSpec((1, lines, LANES), lambda s: (first + s, 0, 0))

    partial = [None] * calls
    for call in [*range(1, calls), 0]:
        table = points[call]
        if call == 0 and half == 4:
            diagonal, table = lax.optimization_barrier((swap(partial[3], 6), table))
        first = call * per_call
        number, part = next((i, part) for i, part in enumerate(parts) if first in part)
        partial[call] = pl.pallas_call(
            functools.partial(collect_kernel, planes, height, unroll),
            grid=(per_call,),
            in_specs=[slab_spec, steps_spec, block_at(first), block_at(part.index(first))],
            out_specs=pl.BlockSpec((1, 2 * rows, CHUNK), lambda s: (s, 0, 0)),
            out_shape=jax.ShapeDtypeStruct((per_call, 2 * rows, CHUNK), F32),
            scratch_shapes=point_scratch + [pltpu.VMEM((planes, 8 * height, LANES), BF)],
            compiler_params=params(24),
            cost_estimate=cost(8e9),
            name="collect_points",
        )(table, table, keep, other[number])
    if half <= 4:
        arrived = [partial[0]] + [swap(partial[j], 2 * j) for j in range(1, min(half, 3))]
        if half == 4:
            arrived.append(diagonal)
    else:
        ids = jnp.arange(slabs)
        blocks = jnp.take(partial[0], (ids ^ me) // 2, axis=0)
        blocks = jnp.where(((ids ^ me) % 2 == 0)[:, None, None], blocks, 0.0)
        arrived = [lax.all_to_all(blocks, "grid", split_axis=0, concat_axis=0, tiled=True)]
    direct = slabs <= 8
    total, part = pl.pallas_call(
        functools.partial(sum_kernel, len(arrived)),
        out_shape=(
            jax.ShapeDtypeStruct((2 * rows, CHUNK), F32),
            jax.ShapeDtypeStruct((1 if direct else slabs, 2 * bands, LANES), F32),
        ),
        compiler_params=params(16),
        cost_estimate=cost(1e9),
        name="sum_points",
    )(*arrived, *coefs)
    if direct:
        pair = part + swap(part, 1)
        sums = [pair] + [swap(pair, 2 * j) for j in range(1, half)]
    else:
        sums = [lax.all_to_all(part, "grid", split_axis=0, concat_axis=0, tiled=True)]
    applied = pl.pallas_call(
        unsort_kernel,
        out_shape=jax.ShapeDtypeStruct((2, 2 * rows, LANES), F32),
        scratch_shapes=[pltpu.VMEM((4 * rows, CHUNK), BF), pltpu.VMEM((2, rows, CHUNK), F32)],
        compiler_params=params(12),
        cost_estimate=cost(6e9),
        name="unsort_points",
    )(total, dest)
    resid, sub = pl.pallas_call(
        functools.partial(residual_kernel, 1.0 / (count * slabs), bands),
        out_shape=(
            jax.ShapeDtypeStruct((2, 2 * rows, LANES), F32),
            jax.ShapeDtypeStruct((2, 1, bands), F32),
        ),
        scratch_shapes=[pltpu.VMEM((half if direct else slabs, 2 * bands, LANES), F32)],
        compiler_params=params(8),
        cost_estimate=cost(2e9),
        name="residual",
    )(applied, *coefs, *sums)
    return sub.transpose(0, 2, 1), resid.reshape(2, 1, count)


def solution(mesh):
    return jax.shard_map(
        local,
        mesh=mesh,
        in_specs=(P(None, "band", "grid"), P("grid"), P("grid", None)),
        out_specs=(P(None, None, "band"), P(None, "band", "grid")),
        check_vma=False,
    )
```

```python
import functools
import math

import jax
import jax.numpy as jnp
import numpy as np
from jax import lax
from jax.experimental import pallas as pl
from jax.experimental.pallas import tpu as pltpu
from jax.sharding import PartitionSpec as P

N = 192
CHUNK = 256
LANES = 128
BF = jnp.bfloat16
F32 = jnp.float32
NT = (((1,), (1,)), ((), ()))


def split(x):
    high = x.astype(BF)
    low = (x - high.astype(F32)).astype(BF)
    return high, low


def mm(a, b):
    return jnp.dot(a, b, preferred_element_type=F32)


def split_table(table):
    table = table.astype(np.float32)
    high = table.astype(BF)
    low = (table - high.astype(np.float32)).astype(BF)
    return high, low


@functools.cache
def tables():
    pos = np.arange(N)
    angle = 2.0 * math.pi * ((pos[:, None] * pos[None, :]) % N) / N
    cb, sb = np.cos(angle), np.sin(angle)
    order = np.concatenate([pos[0::2], pos[1::2]])
    co, so = cb[order], sb[order]
    b_fwd = np.block([[co, -so], [so, co]])
    b_inv = np.block([[co.T, so.T], [-so.T, co.T]])
    freq = np.arange(LANES)
    freq = np.where(freq < 64, freq, freq - LANES)
    keep = (np.abs(freq) < 48)[:, None]
    angle = 2.0 * math.pi * ((freq[:, None] * pos[None, :]) % N) / N
    cc, sc = np.cos(angle) * keep, np.sin(angle) * keep
    c_fwd = np.block([[cc, sc], [-sc, cc]])
    c_inv = np.block([[cc.T, -sc.T], [sc.T, cc.T]]) / float(N) ** 3
    bf_h, bf_l = split_table(b_fwd)
    bi_h, bi_l = split_table(b_inv)
    cf_h, cf_l = split_table(c_fwd)
    ci_h, ci_l = split_table(c_inv)
    return (
        np.concatenate([bf_h, bf_l, bf_h], axis=1),
        np.concatenate([cf_h, cf_l, cf_h], axis=0),
        np.concatenate([ci_h, ci_l, ci_h], axis=0),
        np.concatenate([bi_h, bi_l, bi_h], axis=1),
    )


def fold(x):
    half = x.shape[0] // 2
    return jnp.concatenate([x[:half], x[half:]], axis=1)


def unfold(x):
    return jnp.concatenate([x[:, :LANES], x[:, LANES:]], axis=0)


def wide(row, count):
    tile = jnp.broadcast_to(row, (16, row.shape[1])).astype(BF)
    return jnp.concatenate([tile] * (count // 16), axis=0)


def ident(count):
    return lax.broadcasted_iota(jnp.int32, (count, LANES), 0).astype(F32).astype(BF)


def equal(row, ids):
    code = wide(row, ids.shape[0])
    return code == jnp.concatenate([ids, ids], axis=1)


def one_hot(row, ids):
    one = jnp.ones((ids.shape[0], CHUNK), BF)
    return jnp.where(equal(row, ids), one, jnp.zeros_like(one))


def floor_div(x, divisor):
    return jnp.floor((x + 0.5) * (1.0 / divisor))


def sort_kernel(
    planes, m_hbm, c_hbm, out_ref, d_ref, both_ref, acc_ref, val_ref, gb_ref, cum_ref, tot_ref, lane_ref, m_ref, c_ref, sems
):
    rows = gb_ref.shape[0]
    fetch_m = pltpu.make_async_copy(m_hbm, m_ref, sems.at[0])
    fetch_c = pltpu.make_async_copy(c_hbm, c_ref, sems.at[1])
    fetch_m.start()
    fetch_c.start()
    fetch_m.wait()
    m = fold(m_ref[...]).astype(F32)
    line = floor_div(m, N)
    gc = m - N * line
    ga = floor_div(line, planes)
    gb = line - planes * ga
    ga = jnp.where(ga < 96, ga, ga - 96)
    gc = jnp.where(gc < 96, gc, gc - 64)
    gb_ref[...] = gb
    lane_r = lax.broadcasted_iota(jnp.int32, (CHUNK, 2 * CHUNK), 0)
    lane_c = lax.broadcasted_iota(jnp.int32, (CHUNK, 2 * CHUNK), 1)
    tri = jnp.where((lane_r < lane_c) | (lane_c >= CHUNK), 1.0, 0.0).astype(BF)
    row_r = lax.broadcasted_iota(jnp.int32, (rows + 16, rows), 0)
    row_c = lax.broadcasted_iota(jnp.int32, (rows + 16, rows), 1)
    below = jnp.where(row_c < row_r, 1.0, 0.0).astype(BF)
    masks = [jnp.where(gb == float(g), 1.0, 0.0).astype(BF) for g in range(planes)]
    cum_ref[...] = mm(below, jnp.concatenate(masks, axis=1))
    tot_ref[...] = jnp.zeros_like(tot_ref)
    step = 3 if planes % 3 == 0 and planes > 3 else 1

    def at(g):
        return pl.ds(pl.multiple_of(g * CHUNK, CHUNK), CHUNK)

    def gather(i, carry):
        for j in range(step):
            g = i * step + j
            tot_ref[pl.ds(g, 1), :] = cum_ref[rows : rows + 8, at(g)][0:1]
        return carry

    lax.fori_loop(0, planes // step, gather, 0)
    lane_ref[...] = mm(tot_ref[...].astype(BF), tri)
    step_id = lax.broadcasted_iota(jnp.int32, (8, CHUNK), 1).astype(F32)

    def rank(i, carry):
        base, place, plane_of = carry
        for j in range(step):
            g = i * step + j
            gf = g.astype(F32)
            lanes = lane_ref[pl.ds(g, 1), :]
            here = cum_ref[0:rows, at(g)] + (lanes[:, :CHUNK] + base)
            place = jnp.where(gb_ref[...] == gf, here, place)
            base = base + lanes[:, CHUNK:]
            end = gf + jnp.floor((jnp.maximum(base, 1.0) - 1.0) * (1.0 / CHUNK))
            end = jnp.where(gf < planes - 1.0, end, 1e6)
            plane_of = plane_of + jnp.where(end < step_id, 1.0, 0.0)
        return base, place, plane_of

    _, place, plane_of = lax.fori_loop(
        0,
        planes // step,
        rank,
        (jnp.zeros((1, CHUNK), F32), jnp.zeros((rows, CHUNK), F32), jnp.zeros((8, CHUNK), F32)),
    )
    d_ref[...] = place
    fetch_c.wait()
    re_h, re_l = split(fold(c_ref[0]))
    im_h, im_l = split(fold(c_ref[1]))
    for q, value in enumerate((re_h, re_l, im_h, im_l, ga, gb, gc)):
        val_ref[q] = value.astype(F32)
    acc_ref[...] = jnp.zeros_like(acc_ref)
    hi_id, lo_id = ident(rows), ident(CHUNK)
    zero = jnp.zeros((rows, CHUNK), BF)

    def body(i, carry):
        part = pl.ds(pl.multiple_of(i * 8, 8), 8)
        d = d_ref[part, :]
        hi = jnp.floor(d * (1.0 / CHUNK))
        lo = d - CHUNK * hi
        values = [val_ref[q, part, :] for q in range(7)]
        left, right = [], []
        for j in range(8):
            at_hi = equal(hi[j : j + 1], hi_id)
            left.append(
                jnp.concatenate([jnp.where(at_hi, wide(v[j : j + 1], rows), zero) for v in values], axis=0)
            )
            right.append(one_hot(lo[j : j + 1], lo_id))
        acc_ref[...] += lax.dot_general(
            jnp.concatenate(left, axis=1), jnp.concatenate(right, axis=1), NT, preferred_element_type=F32
        )
        return carry

    lax.fori_loop(0, rows // 8, body, 0)
    got = [acc_ref[q * rows : (q + 1) * rows] for q in range(7)]
    both_ref[0:2] = c_ref[...]
    for q in range(2):
        value = got[2 * q] + got[2 * q + 1]
        out_ref[q * rows : (q + 1) * rows] = value
        both_ref[2 + q] = unfold(value)
    out_ref[2 * rows : 3 * rows] = (got[4] * planes + got[5]) * LANES + got[6]
    out_ref[3 * rows : 3 * rows + 8] = plane_of


def sin_cos(x):
    y = x * x
    s = -1.0 / 39916800.0 + y * (1.0 / 6227020800.0)
    s = 1.0 / 362880.0 + y * s
    s = -1.0 / 5040.0 + y * s
    s = 1.0 / 120.0 + y * s
    s = -1.0 / 6.0 + y * s
    s = x + x * y * s
    c = 1.0 / 479001600.0 - y * (1.0 / 87178291200.0)
    c = -1.0 / 3628800.0 + y * c
    c = 1.0 / 40320.0 + y * c
    c = -1.0 / 720.0 + y * c
    c = 1.0 / 24.0 + y * c
    c = -0.5 + y * c
    c = 1.0 + y * c
    return s, c


def decode(cell, planes):
    line = jnp.floor(cell * (1.0 / LANES))
    gc = cell - LANES * line
    ga = floor_div(line, planes)
    gb = line - planes * ga
    freq = jnp.where(ga < 48, ga, ga - 96)
    return freq, gb, gc


def phase(freq, first):
    turn = freq * first
    turn = turn - N * jnp.floor(turn * (1.0 / N) + 0.5)
    s, c = sin_cos(turn * (math.pi / N))
    return 1.0 - 2.0 * s * s, 2.0 * s * c


def powers(freq, w_ref):
    s, c = sin_cos(freq * (2.0 * math.pi / N))
    for q in range(4):
        w_ref[4 + 2 * q] = c
        w_ref[5 + 2 * q] = s
        s, c = 2.0 * s * c, c * c - s * s


def firsts(planes):
    me = lax.axis_index("grid")
    return (me * planes).astype(F32), ((me ^ 1) * planes).astype(F32)


def pair_code(planes, steps_ref, code_ref, rows, step):
    g = steps_ref[0, step].astype(jnp.int32)
    c = jnp.minimum(step - g, rows - 1)
    wanted = jnp.where(step < rows + planes - 1, g, -1).astype(F32)
    code = jnp.where(code_ref[0, pl.ds(c, 1), :] == wanted, code_ref[1, pl.ds(c, 1), :], -1.0)
    return g, c, code


def row_of(ref, index, c):
    return jnp.broadcast_to(ref[index, pl.ds(c, 1), :], (8, CHUNK))


def rise(w_ref, c):
    k = lax.broadcasted_iota(jnp.int32, (8, CHUNK), 0)
    er = ei = None
    for bit in range(3):
        on = (k & (1 << bit)) != 0
        fr = jnp.where(on, row_of(w_ref, 4 + 2 * bit, c), 1.0)
        fi = jnp.where(on, row_of(w_ref, 5 + 2 * bit, c), 0.0)
        if er is None:
            er, ei = fr, fi
        else:
            er, ei = er * fr - ei * fi, er * fi + ei * fr
    return er, ei


def prepare(planes, cell, w_ref, code_ref, id_ref):
    freq, gb, gc = decode(cell, planes)
    code_ref[0] = gb
    code_ref[1] = gc
    id_ref[...] = ident(LANES)
    for q, first in enumerate(firsts(planes)):
        w_ref[2 * q], w_ref[2 * q + 1] = phase(freq, first)
    powers(freq, w_ref)


def spread_kernel(planes, height, unroll, slab_ref, steps_ref, own_ref, sib_ref, w_ref, code_ref, id_ref):
    rows = w_ref.shape[1]
    prepare(planes, slab_ref[0, 2 * rows : 3 * rows], w_ref, code_ref, id_ref)
    re, im = slab_ref[0, 0:rows], slab_ref[0, rows : 2 * rows]
    for q in range(2):
        sr, si = w_ref[2 * q], w_ref[2 * q + 1]
        w_ref[2 * q] = re * sr - im * si
        w_ref[2 * q + 1] = re * si + im * sr
    own_ref[...] = jnp.zeros_like(own_ref)
    sib_ref[...] = jnp.zeros_like(sib_ref)

    def visit(i, carry):
        ids = id_ref[...]
        for j in range(unroll):
            g, c, code = pair_code(planes, steps_ref, code_ref, rows, i * unroll + j)
            er, ei = rise(w_ref, c)
            jr, ji = row_of(w_ref, 10, c), row_of(w_ref, 11, c)
            lines = []
            for q in range(2):
                zr, zi = row_of(w_ref, 2 * q, c), row_of(w_ref, 2 * q + 1, c)
                zr, zi = er * zr - ei * zi, er * zi + ei * zr
                real, imag = [zr], [zi]
                for _ in range(height // 8 - 1):
                    zr, zi = zr * jr - zi * ji, zr * ji + zi * jr
                    real.append(zr)
                    imag.append(zi)
                lines += real + imag
            high, low = split(jnp.concatenate(lines, axis=0))
            got = lax.dot_general(
                jnp.concatenate([high, low], axis=0), one_hot(code, ids), NT, preferred_element_type=F32
            )
            got = got[: 4 * height] + got[4 * height :]
            where = pl.ds(pl.multiple_of(g * (2 * height), 8), 2 * height)
            own_ref[0, where, :] += got[: 2 * height]
            sib_ref[0, where, :] += got[2 * height :]
        return carry

    lax.fori_loop(0, -(-(rows + planes - 1) // unroll), visit, 0)


def collect_kernel(
    planes, height, unroll, slab_ref, steps_ref, own_ref, sib_ref, h_ref, w_ref, code_ref, id_ref, u2_ref
):
    rows = w_ref.shape[1]
    prepare(planes, slab_ref[0, 2 * rows : 3 * rows], w_ref, code_ref, id_ref)
    for g in range(planes):
        where = slice(g * 2 * height, (g + 1) * 2 * height)
        high, low = split(jnp.concatenate([own_ref[0, where, :], sib_ref[0, where, :]], axis=0))
        u2_ref[g] = jnp.concatenate([high, low], axis=0)
    h_ref[...] = jnp.zeros_like(h_ref)

    def visit(i, carry):
        ids = id_ref[...]
        for j in range(unroll):
            g, c, code = pair_code(planes, steps_ref, code_ref, rows, i * unroll + j)
            got = mm(u2_ref[g], one_hot(code, ids))
            got = got[: 4 * height] + got[4 * height :]
            jr, ji = row_of(w_ref, 10, c), row_of(w_ref, 11, c)
            hr = hi = 0.0
            for q in range(2):
                value = got[q * 2 * height : (q + 1) * 2 * height]
                ar = value[height - 8 : height]
                ai = value[2 * height - 8 : 2 * height]
                for t in range(height // 8 - 2, -1, -1):
                    ar, ai = (
                        ar * jr + ai * ji + value[8 * t : 8 * t + 8],
                        ai * jr - ar * ji + value[height + 8 * t : height + 8 * t + 8],
                    )
                zr, zi = row_of(w_ref, 2 * q, c), row_of(w_ref, 2 * q + 1, c)
                hr, hi = hr + ar * zr + ai * zi, hi + ai * zr - ar * zi
            er, ei = rise(w_ref, c)
            h_ref[0, pl.ds(c, 1), :] += jnp.sum(hr * er + hi * ei, axis=0, keepdims=True)
            h_ref[0, pl.ds(rows + c, 1), :] += jnp.sum(hi * er - hr * ei, axis=0, keepdims=True)
        return carry

    lax.fori_loop(0, -(-(rows + planes - 1) // unroll), visit, 0)


def potential_kernel(planes, calls, parts, *refs):
    own, sib = refs[:calls], refs[calls : 2 * calls]
    v_ref, *tables_hbm = refs[2 * calls : 2 * calls + 5]
    keep_ref = refs[2 * calls + 5]
    send_refs = refs[2 * calls + 6 : 2 * calls + 6 + len(parts)]
    t_ref, u_ref, bf_ref, cf_ref, ci_ref, bi_ref, in_sems, out_sems, table_sems = refs[2 * calls + 6 + len(parts) :]
    step = pl.program_id(0)
    me = lax.axis_index("grid")
    half = keep_ref.shape[0]
    per_call = half // calls
    tiles = t_ref.shape[2]
    last = tiles - 1

    def place(j, q):
        return pl.ds((me ^ (2 * j + q)) * planes, planes)

    def arrivals(t):
        for q, blocks in enumerate((own, sib)):
            for j in range(half):
                yield pltpu.make_async_copy(
                    blocks[j // per_call].at[j % per_call, :, :, t], t_ref.at[place(j, q), :, t], in_sems.at[t, q, j]
                )

    def departures(t):
        for j in range(half):
            yield pltpu.make_async_copy(
                u_ref.at[place(j, 0), :, t], keep_ref.at[j, :, :, t], out_sems.at[t, 0, j]
            )
        for ref, part in zip(send_refs, parts):
            for i, j in enumerate(part):
                yield pltpu.make_async_copy(
                    u_ref.at[place(j, 1), :, t], ref.at[i, :, :, t], out_sems.at[t, 1, j]
                )

    def fetches():
        for q, (source, target) in enumerate(zip(tables_hbm, (bf_ref, cf_ref, ci_ref, bi_ref))):
            yield pltpu.make_async_copy(source, target, table_sems.at[q])

    @pl.when(step == 0)
    def _():
        for copies in (arrivals(0), fetches(), *(arrivals(t) for t in range(1, tiles))):
            for copy in copies:
                copy.start()
        for copies in (arrivals(0), fetches()):
            for copy in copies:
                copy.wait()

    for t in range(1, tiles):

        @pl.when(step == t)
        def _(t=t):
            for copy in arrivals(t):
                copy.wait()

    group = 4

    def turn(x):
        return jnp.transpose(x, (1, 0, 2))

    planes_re, planes_im = (turn(t_ref[:, q, step]) for q in range(2))
    cells = [turn(v_ref[0, :, q]) for q in range(3)]

    def rows_of(first):
        x = jnp.concatenate(
            [
                jnp.concatenate([source[first + j] for j in range(group)], axis=1)
                for source in (planes_re, planes_im)
            ],
            axis=0,
        )
        high, low = split(x)
        return jnp.concatenate([high, high, low], axis=0)

    def columns_of(x):
        x = jnp.concatenate(
            [
                jnp.concatenate([x[q * N : (q + 1) * N, j * LANES : (j + 1) * LANES] for q in range(2)], axis=1)
                for j in range(group)
            ],
            axis=0,
        )
        high, low = split(x)
        return jnp.concatenate([high, high, low], axis=1)

    def weigh(first, x):
        v = []
        for j in range(group):
            t = [cell[first + j] for cell in cells]
            v.append(jnp.concatenate([t[0], t[1][:, :64]], axis=1))
            v.append(jnp.concatenate([t[1][:, 64:], t[2]], axis=1))
        v = jnp.concatenate(v, axis=0)
        high, low = split(x * jnp.concatenate([v, v], axis=1))
        return jnp.concatenate([high, high, low], axis=1)

    def rows_again(x):
        x = jnp.concatenate(
            [
                jnp.concatenate(
                    [x[j * N : (j + 1) * N, q * LANES : (q + 1) * LANES] for j in range(group)], axis=1
                )
                for q in range(2)
            ],
            axis=0,
        )
        high, low = split(x)
        return jnp.concatenate([high, high, low], axis=0)

    chains = (0, group)
    data = [mm(bf_ref[...], rows_of(first)) for first in chains]
    data = [mm(columns_of(x), cf_ref[...]) for x in data]
    data = [mm(weigh(first, x), ci_ref[...]) for first, x in zip(chains, data)]
    data = [mm(bi_ref[...], rows_again(x)) for x in data]
    for q in range(2):
        lines = [x[q * N : (q + 1) * N, j * LANES : (j + 1) * LANES] for x in data for j in range(group)]
        u_ref[:, q, step] = turn(jnp.stack(lines))

    for t in range(tiles):

        @pl.when(step == t)
        def _(t=t):
            for copy in departures(t):
                copy.start()

    @pl.when(step == last)
    def _():
        for t in range(tiles):
            for copy in departures(t):
                copy.wait()


def sum_kernel(arrivals, *refs):
    recv_refs, coef_refs, (total_ref, part_ref) = refs[:arrivals], refs[arrivals:-2], refs[-2:]
    total = None
    for recv in recv_refs:
        for s in range(recv.shape[0]):
            total = recv[s] if total is None else total + recv[s]
    total_ref[...] = total
    rows = total.shape[0] // 2
    hr, hi = unfold(total[:rows]), unfold(total[rows:])
    real, imag = [], []
    for coef in coef_refs:
        cr, ci = coef[2], coef[3]
        real.append(jnp.sum(cr * hr + ci * hi, axis=0, keepdims=True))
        imag.append(jnp.sum(cr * hi - ci * hr, axis=0, keepdims=True))
    sums = jnp.concatenate(real + imag, axis=0)
    for s in range(part_ref.shape[0]):
        part_ref[s] = sums


def unsort_kernel(total_ref, d_ref, h_ref, hl_ref, wide_ref):
    rows = d_ref.shape[0]
    high, low = split(total_ref[...])
    hl_ref[0 : 2 * rows] = high
    hl_ref[2 * rows :] = low
    hi_id = lax.broadcasted_iota(jnp.int32, (rows, CHUNK), 0).astype(F32)
    lo_id = ident(CHUNK)

    def body(i, carry):
        part = pl.ds(pl.multiple_of(i * 8, 8), 8)
        d = d_ref[part, :]
        hi = jnp.floor(d * (1.0 / CHUNK))
        lo = d - CHUNK * hi
        real, imag = [], []
        for j in range(8):
            got = mm(hl_ref[...], one_hot(lo[j : j + 1], lo_id))
            got = got[: 2 * rows] + got[2 * rows :]
            at_hi = jnp.broadcast_to(hi[j : j + 1], (rows, CHUNK)) == hi_id
            real.append(jnp.sum(jnp.where(at_hi, got[:rows], 0.0), axis=0, keepdims=True))
            imag.append(jnp.sum(jnp.where(at_hi, got[rows:], 0.0), axis=0, keepdims=True))
        wide_ref[0, part, :] = jnp.concatenate(real, axis=0)
        wide_ref[1, part, :] = jnp.concatenate(imag, axis=0)
        return carry

    lax.fori_loop(0, rows // 8, body, 0)
    h_ref[0] = unfold(wide_ref[0])
    h_ref[1] = unfold(wide_ref[1])


def residual_kernel(scale, bands, h_ref, *refs):
    coef_refs, sum_refs, (out_ref, sub_ref, all_ref) = refs[:bands], refs[bands:-3], refs[-3:]
    band = lax.axis_index("band")
    me = lax.axis_index("grid")
    if len(sum_refs) > 1:
        for j, part in enumerate(sum_refs):
            all_ref[lax.div(me, 2) ^ j] = part[0]
    else:
        all_ref[...] = sum_refs[0][...]
    sub = all_ref[0]
    for s in range(1, all_ref.shape[0]):
        sub = sub + all_ref[s]
    sub = jnp.sum(sub, axis=1, keepdims=True) * scale
    lane = lax.broadcasted_iota(jnp.int32, (1, LANES), 1)
    hr, hi = h_ref[0], h_ref[1]
    line_re = line_im = jnp.zeros((1, LANES), F32)
    for shift, coef in enumerate(coef_refs):
        sr, si = sub[shift : shift + 1], sub[bands + shift : bands + shift + 1]
        here = lane == lax.rem(band + bands - shift, bands)
        line_re = jnp.where(here, sr, line_re)
        line_im = jnp.where(here, si, line_im)
        cr, ci = coef[0], coef[1]
        hr = hr - (sr * cr - si * ci)
        hi = hi - (si * cr + sr * ci)
    out_ref[0] = hr
    out_ref[1] = hi
    sub_ref[0] = line_re[:, :bands]
    sub_ref[1] = line_im[:, :bands]


def params(mib):
    return pltpu.CompilerParams(vmem_limit_bytes=mib * 1024 * 1024)


def cost(flops):
    return pl.CostEstimate(flops=int(flops), bytes_accessed=0, transcendentals=0)


def whole(shape):
    return pl.BlockSpec(shape, lambda *_: (0,) * len(shape))


def local(coefficients, index_map, potential):
    slabs = lax.axis_size("grid")
    bands = lax.axis_size("band")
    planes = potential.shape[0]
    count = coefficients.shape[2]
    rows = count // CHUNK
    height = -(-planes // 8) * 8
    unroll = 88
    me = lax.axis_index("grid")
    half = slabs // 2
    anywhere = pl.BlockSpec(memory_space=pl.ANY)
    coef = coefficients.reshape(2, 2 * rows, LANES)
    table_rows = 3 * rows + 8
    sorted_pts, dest, both = pl.pallas_call(
        functools.partial(sort_kernel, planes),
        in_specs=[pl.BlockSpec(memory_space=pltpu.HBM)] * 2,
        out_shape=(
            jax.ShapeDtypeStruct((table_rows, CHUNK), F32),
            jax.ShapeDtypeStruct((rows, CHUNK), F32),
            jax.ShapeDtypeStruct((4, 2 * rows, LANES), F32),
        ),
        scratch_shapes=[
            pltpu.VMEM((7 * rows, CHUNK), F32),
            pltpu.VMEM((7, rows, CHUNK), F32),
            pltpu.VMEM((rows, CHUNK), F32),
            pltpu.VMEM((rows + 16, planes * CHUNK), F32),
            pltpu.VMEM((-(-planes // 16) * 16, CHUNK), F32),
            pltpu.VMEM((-(-planes // 16) * 16, 2 * CHUNK), F32),
            pltpu.VMEM((2 * rows, LANES), jnp.int32),
            pltpu.VMEM((2, 2 * rows, LANES), F32),
            pltpu.SemaphoreType.DMA((2,)),
        ],
        compiler_params=params(58),
        cost_estimate=cost(1e10),
        name="sort_points",
    )(index_map.reshape(2 * rows, LANES), coef)

    def swap(x, bits):
        return lax.ppermute(x, "grid", [(i, i ^ bits) for i in range(slabs)])

    if half <= 4:
        points = [sorted_pts[None]] + [swap(sorted_pts, 2 * j)[None] for j in range(1, min(half, 3))]
    else:
        everything = lax.all_gather(sorted_pts, "grid")
        points = [jnp.take(everything, me ^ (2 * jnp.arange(half)), axis=0)]
    calls = half if half <= 4 else 1
    per_call = half // calls
    lines = planes * 2 * height
    slab_spec = pl.BlockSpec((1, table_rows, CHUNK), lambda s: (s, 0, 0))
    steps_spec = pl.BlockSpec((None, 8, CHUNK), lambda s: (s, table_rows // 8 - 1, 0), memory_space=pltpu.SMEM)
    block_spec = pl.BlockSpec((1, lines, LANES), lambda s: (s, 0, 0))
    point_scratch = [pltpu.VMEM((12, rows, CHUNK), F32), pltpu.VMEM((2, rows, CHUNK), F32), pltpu.VMEM((LANES, LANES), BF)]
    spread = pl.pallas_call(
        functools.partial(spread_kernel, planes, height, unroll),
        grid=(per_call,),
        in_specs=[slab_spec, steps_spec],
        out_specs=(block_spec, block_spec),
        out_shape=(jax.ShapeDtypeStruct((per_call, lines, LANES), F32),) * 2,
        scratch_shapes=point_scratch,
        compiler_params=params(20),
        cost_estimate=cost(8e9),
        name="spread_points",
    )
    own, sib = [], []
    for call in range(calls):
        mine, theirs = spread(points[call], points[call])
        if call == 0 and half == 4:
            sorted_pts, theirs = lax.optimization_barrier((sorted_pts, theirs))
            points.append(swap(sorted_pts, 6)[None])
        own.append(mine)
        if call < calls - 1:
            sib.append(swap(theirs, 1))
    sent = theirs
    cells = potential if height == planes else jnp.pad(potential, ((0, height - planes), (0, 0)))
    cells = cells.reshape(height // 8, 8, N * N // LANES, LANES).transpose(0, 2, 1, 3)
    cells = cells.reshape(height // 8, N // 2, 3, 8, LANES)
    *sib, sent, mine = lax.optimization_barrier((*sib, sent, both))
    sib.append(swap(sent, 1))
    coefs = [both]
    for shift in range(1, bands):
        coefs.append(lax.ppermute(mine, "band", [(i, (i + shift) % bands) for i in range(bands)]))
    constants = [jnp.asarray(t) for t in tables()]
    parts = [[1], [0, *range(2, half)]] if 2 <= half <= 4 else [list(range(half))]
    cube = (planes, 2, height // 8, 8, LANES)
    keep, *send = pl.pallas_call(
        functools.partial(potential_kernel, planes, calls, parts),
        grid=(height // 8,),
        in_specs=[anywhere] * (2 * calls)
        + [pl.BlockSpec((1, N // 2, 3, 8, LANES), lambda i: (i, 0, 0, 0, 0))]
        + [anywhere] * 4,
        out_specs=[anywhere] * (1 + len(parts)),
        out_shape=[jax.ShapeDtypeStruct((count_of, *cube), F32) for count_of in (half, *map(len, parts))],
        scratch_shapes=[
            pltpu.VMEM((N, *cube[1:]), F32),
            pltpu.VMEM((N, *cube[1:]), F32),
            *(pltpu.VMEM(t.shape, BF) for t in constants),
            pltpu.SemaphoreType.DMA((height // 8, 2, half)),
            pltpu.SemaphoreType.DMA((height // 8, 2, half)),
            pltpu.SemaphoreType.DMA((4,)),
        ],
        compiler_params=params(40),
        cost_estimate=cost(4e10),
        name="apply_potential",
    )(*(x.reshape(per_call, *cube) for x in (*own, *sib)), cells, *constants)
    tied = lax.optimization_barrier((*send, *coefs))
    coefs = tied[len(parts) :]
    keep = keep.reshape(half, lines, LANES)
    other = []
    for x in tied[: len(parts)]:
        if other:
            other[-1], x = lax.optimization_barrier((other[-1], x))
        other.append(swap(x, 1))
    other = [x.reshape(-1, lines, LANES) for x in other]

    def block_at(first):
        return pl.BlockSpec((1, lines, LANES), lambda s: (first + s, 0, 0))

    partial = [None] * calls
    for call in [*range(1, calls), 0]:
        table = points[call]
        if call == 0 and half == 4:
            diagonal, table = lax.optimization_barrier((swap(partial[3], 6), table))
        first = call * per_call
        number, part = next((i, part) for i, part in enumerate(parts) if first in part)
        partial[call] = pl.pallas_call(
            functools.partial(collect_kernel, planes, height, unroll),
            grid=(per_call,),
            in_specs=[slab_spec, steps_spec, block_at(first), block_at(part.index(first))],
            out_specs=pl.BlockSpec((1, 2 * rows, CHUNK), lambda s: (s, 0, 0)),
            out_shape=jax.ShapeDtypeStruct((per_call, 2 * rows, CHUNK), F32),
            scratch_shapes=point_scratch + [pltpu.VMEM((planes, 8 * height, LANES), BF)],
            compiler_params=params(24),
            cost_estimate=cost(8e9),
            name="collect_points",
        )(table, table, keep, other[number])
    if half <= 4:
        arrived = [partial[0]] + [swap(partial[j], 2 * j) for j in range(1, min(half, 3))]
        if half == 4:
            arrived.append(diagonal)
    else:
        ids = jnp.arange(slabs)
        blocks = jnp.take(partial[0], (ids ^ me) // 2, axis=0)
        blocks = jnp.where(((ids ^ me) % 2 == 0)[:, None, None], blocks, 0.0)
        arrived = [lax.all_to_all(blocks, "grid", split_axis=0, concat_axis=0, tiled=True)]
    direct = slabs <= 8
    total, part = pl.pallas_call(
        functools.partial(sum_kernel, len(arrived)),
        out_shape=(
            jax.ShapeDtypeStruct((2 * rows, CHUNK), F32),
            jax.ShapeDtypeStruct((1 if direct else slabs, 2 * bands, LANES), F32),
        ),
        compiler_params=params(16),
        cost_estimate=cost(1e9),
        name="sum_points",
    )(*arrived, *coefs)
    if direct:
        pair = part + swap(part, 1)
        sums = [pair] + [swap(pair, 2 * j) for j in range(1, half)]
    else:
        sums = [lax.all_to_all(part, "grid", split_axis=0, concat_axis=0, tiled=True)]
    applied = pl.pallas_call(
        unsort_kernel,
        out_shape=jax.ShapeDtypeStruct((2, 2 * rows, LANES), F32),
        scratch_shapes=[pltpu.VMEM((4 * rows, CHUNK), BF), pltpu.VMEM((2, rows, CHUNK), F32)],
        compiler_params=params(12),
        cost_estimate=cost(6e9),
        name="unsort_points",
    )(total, dest)
    resid, sub = pl.pallas_call(
        functools.partial(residual_kernel, 1.0 / (count * slabs), bands),
        out_shape=(
            jax.ShapeDtypeStruct((2, 2 * rows, LANES), F32),
            jax.ShapeDtypeStruct((2, 1, bands), F32),
        ),
        scratch_shapes=[pltpu.VMEM((half if direct else slabs, 2 * bands, LANES), F32)],
        compiler_params=params(8),
        cost_estimate=cost(2e9),
        name="residual",
    )(applied, *coefs, *sums)
    return sub.transpose(0, 2, 1), resid.reshape(2, 1, count)


def solution(mesh):
    return jax.shard_map(
        local,
        mesh=mesh,
        in_specs=(P(None, "band", "grid"), P("grid"), P("grid", None)),
        out_specs=(P(None, None, "band"), P(None, "band", "grid")),
        check_vma=False,
    )
```
